32 devices in a mesh: gx: 8 (over z, core), gy: 4 (over y, x).
Axes of the slice: x: 2, y: 2, z: 4, core: 2. Of those that a mesh axis runs over, the one named last changes fastest.
Arguments:
- features: bfloat16 [8, 4, 32, 64, 256], P('gx', 'gy'), may hold values from -6 to 6
- weights: bfloat16 [27, 256, 256], replicated, may hold values from -0.078125 to 0.078125
- cotangent: bfloat16 [8, 4, 32, 64, 256], P('gx', 'gy'), may hold values from -6 to 6
- send_lists: int32 [8, 4, 8, 8], P('gx', 'gy'), may hold values from 0 to 31, as said below
- block_offset: int32 [8, 4, 108], P('gx', 'gy'), may hold values from 0 to 26, as said below
- block_input: int32 [8, 4, 108, 8], P('gx', 'gy'), may hold values from 0 to 95, as said below
- block_output: int32 [8, 4, 108, 8], P('gx', 'gy'), may hold values from 0 to 32, as said below
- block_count: int32 [8, 4], P('gx', 'gy'), may hold values from 1 to 108, as said below
Outputs:
- out_features: bfloat16 [8, 4, 32, 64, 256], P('gx', 'gy')
- feat_grad: bfloat16 [8, 4, 32, 64, 256], P('gx', 'gy')
- weight_grad: float32 [27, 256, 256], replicated
The draws below stay inside these ranges and needn't reach their ends.
Inputs may be any that keep to these rules, and one draw needn't show every extreme that they name: `send_lists`: each of a device's 8 lists names 8 different tiles that the device holds. `block_offset`: 0 in blocks past block_count. `block_input`: a tile slot of the device or a halo slot as in the reference program; 0 in unused pairs. `block_output`: 32 marks an unused pair; a device's used pairs of one offset name different tiles; the used blocks come first, grouped by offset, and blocks past block_count hold only unused pairs. `block_count`: some device uses all 108 blocks.
All inputs are finite; a program needn't handle non-finite values.
Results may differ from the reference program's by a relative error of at most 0.0029.
Values may be sent and summed in bfloat16 or wider, within the bound.
No kernel may reach another device: no remote copies, remote signals or barrier semaphores. Data moves between devices by JAX's collectives and lax.ppermute only.
A program may use at most 128 MiB of HBM per device.

```python
import math
import jax
import jax.numpy as jnp
from jax import lax

CHANNELS = 256
VOXELS = 64
OFFSETS = 27
BLOCK = 8
TILES_DEV = 32
HALO = 8
PER_OFFSET = 4
BLOCKS = 108
SLABS_X = 8
SLABS_Y = 4
TILES_ALL = 1024


def device_plan(key, active, dense):
    keys = jax.random.split(key, 7)
    slots = jnp.arange(TILES_DEV, dtype=jnp.int32)

    def ordering(order_key):
        noise = jax.random.randint(order_key, (TILES_DEV,), 0, 4096)
        score = noise * (2 * TILES_DEV) + slots + jnp.where(slots >= active, 4096 * 2 * TILES_DEV, 0)
        return jnp.argsort(score).astype(jnp.int32)
    orders = jax.vmap(ordering)(jax.random.split(keys[0], OFFSETS))
    sends = jax.vmap(ordering)(jax.random.split(keys[1], 8))[:, :HALO]
    counts = jax.random.randint(keys[2], (OFFSETS,), -(active // 2), active + 1)
    counts = jnp.maximum(counts, 0)
    counts = jnp.where(dense, TILES_DEV, counts)
    counts = counts.at[OFFSETS // 2].set(active)
    place = jnp.arange(PER_OFFSET * BLOCK, dtype=jnp.int32).reshape(PER_OFFSET, BLOCK)
    used = place[None] < counts[:, None, None]
    picked = orders[:, jnp.minimum(place, TILES_DEV - 1).reshape(-1)].reshape(OFFSETS, PER_OFFSET, BLOCK)
    outputs = jnp.where(used, picked, TILES_DEV)
    shape = (OFFSETS, PER_OFFSET, BLOCK)
    from_halo = jax.random.randint(keys[3], shape, 0, 4) == 0
    halo_slot = jax.random.randint(keys[4], shape, TILES_DEV, TILES_DEV + 8 * HALO)
    local_slot = jax.random.randint(keys[5], shape, 0, active)
    inputs = jnp.where(from_halo, halo_slot, local_slot)
    center = (jnp.arange(OFFSETS) == OFFSETS // 2)[:, None, None]
    inputs = jnp.where(center, picked, inputs)
    inputs = inputs.at[OFFSETS // 2, 0, 0].set(TILES_DEV + 8 * HALO - 1)
    inputs = jnp.where(used, inputs, 0)
    group_score = jax.random.randint(keys[6], (OFFSETS,), 0, 4096) * OFFSETS + jnp.arange(OFFSETS)
    group_place = jnp.argsort(jnp.argsort(group_score))
    live = (place[None, :, 0] < counts[:, None]).reshape(-1)
    block_index = jnp.arange(BLOCKS)
    rank = jnp.where(live, 0, 1) * BLOCKS + group_place[block_index // PER_OFFSET] * PER_OFFSET + block_index % PER_OFFSET
    order = jnp.argsort(rank)
    offsets = jnp.where(live, jnp.repeat(jnp.arange(OFFSETS), PER_OFFSET), 0)[order]
    block_in = inputs.reshape(BLOCKS, BLOCK)[order]
    block_out = outputs.reshape(BLOCKS, BLOCK)[order]
    return (sends.astype(jnp.int32), offsets.astype(jnp.int32), block_in.astype(jnp.int32), block_out.astype(jnp.int32), jnp.sum(live).astype(jnp.int32))


def plan(key):
    keys = jax.random.split(jax.random.fold_in(key, 11), 4)
    devices_all = SLABS_X * SLABS_Y
    dense = jax.random.randint(keys[0], (devices_all,), 0, 4) == 0
    chosen = jax.random.randint(keys[1], (), 0, devices_all)
    dense = dense | (jnp.arange(devices_all) == chosen)
    light = jax.random.randint(keys[2], (devices_all,), TILES_DEV // 3, TILES_DEV // 2 + 1)
    active = jnp.where(dense, TILES_DEV, light)
    pieces = jax.vmap(device_plan)(jax.random.split(keys[3], devices_all), active, dense)
    return [piece.reshape((SLABS_X, SLABS_Y) + piece.shape[1:]) for piece in pieces]


def draw_send_lists(key, part):
    return plan(key)[0]


def draw_block_offset(key, part):
    return plan(key)[1]


def draw_block_input(key, part):
    return plan(key)[2]


def draw_block_output(key, part):
    return plan(key)[3]


def draw_block_count(key, part):
    return plan(key)[4]


def steps_of(stream_key, dims, cuts, low, largest):
    def one(position, shards_of):
        draws = jax.random.uniform(jax.random.fold_in(jax.random.fold_in(stream_key, 6), position), (shards_of,), jnp.float32, low / len(cuts), largest / len(cuts))
        return jnp.repeat(jnp.exp(draws), dims[position] // shards_of).reshape((-1,) + (1,) * (len(dims) - position - 1))

    gain = one(*cuts[0])
    for cut in cuts[1:]:
        gain = gain * one(*cut)
    return gain


def scatter_about(key, extent, width, limit, shards=(), kind=jnp.bfloat16):
    level = steps_of(key, extent, shards, -0.22, 0.18) if shards else 1.0
    values = jax.random.normal(key, extent, jnp.float32) * width * level
    return jnp.minimum(jnp.maximum(values, -limit), limit).astype(kind)


def setup_inputs(seed: int = 0) -> dict:
    streams_of = jax.random.split(jax.random.key(seed), 9)
    features = scatter_about(streams_of[0], (SLABS_X, SLABS_Y, TILES_DEV, VOXELS, CHANNELS), 1.0, 6.0, ((0, 8), (1, 4)))
    weights = scatter_about(streams_of[1], (OFFSETS, CHANNELS, CHANNELS), (OFFSETS * CHANNELS) ** -0.5, 0.078125)
    cotangent = scatter_about(streams_of[2], (SLABS_X, SLABS_Y, TILES_DEV, VOXELS, CHANNELS), 1.0, 6.0, ((0, 8), (1, 4)))
    send_lists = draw_send_lists(jax.random.fold_in(streams_of[8], 71), 0)
    block_offset = draw_block_offset(jax.random.fold_in(streams_of[8], 71), 0)
    block_input = draw_block_input(jax.random.fold_in(streams_of[8], 71), 0)
    block_output = draw_block_output(jax.random.fold_in(streams_of[8], 71), 0)
    block_count = draw_block_count(jax.random.fold_in(streams_of[8], 71), 0)
    return {"features": features, "weights": weights, "cotangent": cotangent, "send_lists": send_lists, "block_offset": block_offset, "block_input": block_input, "block_output": block_output, "block_count": block_count}


DIRECTIONS = ((-1, -1), (-1, 0), (-1, 1), (0, -1), (0, 1), (1, -1), (1, 0), (1, 1))

def neighbour(array, step_x, step_y):
    rolled = jnp.roll(array, (step_x, step_y), axis=(0, 1))
    first = jnp.arange(array.shape[0]) - step_x
    second = jnp.arange(array.shape[1]) - step_y
    inside = ((first >= 0) & (first < array.shape[0]))[:, None] & ((second >= 0) & (second < array.shape[1]))[None, :]
    inside = inside.reshape(inside.shape + (1,) * (array.ndim - 2))
    return jnp.where(inside, rolled, jnp.zeros_like(rolled))

def by_device(array):
    return array.reshape((SLABS_X * SLABS_Y,) + array.shape[2:])

def take_rows(table, places):
    return table[places]

def add_rows(target, places, values):
    return target.at[places].add(values)

def reference(features, weights, cotangent, send_lists, block_offset, block_input, block_output, block_count):
    packets = jax.vmap(jax.vmap(take_rows))(features, send_lists)
    halos = jnp.stack([neighbour(packets[:, :, which], pair[0], pair[1]) for which, pair in enumerate(DIRECTIONS)], axis=2)
    extended = jnp.concatenate([features, halos.reshape(SLABS_X, SLABS_Y, 8 * HALO, VOXELS, CHANNELS)], axis=2)
    live = jnp.arange(BLOCKS)[None, None, :, None] < block_count[:, :, None, None]
    outputs = jnp.where(live, block_output, TILES_DEV).astype(jnp.int32)

    def forward_device(item):
        ext, offsets, inputs, targets = item

        def step(accum, blocks):
            offset, source, target = blocks
            gathered = ext[source].reshape(BLOCK * VOXELS, CHANNELS)
            product = jnp.dot(gathered, weights[offset], preferred_element_type=jnp.float32)
            return (accum.at[target].add(product.reshape(BLOCK, VOXELS, CHANNELS), mode='drop'), None)
        result, _ = lax.scan(step, jnp.zeros((TILES_DEV, VOXELS, CHANNELS), jnp.float32), (offsets, inputs, targets))
        return result
    items = (by_device(extended), by_device(block_offset), by_device(block_input), by_device(outputs))
    pre = lax.map(forward_device, items).reshape(features.shape)
    sigma = jax.nn.sigmoid(pre)
    out_features = (features.astype(jnp.float32) + pre * sigma).astype(jnp.bfloat16)
    pre_grad = (cotangent.astype(jnp.float32) * sigma * (1.0 + pre * (1.0 - sigma))).astype(jnp.bfloat16)
    padded_grad = jnp.concatenate([pre_grad, jnp.zeros((SLABS_X, SLABS_Y, 1, VOXELS, CHANNELS), jnp.bfloat16)], axis=2)

    def backward_device(weight_sum, item):
        ext, grads, offsets, inputs, targets = item

        def step(carry, blocks):
            ext_grad, partial_value = carry
            offset, source, target = blocks
            gathered = ext[source].reshape(BLOCK * VOXELS, CHANNELS)
            incoming = grads[target].reshape(BLOCK * VOXELS, CHANNELS)
            back = jnp.dot(incoming, weights[offset].T, preferred_element_type=jnp.float32)
            ext_grad = ext_grad.at[source].add(back.reshape(BLOCK, VOXELS, CHANNELS))
            partial_value = partial_value.at[offset].add(jnp.dot(gathered.T, incoming, preferred_element_type=jnp.float32))
            return ((ext_grad, partial_value), None)
        start = jnp.zeros((TILES_DEV + 8 * HALO, VOXELS, CHANNELS), jnp.float32)
        (ext_grad, weight_sum), _ = lax.scan(step, (start, weight_sum), (offsets, inputs, targets))
        return (weight_sum, ext_grad)
    items = (by_device(extended), by_device(padded_grad), by_device(block_offset), by_device(block_input), by_device(outputs))
    weight_sum, ext_grad = lax.scan(backward_device, jnp.zeros((OFFSETS, CHANNELS, CHANNELS), jnp.float32), items)
    ext_grad = ext_grad.reshape(SLABS_X, SLABS_Y, TILES_DEV + 8 * HALO, VOXELS, CHANNELS)
    adjoints = ext_grad[:, :, TILES_DEV:].reshape(SLABS_X, SLABS_Y, 8, HALO, VOXELS, CHANNELS)
    feat_sum = cotangent.astype(jnp.float32) + ext_grad[:, :, :TILES_DEV]
    for which, pair in enumerate(DIRECTIONS):
        returned = neighbour(adjoints[:, :, which], -pair[0], -pair[1])
        feat_sum = jax.vmap(jax.vmap(add_rows))(feat_sum, send_lists[:, :, which], returned)
    feat_grad = feat_sum.astype(jnp.bfloat16)
    weight_grad = weight_sum / math.sqrt(VOXELS * TILES_ALL)
    return (out_features, feat_grad, weight_grad)
```

```python
import math

import jax
import jax.numpy as jnp
from jax import lax
from jax.experimental import pallas as pl
from jax.experimental.pallas import tpu as pltpu
from jax.sharding import PartitionSpec as P

DIRECTIONS = ((-1, -1), (-1, 0), (-1, 1), (0, -1), (0, 1), (1, -1), (1, 0), (1, 1))
MIB = 1024 * 1024
ANY = pl.BlockSpec(memory_space=pl.ANY)
VMEM = pl.BlockSpec(memory_space=pltpu.VMEM)
SMEM = pl.BlockSpec(memory_space=pltpu.SMEM)


def chunk_of(size, wanted):
    return max(c for c in range(1, wanted + 1) if size % c == 0)


def travel(packet, step_x, step_y):
    size_x, size_y = lax.axis_size("gx"), lax.axis_size("gy")
    pairs = [
        (i * size_y + j, (i + step_x) * size_y + j + step_y)
        for i in range(size_x)
        for j in range(size_y)
        if 0 <= i + step_x < size_x and 0 <= j + step_y < size_y
    ]
    return lax.ppermute(packet, ("gx", "gy"), pairs)


def pack(tiles, lists):
    directions, halo = lists.shape
    _, voxels, channels = tiles.shape

    def kernel(lists_ref, tiles_ref, *packets):
        for d in range(directions):
            for h in range(halo):
                packets[d][h] = tiles_ref[lists_ref[d, h]]

    return pl.pallas_call(
        kernel,
        out_shape=[jax.ShapeDtypeStruct((halo, voxels, channels), tiles.dtype)] * directions,
        in_specs=[SMEM, VMEM],
        out_specs=[VMEM] * directions,
        compiler_params=pltpu.CompilerParams(vmem_limit_bytes=16 * MIB),
        name="pack",
    )(lists, tiles)


def source_table(offsets, inputs, outputs, count, offset_count, tile_slots, empty):
    blocks, rows = inputs.shape

    def kernel(offsets_ref, inputs_ref, outputs_ref, count_ref, table_ref):
        def clear(k, carry):
            for t in range(tile_slots):
                table_ref[k, t] = empty
            return carry

        lax.fori_loop(0, offset_count, clear, 0)

        def block(n, carry):
            k = offsets_ref[n]
            for q in range(rows):
                target = outputs_ref[n, q]

                @pl.when(target < tile_slots)
                def _():
                    table_ref[k, target] = inputs_ref[n, q]

            return carry

        lax.fori_loop(0, jnp.minimum(count_ref[0], blocks), block, 0)

    return pl.pallas_call(
        kernel,
        out_shape=jax.ShapeDtypeStruct((offset_count, tile_slots), jnp.int32),
        in_specs=[SMEM] * 4,
        out_specs=SMEM,
        name="source_table",
    )(offsets, inputs, outputs, count)


def forward(table, tiles, halos, weights, cotangent, scale):
    tile_slots, voxels, channels = tiles.shape
    offset_count = weights.shape[0]
    halo = halos[0].shape[0]
    directions = len(halos)
    empty = tile_slots + directions * halo
    group = chunk_of(tile_slots, 8)
    groups = tile_slots // group
    rows = group * voxels
    deep = chunk_of(offset_count, 3)

    def kernel(table_ref, tiles_ref, *refs):
        halo_refs = refs[:directions]
        w_ref, cot_ref, out_ref, grad_ref, wgrad_ref, ext, acc, turned, sems = refs[directions:]
        copies = [pltpu.make_async_copy(tiles_ref, ext.at[pl.ds(0, tile_slots)], sems.at[0])]
        for d in range(directions):
            copies.append(
                pltpu.make_async_copy(
                    halo_refs[d], ext.at[pl.ds(tile_slots + d * halo, halo)], sems.at[d + 1]
                )
            )
        for copy in copies:
            copy.start()
        ext[empty] = jnp.zeros((voxels, channels), ext.dtype)
        acc[...] = jnp.zeros_like(acc)
        for copy in copies:
            copy.wait()

        def gathered(k, first, count):
            return jnp.concatenate([ext[table_ref[k, first + t]] for t in range(count)], axis=0)

        def forward_turn(turn, carry):
            mats = w_ref[pl.ds(turn * deep, deep)].reshape(deep * channels, channels)
            for g in range(groups):
                lhs = jnp.concatenate(
                    [gathered(turn * deep + j, g * group, group) for j in range(deep)], axis=1
                )
                acc[g] += jnp.dot(lhs, mats, preferred_element_type=jnp.float32)
            return carry

        lax.fori_loop(0, offset_count // deep, forward_turn, 0)

        def finish(t, carry):
            pre = acc[t // group, pl.ds(pl.multiple_of((t % group) * voxels, voxels), voxels), :]
            sigma = jax.nn.sigmoid(pre)
            out_ref[t] = (ext[t].astype(jnp.float32) + pre * sigma).astype(out_ref.dtype)
            incoming = cot_ref[t].astype(jnp.float32)
            grad = incoming * sigma * (1.0 + pre * (1.0 - sigma))
            grad_ref[t] = grad.astype(grad_ref.dtype)
            return carry

        lax.fori_loop(0, tile_slots, finish, 0)
        for g in range(groups):
            part = grad_ref[pl.ds(g * group, group)].reshape(rows, channels)
            turned[:, pl.ds(g * rows, rows)] = part.astype(jnp.float32).T.astype(turned.dtype)

        def weight_turn(k, carry):
            terms = jnp.dot(
                turned[...], gathered(k, 0, tile_slots), preferred_element_type=jnp.float32
            )
            wgrad_ref[k] = (terms.T * scale).astype(wgrad_ref.dtype)
            return carry

        lax.fori_loop(0, offset_count, weight_turn, 0)

    flops = 4 * offset_count * tile_slots * voxels * channels * channels
    return pl.pallas_call(
        kernel,
        out_shape=[
            jax.ShapeDtypeStruct(tiles.shape, jnp.bfloat16),
            jax.ShapeDtypeStruct(tiles.shape, jnp.bfloat16),
            jax.ShapeDtypeStruct(weights.shape, jnp.float32),
        ],
        in_specs=[SMEM, ANY] + [ANY] * directions + [VMEM, VMEM],
        out_specs=[VMEM, VMEM, VMEM],
        scratch_shapes=[
            pltpu.VMEM((empty + 1, voxels, channels), jnp.bfloat16),
            pltpu.VMEM((groups, rows, channels), jnp.float32),
            pltpu.VMEM((channels, tile_slots * voxels), jnp.bfloat16),
            pltpu.SemaphoreType.DMA((directions + 1,)),
        ],
        compiler_params=pltpu.CompilerParams(vmem_limit_bytes=48 * MIB),
        cost_estimate=pl.CostEstimate(flops=flops, bytes_accessed=20 * MIB, transcendentals=0),
        name="forward_and_weight_grad",
    )(table, tiles, *halos, weights, cotangent)


def input_grad(table, pre_grad, weights, directions, halo):
    tile_slots, voxels, channels = pre_grad.shape
    offset_count = weights.shape[0]
    empty = tile_slots + directions * halo
    group = chunk_of(tile_slots, 8)
    groups = tile_slots // group
    rows = group * voxels

    def kernel(table_ref, grad_ref, w_ref, own_ref, *refs):
        adjoints = refs[:directions]
        sums = refs[directions:]
        for one in sums:
            one[...] = jnp.zeros_like(one)

        def turn(k, carry):
            for g in range(groups):
                back = lax.dot_general(
                    grad_ref[pl.ds(g * group, group)].reshape(rows, channels),
                    w_ref[k],
                    (((1,), (1,)), ((), ())),
                    preferred_element_type=jnp.float32,
                )
                for t in range(group):
                    slot = table_ref[k, g * group + t]
                    sums[t % 2][slot] += back[t * voxels : (t + 1) * voxels]
            return carry

        lax.fori_loop(0, offset_count, turn, 0)

        def own(t, carry):
            own_ref[t] = sums[0][t] + sums[1][t]
            return carry

        lax.fori_loop(0, tile_slots, own, 0)
        for d in range(directions):
            for h in range(halo):
                slot = tile_slots + d * halo + h
                adjoints[d][h] = (sums[0][slot] + sums[1][slot]).astype(jnp.bfloat16)

    flops = 2 * offset_count * tile_slots * voxels * channels * channels
    return pl.pallas_call(
        kernel,
        out_shape=[jax.ShapeDtypeStruct(pre_grad.shape, jnp.float32)]
        + [jax.ShapeDtypeStruct((halo, voxels, channels), jnp.bfloat16)] * directions,
        in_specs=[SMEM, VMEM, VMEM],
        out_specs=[VMEM] * (directions + 1),
        scratch_shapes=[pltpu.VMEM((empty + 1, voxels, channels), jnp.float32)] * 2,
        compiler_params=pltpu.CompilerParams(vmem_limit_bytes=48 * MIB),
        cost_estimate=pl.CostEstimate(flops=flops, bytes_accessed=12 * MIB, transcendentals=0),
        name="input_grad",
    )(table, pre_grad, weights)


def combine(lists, own, cotangent, returned):
    directions, halo = lists.shape
    tile_slots, voxels, channels = own.shape

    def kernel(lists_ref, own_ref, cot_ref, *refs):
        returned_refs = refs[:directions]
        out_ref, acc = refs[directions:]

        def start(t, carry):
            acc[t] = own_ref[t] + cot_ref[t].astype(jnp.float32)
            return carry

        lax.fori_loop(0, tile_slots, start, 0)
        for d in range(directions):
            for h in range(halo):
                acc[lists_ref[d, h]] += returned_refs[d][h].astype(jnp.float32)

        def finish(t, carry):
            out_ref[t] = acc[t].astype(out_ref.dtype)
            return carry

        lax.fori_loop(0, tile_slots, finish, 0)

    return pl.pallas_call(
        kernel,
        out_shape=jax.ShapeDtypeStruct(own.shape, jnp.bfloat16),
        in_specs=[SMEM] + [VMEM] * (directions + 2),
        out_specs=VMEM,
        scratch_shapes=[pltpu.VMEM(own.shape, jnp.float32)],
        compiler_params=pltpu.CompilerParams(vmem_limit_bytes=32 * MIB),
        name="combine",
    )(lists, own, cotangent, *returned)


def shards(
    features, weights, cotangent, send_lists, block_offset, block_input, block_output, block_count
):
    tiles = features[0, 0]
    incoming = cotangent[0, 0]
    lists = send_lists[0, 0]
    tile_slots, voxels, channels = tiles.shape
    directions, halo = lists.shape
    device_total = lax.axis_size("gx") * lax.axis_size("gy")
    scale = 1.0 / math.sqrt(voxels * tile_slots * device_total)

    packets = pack(tiles, lists)
    halos = [travel(packets[d], *DIRECTIONS[d]) for d in range(directions)]
    table = source_table(
        block_offset[0, 0],
        block_input[0, 0],
        block_output[0, 0],
        block_count[0],
        weights.shape[0],
        tile_slots,
        tile_slots + directions * halo,
    )
    out_features, pre_grad, weight_part = forward(table, tiles, halos, weights, incoming, scale)
    weight_grad = lax.psum(weight_part, ("gx", "gy"))
    own, *adjoints = input_grad(table, pre_grad, weights, directions, halo)
    returned = [
        travel(adjoints[d], -DIRECTIONS[d][0], -DIRECTIONS[d][1]) for d in range(directions)
    ]
    feat_grad = combine(lists, own, incoming, returned)
    return (out_features[None, None], feat_grad[None, None], weight_grad)


def solution(mesh):
    in_specs = (
        P("gx", "gy", None, None, None),
        P(),
        P("gx", "gy", None, None, None),
        P("gx", "gy", None, None),
        P("gx", "gy", None),
        P("gx", "gy", None, None),
        P("gx", "gy", None, None),
        P("gx", "gy"),
    )
    out_specs = (P("gx", "gy", None, None, None), P("gx", "gy", None, None, None), P())
    return jax.shard_map(shards, mesh=mesh, in_specs=in_specs, out_specs=out_specs, check_vma=False)
```

```python
import math

import jax
import jax.numpy as jnp
from jax import lax
from jax.experimental import pallas as pl
from jax.experimental.pallas import tpu as pltpu
from jax.sharding import PartitionSpec as P

DIRECTIONS = ((-1, -1), (-1, 0), (-1, 1), (0, -1), (0, 1), (1, -1), (1, 0), (1, 1))
MIB = 1024 * 1024
ANY = pl.BlockSpec(memory_space=pl.ANY)
VMEM = pl.BlockSpec(memory_space=pltpu.VMEM)
SMEM = pl.BlockSpec(memory_space=pltpu.SMEM)


def chunk_of(size, wanted):
    return max(c for c in range(1, wanted + 1) if size % c == 0)


def travel(packet, step_x, step_y):
    size_x, size_y = lax.axis_size("gx"), lax.axis_size("gy")
    pairs = [
        (i * size_y + j, (i + step_x) * size_y + j + step_y)
        for i in range(size_x)
        for j in range(size_y)
        if 0 <= i + step_x < size_x and 0 <= j + step_y < size_y
    ]
    return lax.ppermute(packet, ("gx", "gy"), pairs)


def pack(tiles, lists, first, count):
    halo = lists.shape[1]
    _, voxels, channels = tiles.shape

    def kernel(lists_ref, tiles_ref, *packets):
        for d in range(count):
            for h in range(halo):
                packets[d][h] = tiles_ref[lists_ref[first + d, h]]

    return pl.pallas_call(
        kernel,
        out_shape=[jax.ShapeDtypeStruct((halo, voxels, channels), tiles.dtype)] * count,
        in_specs=[SMEM, VMEM],
        out_specs=[VMEM] * count,
        compiler_params=pltpu.CompilerParams(vmem_limit_bytes=16 * MIB),
        name="pack",
    )(lists, tiles)


def pack_and_table(tiles, lists, first, offsets, inputs, outputs, count, offset_count, after):
    directions, halo = lists.shape
    tile_slots, voxels, channels = tiles.shape
    blocks, rows = inputs.shape
    empty = tile_slots + directions * halo
    packed = directions - first

    def kernel(lists_ref, offsets_ref, inputs_ref, outputs_ref, count_ref, tiles_ref, _, table_ref, *packets):
        for d in range(packed):
            for h in range(halo):
                packets[d][h] = tiles_ref[lists_ref[first + d, h]]

        def clear(k, carry):
            for t in range(tile_slots):
                table_ref[k, t] = empty
            return carry

        lax.fori_loop(0, offset_count, clear, 0)

        def block(n, carry):
            k = offsets_ref[n]
            for q in range(rows):
                target = outputs_ref[n, q]

                @pl.when(target < tile_slots)
                def _():
                    table_ref[k, target] = inputs_ref[n, q]

            return carry

        lax.fori_loop(0, jnp.minimum(count_ref[0], blocks), block, 0)

    return pl.pallas_call(
        kernel,
        out_shape=[jax.ShapeDtypeStruct((offset_count, tile_slots), jnp.int32)]
        + [jax.ShapeDtypeStruct((halo, voxels, channels), tiles.dtype)] * packed,
        in_specs=[SMEM] * 5 + [VMEM, ANY],
        out_specs=[SMEM] + [VMEM] * packed,
        compiler_params=pltpu.CompilerParams(vmem_limit_bytes=16 * MIB),
        name="pack_and_table",
    )(lists, offsets, inputs, outputs, count, tiles, after)


def extended_copies(tiles_ref, halo_refs, ext, sems):
    tile_slots, halo = tiles_ref.shape[0], halo_refs[0].shape[0]
    copies = [pltpu.make_async_copy(tiles_ref, ext.at[pl.ds(0, tile_slots)], sems.at[0])]
    for d, halo_ref in enumerate(halo_refs):
        place = ext.at[pl.ds(tile_slots + d * halo, halo)]
        copies.append(pltpu.make_async_copy(halo_ref, place, sems.at[d + 1]))
    return copies


def gathered(table_ref, ext, k, first, count):
    return jnp.concatenate([ext[table_ref[k, first + t]] for t in range(count)], axis=0)


def forward(table, tiles, halos, weights, cotangent):
    tile_slots, voxels, channels = tiles.shape
    offset_count = weights.shape[0]
    directions = len(halos)
    empty = tile_slots + directions * halos[0].shape[0]
    group = chunk_of(tile_slots, 8)
    groups = tile_slots // group
    rows = group * voxels
    deep = chunk_of(offset_count, 9)

    def kernel(table_ref, tiles_ref, *refs):
        halo_refs = refs[:directions]
        w_ref, cot_ref, out_ref, grad_ref, turned_ref, ext, acc, sems = refs[directions:]
        copies = extended_copies(tiles_ref, halo_refs, ext, sems)
        for copy in copies:
            copy.start()
        ext[empty] = jnp.zeros((voxels, channels), ext.dtype)
        acc[...] = jnp.zeros_like(acc)
        for copy in copies:
            copy.wait()

        def turn(step, carry):
            mats = w_ref[pl.ds(step * deep, deep)].reshape(deep * channels, channels)
            for g in range(groups):
                lhs = jnp.concatenate(
                    [
                        gathered(table_ref, ext, step * deep + j, g * group, group)
                        for j in range(deep)
                    ],
                    axis=1,
                )
                acc[g] += jnp.dot(lhs, mats, preferred_element_type=jnp.float32)
            return carry

        lax.fori_loop(0, offset_count // deep, turn, 0)

        def finish(t, carry):
            pre = acc[t // group, pl.ds(pl.multiple_of((t % group) * voxels, voxels), voxels), :]
            sigma = jax.nn.sigmoid(pre)
            out_ref[t] = (ext[t].astype(jnp.float32) + pre * sigma).astype(out_ref.dtype)
            incoming = cot_ref[t].astype(jnp.float32)
            grad = incoming * sigma * (1.0 + pre * (1.0 - sigma))
            grad_ref[t] = grad.astype(grad_ref.dtype)
            return carry

        lax.fori_loop(0, tile_slots, finish, 0)
        for g in range(groups):
            part = grad_ref[pl.ds(g * group, group)].reshape(rows, channels)
            turned_ref[:, pl.ds(g * rows, rows)] = part.astype(jnp.float32).T.astype(jnp.bfloat16)

    flops = 2 * offset_count * tile_slots * voxels * channels * channels
    return pl.pallas_call(
        kernel,
        out_shape=[
            jax.ShapeDtypeStruct(tiles.shape, jnp.bfloat16),
            jax.ShapeDtypeStruct(tiles.shape, jnp.bfloat16),
            jax.ShapeDtypeStruct((channels, tile_slots * voxels), jnp.bfloat16),
        ],
        in_specs=[SMEM, ANY] + [ANY] * directions + [VMEM, VMEM],
        out_specs=[VMEM, VMEM, VMEM],
        scratch_shapes=[
            pltpu.VMEM((empty + 1, voxels, channels), jnp.bfloat16),
            pltpu.VMEM((groups, rows, channels), jnp.float32),
            pltpu.SemaphoreType.DMA((directions + 1,)),
        ],
        compiler_params=pltpu.CompilerParams(vmem_limit_bytes=40 * MIB),
        cost_estimate=pl.CostEstimate(flops=flops, bytes_accessed=12 * MIB, transcendentals=0),
        name="forward",
    )(table, tiles, *halos, weights, cotangent)


def weight_terms(table, core, tiles, halos, turned, first, count, scale):
    tile_slots, voxels, channels = tiles.shape
    directions = len(halos)
    empty = tile_slots + directions * halos[0].shape[0]
    part = channels // 2

    def kernel(table_ref, core_ref, tiles_ref, *refs):
        halo_refs = refs[:directions]
        turned_ref, keep_ref, send_ref, ext, sems = refs[directions:]
        copies = extended_copies(tiles_ref, halo_refs, ext, sems)
        for copy in copies:
            copy.start()
        ext[empty] = jnp.zeros((voxels, channels), ext.dtype)
        for copy in copies:
            copy.wait()

        def turn(k, carry):
            terms = jnp.dot(
                turned_ref[...],
                gathered(table_ref, ext, first + k, 0, tile_slots),
                preferred_element_type=jnp.float32,
            )
            terms = terms.T * scale
            for h in range(2):
                place = 2 * k + h
                half = (place >= count).astype(jnp.int32)
                rest = place - half * count
                values = terms[h * part : (h + 1) * part]

                @pl.when(half == core_ref[0])
                def _():
                    keep_ref[rest] = values

                @pl.when(half != core_ref[0])
                def _():
                    send_ref[rest] = values

            return carry

        lax.fori_loop(0, count, turn, 0)

    flops = 2 * count * tile_slots * voxels * channels * channels
    return pl.pallas_call(
        kernel,
        out_shape=[jax.ShapeDtypeStruct((count, part, channels), jnp.float32)] * 2,
        in_specs=[SMEM, SMEM, ANY] + [ANY] * directions + [VMEM],
        out_specs=[VMEM, VMEM],
        scratch_shapes=[
            pltpu.VMEM((empty + 1, voxels, channels), jnp.bfloat16),
            pltpu.SemaphoreType.DMA((directions + 1,)),
        ],
        compiler_params=pltpu.CompilerParams(vmem_limit_bytes=32 * MIB),
        cost_estimate=pl.CostEstimate(flops=flops, bytes_accessed=12 * MIB, transcendentals=0),
        name="weight_terms",
    )(table, core, tiles, *halos, turned)


def to_other_core(x):
    size = lax.axis_size("gx")
    return lax.ppermute(x, "gx", [(i, i ^ 1) for i in range(size)])


def along_chips(x, by):
    size = lax.axis_size("gx")
    return lax.ppermute(x, "gx", [(i, (i + 2 * by) % size) for i in range(size)])


def along_gy(x, by):
    size = lax.axis_size("gy")
    return lax.ppermute(x, "gy", [(j, (j + by) % size) for j in range(size)])


def summed_half(keep, received, levels):
    rows, channels = keep.shape[0] * keep.shape[1], keep.shape[2]
    total = (keep + received).reshape(rows, channels)
    for size, place, move in levels:
        blocks = total.reshape(size, total.shape[0] // size, channels)
        parts = [
            lax.dynamic_index_in_dim(blocks, (place + s) % size, keepdims=False) for s in range(size)
        ]
        moved = [move(parts[s].astype(jnp.bfloat16), s) for s in range(1, size)]
        total = parts[0]
        for one in moved:
            total = total + one.astype(jnp.float32)
    piece = total.astype(jnp.bfloat16)
    for size, place, move in levels[::-1]:
        whole = jnp.zeros((size,) + piece.shape, piece.dtype)
        for s in range(size):
            one = piece if s == 0 else move(piece, -s)
            whole = lax.dynamic_update_index_in_dim(whole, one, (place + s) % size, 0)
        piece = whole.reshape(size * piece.shape[0], channels)
    return piece


def widen(core, near, far):
    step, channels = near[0].shape

    def kernel(core_ref, far_own, far_other, near_own, near_other, out_ref):
        turn = pl.program_id(0)
        half = jnp.where(turn < 4, turn // 2, turn - 4)
        mine = half == core_ref[0]
        for late, own_ref, other_ref in ((False, far_own, far_other), (True, near_own, near_other)):
            here = (turn >= 4) == late

            @pl.when(here & mine)
            def _():
                out_ref[...] = own_ref[...].astype(jnp.float32)

            @pl.when(here & jnp.logical_not(mine))
            def _():
                out_ref[...] = other_ref[...].astype(jnp.float32)

    far_spec = pl.BlockSpec((step, channels), lambda i: (jnp.where(i < 4, i % 2, 1), 0))
    near_spec = pl.BlockSpec((step, channels), lambda i: (0, 0))
    return pl.pallas_call(
        kernel,
        grid=(6,),
        out_shape=jax.ShapeDtypeStruct((6 * step, channels), jnp.float32),
        in_specs=[SMEM, far_spec, far_spec, near_spec, near_spec],
        out_specs=pl.BlockSpec((step, channels), lambda i: (i, 0)),
        compiler_params=pltpu.CompilerParams(vmem_limit_bytes=24 * MIB),
        name="widen",
    )(core, *far, *near)


def input_grad(table, pre_grad, weights, directions, halo):
    tile_slots, voxels, channels = pre_grad.shape
    offset_count = weights.shape[0]
    empty = tile_slots + directions * halo
    group = chunk_of(tile_slots, 8)
    groups = tile_slots // group
    rows = group * voxels

    def kernel(table_ref, grad_ref, w_ref, own_ref, *refs):
        adjoints = refs[:directions]
        sums = refs[directions:]
        for one in sums:
            one[...] = jnp.zeros_like(one)

        def turn(k, carry):
            for g in range(groups):
                back = lax.dot_general(
                    grad_ref[pl.ds(g * group, group)].reshape(rows, channels),
                    w_ref[k],
                    (((1,), (1,)), ((), ())),
                    preferred_element_type=jnp.float32,
                )
                for t in range(group):
                    slot = table_ref[k, g * group + t]
                    sums[t % 2][slot] += back[t * voxels : (t + 1) * voxels]
            return carry

        lax.fori_loop(0, offset_count, turn, 0)

        def own(t, carry):
            own_ref[t] = sums[0][t] + sums[1][t]
            return carry

        lax.fori_loop(0, tile_slots, own, 0)
        for d in range(directions):
            for h in range(halo):
                slot = tile_slots + d * halo + h
                adjoints[d][h] = (sums[0][slot] + sums[1][slot]).astype(jnp.bfloat16)

    flops = 2 * offset_count * tile_slots * voxels * channels * channels
    return pl.pallas_call(
        kernel,
        out_shape=[jax.ShapeDtypeStruct(pre_grad.shape, jnp.float32)]
        + [jax.ShapeDtypeStruct((halo, voxels, channels), jnp.bfloat16)] * directions,
        in_specs=[SMEM, VMEM, VMEM],
        out_specs=[VMEM] * (directions + 1),
        scratch_shapes=[pltpu.VMEM((empty + 1, voxels, channels), jnp.float32)] * 2,
        compiler_params=pltpu.CompilerParams(vmem_limit_bytes=48 * MIB),
        cost_estimate=pl.CostEstimate(flops=flops, bytes_accessed=12 * MIB, transcendentals=0),
        name="input_grad",
    )(table, pre_grad, weights)


def combine(lists, own, cotangent, returned):
    directions, halo = lists.shape
    tile_slots, voxels, channels = own.shape

    def kernel(lists_ref, own_ref, cot_ref, *refs):
        returned_refs = refs[:directions]
        out_ref, acc = refs[directions:]

        def start(t, carry):
            acc[t] = own_ref[t] + cot_ref[t].astype(jnp.float32)
            return carry

        lax.fori_loop(0, tile_slots, start, 0)
        for d in range(directions):
            for h in range(halo):
                acc[lists_ref[d, h]] += returned_refs[d][h].astype(jnp.float32)

        def finish(t, carry):
            out_ref[t] = acc[t].astype(out_ref.dtype)
            return carry

        lax.fori_loop(0, tile_slots, finish, 0)

    return pl.pallas_call(
        kernel,
        out_shape=jax.ShapeDtypeStruct(own.shape, jnp.bfloat16),
        in_specs=[SMEM] + [VMEM] * (directions + 2),
        out_specs=VMEM,
        scratch_shapes=[pltpu.VMEM(own.shape, jnp.float32)],
        compiler_params=pltpu.CompilerParams(vmem_limit_bytes=32 * MIB),
        name="combine",
    )(lists, own, cotangent, *returned)


def shards(
    features, weights, cotangent, send_lists, block_offset, block_input, block_output, block_count
):
    tiles = features[0, 0]
    incoming = cotangent[0, 0]
    lists = send_lists[0, 0]
    tile_slots, voxels, channels = tiles.shape
    directions, halo = lists.shape
    device_total = lax.axis_size("gx") * lax.axis_size("gy")
    scale = 1.0 / math.sqrt(voxels * tile_slots * device_total)

    offset_count = weights.shape[0]
    core = (lax.axis_index("gx") % 2).astype(jnp.int32)[None]

    order = sorted(range(directions), key=lambda d: DIRECTIONS[d][1] == 0)
    early = directions // 2
    ordered = lists[jnp.array(order)]
    packets = pack(tiles, ordered, 0, early)
    table, *rest = pack_and_table(
        tiles,
        ordered,
        early,
        block_offset[0, 0],
        block_input[0, 0],
        block_output[0, 0],
        block_count[0],
        offset_count,
        packets[0],
    )
    arrived = {d: travel(one, *DIRECTIONS[d]) for d, one in zip(order, [*packets, *rest])}
    halos = [arrived[d] for d in range(directions)]
    out_features, pre_grad, turned = forward(table, tiles, halos, weights, incoming)

    near = offset_count // 3
    far = offset_count - near
    chips, columns = lax.axis_size("gx") // 2, lax.axis_size("gy")
    by_chip = (chips, lax.axis_index("gx") // 2, along_chips)
    by_gy = (columns, lax.axis_index("gy"), along_gy)
    halves = []
    for first, count, levels in ((far, near, (by_chip, by_gy)), (0, far, (by_gy, by_chip))):
        keep, send = weight_terms(table, core, tiles, halos, turned, first, count, scale)
        own_half = summed_half(keep, to_other_core(send), levels)
        halves.append((own_half, to_other_core(own_half)))
    weight_grad = widen(core, *halves).reshape(weights.shape)
    own, *adjoints = input_grad(table, pre_grad, weights, directions, halo)
    returned = [
        travel(adjoints[d], -DIRECTIONS[d][0], -DIRECTIONS[d][1]) for d in range(directions)
    ]
    feat_grad = combine(lists, own, incoming, returned)
    return (out_features[None, None], feat_grad[None, None], weight_grad)


def solution(mesh):
    in_specs = (
        P("gx", "gy", None, None, None),
        P(),
        P("gx", "gy", None, None, None),
        P("gx", "gy", None, None),
        P("gx", "gy", None),
        P("gx", "gy", None, None),
        P("gx", "gy", None, None),
        P("gx", "gy"),
    )
    out_specs = (P("gx", "gy", None, None, None), P("gx", "gy", None, None, None), P())
    return jax.shard_map(shards, mesh=mesh, in_specs=in_specs, out_specs=out_specs, check_vma=False)
```

```python
import math

import jax
import jax.numpy as jnp
from jax import lax
from jax.experimental import pallas as pl
from jax.experimental.pallas import tpu as pltpu
from jax.sharding import PartitionSpec as P

DIRECTIONS = ((-1, -1), (-1, 0), (-1, 1), (0, -1), (0, 1), (1, -1), (1, 0), (1, 1))
MIB = 1024 * 1024
ANY = pl.BlockSpec(memory_space=pl.ANY)
VMEM = pl.BlockSpec(memory_space=pltpu.VMEM)
SMEM = pl.BlockSpec(memory_space=pltpu.SMEM)


def chunk_of(size, wanted):
    return max(c for c in range(1, wanted + 1) if size % c == 0)


def travel(packet, step_x, step_y):
    size_x, size_y = lax.axis_size("gx"), lax.axis_size("gy")
    pairs = [
        (i * size_y + j, (i + step_x) * size_y + j + step_y)
        for i in range(size_x)
        for j in range(size_y)
        if 0 <= i + step_x < size_x and 0 <= j + step_y < size_y
    ]
    return lax.ppermute(packet, ("gx", "gy"), pairs)


def start_packets(lists_ref, tiles_ref, chosen, packets, sems):
    waits = []
    for n, d in enumerate(chosen):
        halo = packets[n].shape[0]
        for h in range(halo):
            pltpu.make_async_copy(tiles_ref.at[lists_ref[d, h]], packets[n].at[h], sems.at[n]).start()
        waits.append(pltpu.make_async_copy(tiles_ref.at[pl.ds(0, halo)], packets[n], sems.at[n]))
    return waits


def pack(tiles, lists, chosen):
    halo = lists.shape[1]
    _, voxels, channels = tiles.shape

    def kernel(lists_ref, tiles_ref, *refs):
        for wait in start_packets(lists_ref, tiles_ref, chosen, refs[:-1], refs[-1]):
            wait.wait()

    return pl.pallas_call(
        kernel,
        out_shape=[jax.ShapeDtypeStruct((halo, voxels, channels), tiles.dtype)] * len(chosen),
        in_specs=[SMEM, ANY],
        out_specs=[VMEM] * len(chosen),
        scratch_shapes=[pltpu.SemaphoreType.DMA((len(chosen),))],
        compiler_params=pltpu.CompilerParams(vmem_limit_bytes=16 * MIB),
        name="pack",
    )(lists, tiles)


def pack_and_table(tiles, lists, chosen, offsets, inputs, outputs, count, offset_count, after):
    directions, halo = lists.shape
    tile_slots, voxels, channels = tiles.shape
    blocks, rows = inputs.shape
    empty = tile_slots + directions * halo

    def kernel(lists_ref, offsets_ref, inputs_ref, outputs_ref, count_ref, tiles_ref, _, table_ref, *refs):
        waits = start_packets(lists_ref, tiles_ref, chosen, refs[:-1], refs[-1])

        def clear(k, carry):
            for t in range(tile_slots):
                table_ref[k, t] = empty
            return carry

        lax.fori_loop(0, offset_count, clear, 0)

        def block(n, carry):
            k = offsets_ref[n]
            for q in range(rows):
                target = outputs_ref[n, q]

                @pl.when(target < tile_slots)
                def _():
                    table_ref[k, target] = inputs_ref[n, q]

            return carry

        lax.fori_loop(0, jnp.minimum(count_ref[0], blocks), block, 0)
        for wait in waits:
            wait.wait()

    return pl.pallas_call(
        kernel,
        out_shape=[jax.ShapeDtypeStruct((offset_count, tile_slots), jnp.int32)]
        + [jax.ShapeDtypeStruct((halo, voxels, channels), tiles.dtype)] * len(chosen),
        in_specs=[SMEM] * 5 + [ANY, ANY],
        out_specs=[SMEM] + [VMEM] * len(chosen),
        scratch_shapes=[pltpu.SemaphoreType.DMA((len(chosen),))],
        compiler_params=pltpu.CompilerParams(vmem_limit_bytes=16 * MIB),
        name="pack_and_table",
    )(lists, offsets, inputs, outputs, count, tiles, after)


def turn_weights(weights):
    def kernel(w_ref, out_ref):
        for k in range(w_ref.shape[0]):
            out_ref[k] = w_ref[k].astype(jnp.float32).T.astype(out_ref.dtype)

    offset_count, channels, _ = weights.shape
    step = chunk_of(offset_count, 3)
    spec = pl.BlockSpec((step, channels, channels), lambda k: (k, 0, 0))
    return pl.pallas_call(
        kernel,
        grid=(offset_count // step,),
        out_shape=jax.ShapeDtypeStruct(weights.shape, weights.dtype),
        in_specs=[spec],
        out_specs=spec,
        compiler_params=pltpu.CompilerParams(vmem_limit_bytes=16 * MIB),
        cost_estimate=pl.CostEstimate(flops=8 * 10**9, bytes_accessed=7 * MIB, transcendentals=0),
        name="turn_weights",
    )(weights)


def extended_copies(tiles_ref, halo_refs, ext, sems):
    tile_slots, halo = tiles_ref.shape[0], halo_refs[0].shape[0]
    copies = [pltpu.make_async_copy(tiles_ref, ext.at[pl.ds(0, tile_slots)], sems.at[0])]
    for d, halo_ref in enumerate(halo_refs):
        place = ext.at[pl.ds(tile_slots + d * halo, halo)]
        copies.append(pltpu.make_async_copy(halo_ref, place, sems.at[d + 1]))
    return copies


def gathered(table_ref, ext, k, first, count):
    return jnp.concatenate([ext[table_ref[k, first + t]] for t in range(count)], axis=0)


def forward_and_input_grad(table, tiles, halos, weights, turned_weights, cotangent):
    tile_slots, voxels, channels = tiles.shape
    offset_count = weights.shape[0]
    directions, halo = len(halos), halos[0].shape[0]
    empty = tile_slots + directions * halo
    group = chunk_of(tile_slots, 8)
    groups = tile_slots // group
    rows = group * voxels
    deep = chunk_of(offset_count, 9)
    unroll = chunk_of(offset_count, 3)

    def kernel(table_ref, tiles_ref, *refs):
        halo_refs, refs = refs[:directions], refs[directions:]
        w_hbm, wt_hbm, cot_hbm, out_ref, turned_ref, own_ref = refs[:6]
        adjoints, refs = refs[6 : 6 + directions], refs[6 + directions :]
        w_ref, wt_ref, cot_ref, ext, acc, grad, even, odd, sems, more = refs
        copies = extended_copies(tiles_ref, halo_refs, ext, sems)
        loads = [
            pltpu.make_async_copy(w_hbm, w_ref, more.at[0]),
            pltpu.make_async_copy(cot_hbm, cot_ref, more.at[1]),
            pltpu.make_async_copy(wt_hbm, wt_ref, more.at[2]),
        ]
        for copy in copies + loads:
            copy.start()
        ext[empty] = jnp.zeros((voxels, channels), ext.dtype)
        for one in (acc, even, odd):
            one[...] = jnp.zeros_like(one)
        for copy in copies + loads[:1]:
            copy.wait()

        def turn(step, carry):
            mats = w_ref[pl.ds(step * deep, deep)].reshape(deep * channels, channels)
            for g in range(groups):
                lhs = jnp.concatenate(
                    [
                        gathered(table_ref, ext, step * deep + j, g * group, group)
                        for j in range(deep)
                    ],
                    axis=1,
                )
                acc[g] += jnp.dot(lhs, mats, preferred_element_type=jnp.float32)
            return carry

        lax.fori_loop(0, offset_count // deep, turn, 0)
        for copy in loads[1:]:
            copy.wait()

        def finish(t, carry):
            pre = acc[t // group, pl.ds(pl.multiple_of((t % group) * voxels, voxels), voxels), :]
            sigma = jax.nn.sigmoid(pre)
            out_ref[t] = (ext[t].astype(jnp.float32) + pre * sigma).astype(out_ref.dtype)
            incoming = cot_ref[t].astype(jnp.float32)
            grad[t] = (incoming * sigma * (1.0 + pre * (1.0 - sigma))).astype(grad.dtype)
            return carry

        lax.fori_loop(0, tile_slots, finish, 0)
        for g in range(groups):
            part = grad[pl.ds(g * group, group)].reshape(rows, channels)
            turned_ref[:, pl.ds(g * rows, rows)] = part.astype(jnp.float32).T.astype(jnp.bfloat16)

        def back_turn(step, carry):
            for j in range(unroll):
                k = step * unroll + j
                for g in range(groups):
                    back = jnp.dot(
                        grad[pl.ds(g * group, group)].reshape(rows, channels),
                        wt_ref[k],
                        preferred_element_type=jnp.float32,
                    )
                    for t in range(group):
                        slot = table_ref[k, g * group + t]
                        sums = (even, odd)[t % 2]
                        sums[slot] += back[t * voxels : (t + 1) * voxels]
            return carry

        lax.fori_loop(0, offset_count // unroll, back_turn, 0)

        def own(t, carry):
            own_ref[t] = even[t] + odd[t]
            return carry

        lax.fori_loop(0, tile_slots, own, 0)
        for d in range(directions):
            for h in range(halo):
                slot = tile_slots + d * halo + h
                adjoints[d][h] = (even[slot] + odd[slot]).astype(jnp.bfloat16)

    flops = 4 * offset_count * tile_slots * voxels * channels * channels
    return pl.pallas_call(
        kernel,
        out_shape=[
            jax.ShapeDtypeStruct(tiles.shape, jnp.bfloat16),
            jax.ShapeDtypeStruct((channels, tile_slots * voxels), jnp.bfloat16),
            jax.ShapeDtypeStruct(tiles.shape, jnp.float32),
        ]
        + [jax.ShapeDtypeStruct((halo, voxels, channels), jnp.bfloat16)] * directions,
        in_specs=[SMEM] + [ANY] * (directions + 4),
        out_specs=[VMEM] * (directions + 3),
        scratch_shapes=[
            pltpu.VMEM(weights.shape, jnp.bfloat16),
            pltpu.VMEM(weights.shape, jnp.bfloat16),
            pltpu.VMEM(tiles.shape, jnp.bfloat16),
            pltpu.VMEM((empty + 1, voxels, channels), jnp.bfloat16),
            pltpu.VMEM((groups, rows, channels), jnp.float32),
            pltpu.VMEM(tiles.shape, jnp.bfloat16),
            pltpu.VMEM((empty + 1, voxels, channels), jnp.float32),
            pltpu.VMEM((empty + 1, voxels, channels), jnp.float32),
            pltpu.SemaphoreType.DMA((directions + 1,)),
            pltpu.SemaphoreType.DMA((3,)),
        ],
        compiler_params=pltpu.CompilerParams(vmem_limit_bytes=48 * MIB),
        cost_estimate=pl.CostEstimate(flops=flops, bytes_accessed=20 * MIB, transcendentals=0),
        name="forward_and_input_grad",
    )(table, tiles, *halos, weights, turned_weights, cotangent)


def weight_terms(table, core, tiles, halos, turned, first, count, scale):
    tile_slots, voxels, channels = tiles.shape
    directions = len(halos)
    empty = tile_slots + directions * halos[0].shape[0]
    part = channels // 2
    unroll = chunk_of(count, 3)

    def kernel(table_ref, core_ref, tiles_ref, *refs):
        halo_refs = refs[:directions]
        turned_ref, keep_ref, send_ref, ext, sems = refs[directions:]
        copies = extended_copies(tiles_ref, halo_refs, ext, sems)
        for copy in copies:
            copy.start()
        ext[empty] = jnp.zeros((voxels, channels), ext.dtype)
        for copy in copies:
            copy.wait()

        def one(k):
            terms = jnp.dot(
                turned_ref[...],
                gathered(table_ref, ext, first + k, 0, tile_slots),
                preferred_element_type=jnp.float32,
            )
            terms = terms.T * scale
            for h in range(2):
                place = 2 * k + h
                half = (place >= count).astype(jnp.int32)
                rest = place - half * count
                values = terms[h * part : (h + 1) * part]

                @pl.when(half == core_ref[0])
                def _():
                    keep_ref[rest] = values

                @pl.when(half != core_ref[0])
                def _():
                    send_ref[rest] = values

        def turn(step, carry):
            for j in range(unroll):
                one(step * unroll + j)
            return carry

        lax.fori_loop(0, count // unroll, turn, 0)

    flops = 2 * count * tile_slots * voxels * channels * channels
    return pl.pallas_call(
        kernel,
        out_shape=[jax.ShapeDtypeStruct((count, part, channels), jnp.float32)] * 2,
        in_specs=[SMEM, SMEM, ANY] + [ANY] * directions + [VMEM],
        out_specs=[VMEM, VMEM],
        scratch_shapes=[
            pltpu.VMEM((empty + 1, voxels, channels), jnp.bfloat16),
            pltpu.SemaphoreType.DMA((directions + 1,)),
        ],
        compiler_params=pltpu.CompilerParams(vmem_limit_bytes=32 * MIB),
        cost_estimate=pl.CostEstimate(flops=flops, bytes_accessed=12 * MIB, transcendentals=0),
        name="weight_terms",
    )(table, core, tiles, *halos, turned)


def to_other_core(x):
    size = lax.axis_size("gx")
    return lax.ppermute(x, "gx", [(i, i ^ 1) for i in range(size)])


def swap(x, partner):
    size_x, size_y = lax.axis_size("gx"), lax.axis_size("gy")
    pairs = []
    for i in range(size_x):
        for j in range(size_y):
            to_x, to_y = partner(i, j)
            pairs.append((i * size_y + j, to_x * size_y + to_y))
    return lax.ppermute(x, ("gx", "gy"), pairs)


def gy_levels():
    i, j = lax.axis_index("gx"), lax.axis_index("gy")
    bits = lax.axis_size("gy").bit_length() - 1
    levels = []
    for n in range(bits):
        up, down = 1 << n, 1 << (bits - 1 - n)
        bit = jnp.where(i % 2 == 0, (j // up) % 2, (j // down) % 2)
        levels.append((bit, lambda i, j, up=up, down=down: (i, j ^ (up if i % 2 == 0 else down))))
    return levels


def chip_levels():
    i = lax.axis_index("gx")
    bits = lax.axis_size("gx").bit_length() - 1
    return [((i >> n) % 2, lambda i, j, by=1 << n: (i ^ by, j)) for n in range(1, bits)]


def halved(total, level, kind):
    bit, partner = level
    blocks = total.reshape(2, total.shape[0] // 2, total.shape[1])
    given = lax.dynamic_index_in_dim(blocks, 1 - bit, keepdims=False).astype(kind)
    kept = lax.dynamic_index_in_dim(blocks, bit, keepdims=False)
    return kept + swap(given, partner).astype(jnp.float32)


def doubled(piece, level):
    bit, partner = level
    other = swap(piece, partner)
    return jnp.where(
        bit == 0,
        jnp.concatenate([piece, other], axis=0),
        jnp.concatenate([other, piece], axis=0),
    )


def widen(core, near, far):
    step, channels = near[0].shape

    def kernel(core_ref, far_own, far_other, near_own, near_other, out_ref):
        turn = pl.program_id(0)
        half = jnp.where(turn < 4, turn // 2, turn - 4)
        mine = half == core_ref[0]
        for late, own_ref, other_ref in ((False, far_own, far_other), (True, near_own, near_other)):
            here = (turn >= 4) == late

            @pl.when(here & mine)
            def _():
                out_ref[...] = own_ref[...].astype(jnp.float32)

            @pl.when(here & jnp.logical_not(mine))
            def _():
                out_ref[...] = other_ref[...].astype(jnp.float32)

    far_spec = pl.BlockSpec((step, channels), lambda i: (jnp.where(i < 4, i % 2, 1), 0))
    near_spec = pl.BlockSpec((step, channels), lambda i: (0, 0))
    return pl.pallas_call(
        kernel,
        grid=(6,),
        out_shape=jax.ShapeDtypeStruct((6 * step, channels), jnp.float32),
        in_specs=[SMEM, far_spec, far_spec, near_spec, near_spec],
        out_specs=pl.BlockSpec((step, channels), lambda i: (i, 0)),
        compiler_params=pltpu.CompilerParams(vmem_limit_bytes=24 * MIB),
        name="widen",
    )(core, *far, *near)


def combine(lists, own, cotangent, returned):
    directions, halo = lists.shape
    tile_slots, voxels, channels = own.shape

    def kernel(lists_ref, own_ref, cot_ref, *refs):
        returned_refs = refs[:directions]
        out_ref, acc = refs[directions:]

        def start(t, carry):
            acc[t] = own_ref[t] + cot_ref[t].astype(jnp.float32)
            return carry

        lax.fori_loop(0, tile_slots, start, 0)
        for d in range(directions):
            for h in range(halo):
                acc[lists_ref[d, h]] += returned_refs[d][h].astype(jnp.float32)

        def finish(t, carry):
            out_ref[t] = acc[t].astype(out_ref.dtype)
            return carry

        lax.fori_loop(0, tile_slots, finish, 0)

    return pl.pallas_call(
        kernel,
        out_shape=jax.ShapeDtypeStruct(own.shape, jnp.bfloat16),
        in_specs=[SMEM] + [VMEM] * (directions + 2),
        out_specs=VMEM,
        scratch_shapes=[pltpu.VMEM(own.shape, jnp.float32)],
        compiler_params=pltpu.CompilerParams(vmem_limit_bytes=32 * MIB),
        name="combine",
    )(lists, own, cotangent, *returned)


def shards(
    features, weights, cotangent, send_lists, block_offset, block_input, block_output, block_count
):
    tiles = features[0, 0]
    incoming = cotangent[0, 0]
    lists = send_lists[0, 0]
    tile_slots, voxels, channels = tiles.shape
    directions, halo = lists.shape
    device_total = lax.axis_size("gx") * lax.axis_size("gy")
    scale = 1.0 / math.sqrt(voxels * tile_slots * device_total)

    offset_count = weights.shape[0]
    core = (lax.axis_index("gx") % 2).astype(jnp.int32)[None]

    order = sorted(range(directions), key=lambda d: DIRECTIONS[d][1] == 0)
    early, late = order[: directions // 2], order[directions // 2 :]
    packets = pack(tiles, lists, early)
    table, *rest = pack_and_table(
        tiles,
        lists,
        late,
        block_offset[0, 0],
        block_input[0, 0],
        block_output[0, 0],
        block_count[0],
        offset_count,
        packets[0],
    )
    turned_weights = turn_weights(weights)
    arrived = {d: travel(one, *DIRECTIONS[d]) for d, one in zip(order, [*packets, *rest])}
    halos = [arrived[d] for d in range(directions)]
    out_features, turned, own, *adjoints = forward_and_input_grad(
        table, tiles, halos, weights, turned_weights, incoming
    )
    back = {d: travel(adjoints[d], -DIRECTIONS[d][0], -DIRECTIONS[d][1]) for d in order}
    returned = [back[d] for d in range(directions)]

    near = offset_count // 3
    far = offset_count - near
    near_levels = chip_levels() + gy_levels()
    far_levels = gy_levels() + chip_levels()

    def half_sum(first, count):
        keep, send = weight_terms(table, core, tiles, halos, turned, first, count, scale)
        return (keep + to_other_core(send)).reshape(-1, channels)

    far_sum, near_sum = half_sum(0, far), half_sum(far, near)
    for n in range(len(far_levels)):
        kind = jnp.float32 if n == len(far_levels) - 1 else jnp.bfloat16
        far_sum, near_sum = halved(far_sum, far_levels[n], kind), halved(near_sum, near_levels[n], kind)
        if n == 0:
            feat_grad = combine(lists, own, incoming, returned)
            far_sum, feat_grad = lax.optimization_barrier((far_sum, feat_grad))
    far_sum, near_sum = far_sum.astype(jnp.bfloat16), near_sum.astype(jnp.bfloat16)
    for n in reversed(range(len(far_levels))):
        far_sum, near_sum = doubled(far_sum, far_levels[n]), doubled(near_sum, near_levels[n])
    halves = [(one, to_other_core(one)) for one in (near_sum, far_sum)]
    weight_grad = widen(core, *halves).reshape(weights.shape)
    return (out_features[None, None], feat_grad[None, None], weight_grad)


def solution(mesh):
    in_specs = (
        P("gx", "gy", None, None, None),
        P(),
        P("gx", "gy", None, None, None),
        P("gx", "gy", None, None),
        P("gx", "gy", None),
        P("gx", "gy", None, None),
        P("gx", "gy", None, None),
        P("gx", "gy"),
    )
    out_specs = (P("gx", "gy", None, None, None), P("gx", "gy", None, None, None), P())
    return jax.shard_map(shards, mesh=mesh, in_specs=in_specs, out_specs=out_specs, check_vma=False)
```

```python
import math

import jax
import jax.numpy as jnp
from jax import lax
from jax.experimental import pallas as pl
from jax.experimental.pallas import tpu as pltpu
from jax.sharding import Mesh
from jax.sharding import PartitionSpec as P

DIRECTIONS = ((-1, -1), (-1, 0), (-1, 1), (0, -1), (0, 1), (1, -1), (1, 0), (1, 1))
MIB = 1024 * 1024
ANY = pl.BlockSpec(memory_space=pl.ANY)
HBM = pl.BlockSpec(memory_space=pltpu.HBM)
VMEM = pl.BlockSpec(memory_space=pltpu.VMEM)
SMEM = pl.BlockSpec(memory_space=pltpu.SMEM)


def chunk_of(size, wanted):
    return max(c for c in range(1, wanted + 1) if size % c == 0)


def x_size():
    return lax.axis_size("gz") * lax.axis_size("core")


def travel(packet, step_x, step_y):
    size_x, size_y = x_size(), lax.axis_size("gy")
    pairs = [
        (i * size_y + j, (i + step_x) * size_y + j + step_y)
        for i in range(size_x)
        for j in range(size_y)
        if 0 <= i + step_x < size_x and 0 <= j + step_y < size_y
    ]
    return lax.ppermute(packet, ("gz", "core", "gy"), pairs)


def pack(tiles, lists, chosen):
    halo = lists.shape[1]
    _, voxels, channels = tiles.shape

    def kernel(lists_ref, tiles_ref, *packets):
        for n, d in enumerate(chosen):
            for h in range(halo):
                packets[n][h] = tiles_ref[lists_ref[d, h]]

    return pl.pallas_call(
        kernel,
        out_shape=[jax.ShapeDtypeStruct((halo, voxels, channels), tiles.dtype)] * len(chosen),
        in_specs=[SMEM, VMEM],
        out_specs=[VMEM] * len(chosen),
        compiler_params=pltpu.CompilerParams(vmem_limit_bytes=16 * MIB),
        name="pack",
    )(lists, tiles)


def pack_and_table(tiles, lists, chosen, offsets, inputs, outputs, count, offset_count, after):
    directions, halo = lists.shape
    tile_slots, voxels, channels = tiles.shape
    blocks, rows = inputs.shape
    empty = tile_slots + directions * halo

    def kernel(
        lists_ref, offsets_ref, inputs_ref, outputs_ref, count_ref, tiles_ref, _, table_ref, *packets
    ):
        for n, d in enumerate(chosen):
            for h in range(halo):
                packets[n][h] = tiles_ref[lists_ref[d, h]]

        def clear(k, carry):
            for t in range(tile_slots):
                table_ref[k, t] = empty
            return carry

        lax.fori_loop(0, offset_count, clear, 0)

        def block(n, carry):
            k = offsets_ref[n]
            for q in range(rows):
                target = outputs_ref[n, q]

                @pl.when(target < tile_slots)
                def _():
                    table_ref[k, target] = inputs_ref[n, q]

            return carry

        lax.fori_loop(0, jnp.minimum(count_ref[0], blocks), block, 0)

    return pl.pallas_call(
        kernel,
        out_shape=[jax.ShapeDtypeStruct((offset_count, tile_slots), jnp.int32)]
        + [jax.ShapeDtypeStruct((halo, voxels, channels), tiles.dtype)] * len(chosen),
        in_specs=[SMEM] * 5 + [VMEM, ANY],
        out_specs=[SMEM] + [VMEM] * len(chosen),
        compiler_params=pltpu.CompilerParams(vmem_limit_bytes=16 * MIB),
        name="pack_and_table",
    )(lists, offsets, inputs, outputs, count, tiles, after)


def turn_weights(weights):
    def kernel(w_ref, out_ref):
        for k in range(w_ref.shape[0]):
            out_ref[k] = w_ref[k].astype(jnp.float32).T.astype(out_ref.dtype)

    offset_count, channels, _ = weights.shape
    step = chunk_of(offset_count, 3)
    spec = pl.BlockSpec((step, channels, channels), lambda k: (k, 0, 0))
    return pl.pallas_call(
        kernel,
        grid=(offset_count // step,),
        out_shape=jax.ShapeDtypeStruct(weights.shape, weights.dtype),
        in_specs=[spec],
        out_specs=spec,
        compiler_params=pltpu.CompilerParams(vmem_limit_bytes=16 * MIB),
        cost_estimate=pl.CostEstimate(flops=8 * 10**9, bytes_accessed=7 * MIB, transcendentals=0),
        name="turn_weights",
    )(weights)


def gathered(table_ref, ext, k, first, count):
    return jnp.concatenate([ext[table_ref[k, first + t]] for t in range(count)], axis=0)


def add_weight_terms(table_ref, core_ref, ext, turned_ref, keep_ref, send_ref, first, count, scale):
    _, part, channels = keep_ref.shape
    tile_slots = table_ref.shape[1]

    def turn(k, carry):
        terms = jnp.dot(
            turned_ref[...],
            gathered(table_ref, ext, first + k, 0, tile_slots),
            preferred_element_type=jnp.float32,
        )
        terms = terms.T * scale
        for h in range(channels // part):
            place = 2 * k + h
            half = (place >= count).astype(jnp.int32)
            rest = place - half * count
            values = terms[h * part : (h + 1) * part]

            @pl.when(half == core_ref[0])
            def _():
                keep_ref[rest] = values

            @pl.when(half != core_ref[0])
            def _():
                send_ref[rest] = values

        return carry

    lax.fori_loop(0, count, turn, 0)


def forward_and_terms(table, core, tiles, halos, weights, cotangent, count, scale, after):
    tile_slots, voxels, channels = tiles.shape
    offset_count = weights.shape[0]
    directions, halo = len(halos), halos[0].shape[0]
    empty = tile_slots + directions * halo
    group = chunk_of(tile_slots, 8)
    groups = tile_slots // group
    rows = group * voxels
    deep = chunk_of(offset_count, 9)

    def kernel(table_ref, core_ref, tiles_ref, *refs):
        halo_refs, refs = refs[:directions], refs[directions:]
        w_hbm, cot_hbm, _, out_ref, grad, turned_ref, ext, keep_ref, send_ref = refs[:9]
        w_ref, cot_ref, acc, sems = refs[9:]
        copies = [
            pltpu.make_async_copy(tiles_ref, ext.at[pl.ds(0, tile_slots)], sems.at[0]),
            pltpu.make_async_copy(w_hbm, w_ref, sems.at[1]),
            pltpu.make_async_copy(cot_hbm, cot_ref, sems.at[2]),
        ]
        for d, halo_ref in enumerate(halo_refs):
            place = ext.at[pl.ds(tile_slots + d * halo, halo)]
            copies.append(pltpu.make_async_copy(halo_ref, place, sems.at[d + 3]))
        for copy in copies:
            copy.start()
        ext[empty] = jnp.zeros((voxels, channels), ext.dtype)
        acc[...] = jnp.zeros_like(acc)
        for copy in copies:
            copy.wait()

        def turn(step, carry):
            mats = w_ref[pl.ds(step * deep, deep)].reshape(deep * channels, channels)
            for g in range(groups):
                lhs = jnp.concatenate(
                    [
                        gathered(table_ref, ext, step * deep + j, g * group, group)
                        for j in range(deep)
                    ],
                    axis=1,
                )
                acc[g] += jnp.dot(lhs, mats, preferred_element_type=jnp.float32)
            return carry

        lax.fori_loop(0, offset_count // deep, turn, 0)

        def finish(t, carry):
            pre = acc[t // group, pl.ds(pl.multiple_of((t % group) * voxels, voxels), voxels), :]
            sigma = jax.nn.sigmoid(pre)
            out_ref[t] = (ext[t].astype(jnp.float32) + pre * sigma).astype(out_ref.dtype)
            incoming = cot_ref[t].astype(jnp.float32)
            grad[t] = (incoming * sigma * (1.0 + pre * (1.0 - sigma))).astype(grad.dtype)
            return carry

        lax.fori_loop(0, tile_slots, finish, 0)
        for g in range(groups):
            part = grad[pl.ds(g * group, group)].reshape(rows, channels)
            turned_ref[:, pl.ds(g * rows, rows)] = part.astype(jnp.float32).T.astype(jnp.bfloat16)
        add_weight_terms(table_ref, core_ref, ext, turned_ref, keep_ref, send_ref, 0, count, scale)

    flops = 2 * (offset_count + count) * tile_slots * voxels * channels * channels
    half = jax.ShapeDtypeStruct((count, channels // 2, channels), jnp.float32)
    return pl.pallas_call(
        kernel,
        out_shape=[
            jax.ShapeDtypeStruct(tiles.shape, jnp.bfloat16),
            jax.ShapeDtypeStruct(tiles.shape, jnp.bfloat16),
            jax.ShapeDtypeStruct((channels, tile_slots * voxels), jnp.bfloat16),
            jax.ShapeDtypeStruct((empty + 1, voxels, channels), jnp.bfloat16),
            half,
            half,
        ],
        in_specs=[SMEM, SMEM, HBM] + [ANY] * directions + [HBM, HBM, ANY],
        out_specs=[VMEM] * 6,
        scratch_shapes=[
            pltpu.VMEM(weights.shape, jnp.bfloat16),
            pltpu.VMEM(tiles.shape, jnp.bfloat16),
            pltpu.VMEM((groups, rows, channels), jnp.float32),
            pltpu.SemaphoreType.DMA((directions + 3,)),
        ],
        compiler_params=pltpu.CompilerParams(vmem_limit_bytes=28 * MIB),
        cost_estimate=pl.CostEstimate(flops=flops, bytes_accessed=20 * MIB, transcendentals=0),
        name="forward_and_terms",
    )(table, core, tiles, *halos, weights, cotangent, after)


def weight_terms(table, core, ext, turned, first, count, scale):
    channels = ext.shape[2]

    def kernel(table_ref, core_ref, ext_ref, turned_ref, keep_ref, send_ref):
        add_weight_terms(
            table_ref, core_ref, ext_ref, turned_ref, keep_ref, send_ref, first, count, scale
        )

    flops = 2 * count * turned.shape[1] * channels * channels
    return pl.pallas_call(
        kernel,
        out_shape=[jax.ShapeDtypeStruct((count, channels // 2, channels), jnp.float32)] * 2,
        in_specs=[SMEM, SMEM, VMEM, VMEM],
        out_specs=[VMEM, VMEM],
        compiler_params=pltpu.CompilerParams(vmem_limit_bytes=16 * MIB),
        cost_estimate=pl.CostEstimate(flops=flops, bytes_accessed=6 * MIB, transcendentals=0),
        name="weight_terms",
    )(table, core, ext, turned)


def input_grad(table, pre_grad, turned_weights, directions, halo):
    tile_slots, voxels, channels = pre_grad.shape
    offset_count = turned_weights.shape[0]
    empty = tile_slots + directions * halo
    group = chunk_of(tile_slots, 8)
    groups = tile_slots // group
    rows = group * voxels
    unroll = chunk_of(offset_count, 3)

    def kernel(table_ref, grad, wt_ref, own_ref, *refs):
        adjoints = refs[:directions]
        even, odd = refs[directions:]
        for one in (even, odd):
            one[...] = jnp.zeros_like(one)

        def turn(step, carry):
            for j in range(unroll):
                k = step * unroll + j
                for g in range(groups):
                    back = jnp.dot(
                        grad[pl.ds(g * group, group)].reshape(rows, channels),
                        wt_ref[k],
                        preferred_element_type=jnp.float32,
                    )
                    for t in range(group):
                        slot = table_ref[k, g * group + t]
                        sums = (even, odd)[t % 2]
                        sums[slot] += back[t * voxels : (t + 1) * voxels]
            return carry

        lax.fori_loop(0, offset_count // unroll, turn, 0)

        def own(t, carry):
            own_ref[t] = even[t] + odd[t]
            return carry

        lax.fori_loop(0, tile_slots, own, 0)
        for d in range(directions):
            for h in range(halo):
                slot = tile_slots + d * halo + h
                adjoints[d][h] = (even[slot] + odd[slot]).astype(jnp.bfloat16)

    flops = 2 * offset_count * tile_slots * voxels * channels * channels
    return pl.pallas_call(
        kernel,
        out_shape=[jax.ShapeDtypeStruct(pre_grad.shape, jnp.float32)]
        + [jax.ShapeDtypeStruct((halo, voxels, channels), jnp.bfloat16)] * directions,
        in_specs=[SMEM, VMEM, VMEM],
        out_specs=[VMEM] * (directions + 1),
        scratch_shapes=[pltpu.VMEM((empty + 1, voxels, channels), jnp.float32)] * 2,
        compiler_params=pltpu.CompilerParams(vmem_limit_bytes=32 * MIB),
        cost_estimate=pl.CostEstimate(flops=flops, bytes_accessed=12 * MIB, transcendentals=0),
        name="input_grad",
    )(table, pre_grad, turned_weights)


def to_other_core(x):
    return lax.ppermute(x, "core", [(0, 1), (1, 0)])


def scattered_sum(keep, send):
    mine = (keep + to_other_core(send)).reshape(-1, keep.shape[2])
    return lax.psum_scatter(mine, ("gz", "gy"), scatter_dimension=0, tiled=True)


def gathered_halves(piece):
    whole = lax.all_gather(piece.astype(jnp.bfloat16), ("gz", "gy"), axis=0, tiled=True)
    return whole, to_other_core(whole)


def widen(core, near, far):
    step, channels = near[0].shape

    def kernel(core_ref, far_own, far_other, near_own, near_other, out_ref):
        turn = pl.program_id(0)
        half = jnp.where(turn < 4, turn // 2, turn - 4)
        mine = half == core_ref[0]
        for late, own_ref, other_ref in ((False, far_own, far_other), (True, near_own, near_other)):
            here = (turn >= 4) == late

            @pl.when(here & mine)
            def _():
                out_ref[...] = own_ref[...].astype(jnp.float32)

            @pl.when(here & jnp.logical_not(mine))
            def _():
                out_ref[...] = other_ref[...].astype(jnp.float32)

    far_spec = pl.BlockSpec((step, channels), lambda i: (jnp.where(i < 4, i % 2, 1), 0))
    near_spec = pl.BlockSpec((step, channels), lambda i: (0, 0))
    return pl.pallas_call(
        kernel,
        grid=(6,),
        out_shape=jax.ShapeDtypeStruct((6 * step, channels), jnp.float32),
        in_specs=[SMEM, far_spec, far_spec, near_spec, near_spec],
        out_specs=pl.BlockSpec((step, channels), lambda i: (i, 0)),
        compiler_params=pltpu.CompilerParams(vmem_limit_bytes=24 * MIB),
        name="widen",
    )(core, *far, *near)


def combine(lists, own, cotangent, returned):
    directions, halo = lists.shape
    tile_slots, voxels, channels = own.shape

    def kernel(lists_ref, own_ref, cot_ref, *refs):
        returned_refs = refs[:directions]
        out_ref, acc = refs[directions:]

        def start(t, carry):
            acc[t] = own_ref[t] + cot_ref[t].astype(jnp.float32)
            return carry

        lax.fori_loop(0, tile_slots, start, 0)
        for d in range(directions):
            for h in range(halo):
                acc[lists_ref[d, h]] += returned_refs[d][h].astype(jnp.float32)

        def finish(t, carry):
            out_ref[t] = acc[t].astype(out_ref.dtype)
            return carry

        lax.fori_loop(0, tile_slots, finish, 0)

    return pl.pallas_call(
        kernel,
        out_shape=jax.ShapeDtypeStruct(own.shape, jnp.bfloat16),
        in_specs=[SMEM] + [VMEM] * (directions + 2),
        out_specs=VMEM,
        scratch_shapes=[pltpu.VMEM(own.shape, jnp.float32)],
        compiler_params=pltpu.CompilerParams(vmem_limit_bytes=32 * MIB),
        name="combine",
    )(lists, own, cotangent, *returned)


def shards(
    features, weights, cotangent, send_lists, block_offset, block_input, block_output, block_count
):
    tiles = features[0, 0]
    incoming = cotangent[0, 0]
    lists = send_lists[0, 0]
    tile_slots, voxels, channels = tiles.shape
    directions, halo = lists.shape
    device_total = x_size() * lax.axis_size("gy")
    scale = 1.0 / math.sqrt(voxels * tile_slots * device_total)
    offset_count = weights.shape[0]
    core = lax.axis_index("core").astype(jnp.int32)[None]

    order = sorted(range(directions), key=lambda d: DIRECTIONS[d][1] == 0)
    early, late = order[: directions // 2], order[directions // 2 :]
    packets = pack(tiles, lists, early)
    table, *rest = pack_and_table(
        tiles,
        lists,
        late,
        block_offset[0, 0],
        block_input[0, 0],
        block_output[0, 0],
        block_count[0],
        offset_count,
        packets[0],
    )
    turned_weights = turn_weights(weights)
    arrived = {d: travel(one, *DIRECTIONS[d]) for d, one in zip(order, [*packets, *rest])}
    halos = [arrived[d] for d in range(directions)]
    near = offset_count // 3
    far = offset_count - near
    out_features, pre_grad, turned, ext, *far_terms = forward_and_terms(
        table, core, tiles, halos, weights, incoming, far, scale, turned_weights
    )
    near_terms = weight_terms(table, core, ext, turned, far, near, scale)
    far_piece, near_piece = scattered_sum(*far_terms), scattered_sum(*near_terms)
    own, *adjoints = input_grad(table, pre_grad, turned_weights, directions, halo)
    back = {d: travel(adjoints[d], -DIRECTIONS[d][0], -DIRECTIONS[d][1]) for d in order}
    feat_grad = combine(lists, own, incoming, [back[d] for d in range(directions)])
    far_piece, near_piece, feat_grad = lax.optimization_barrier((far_piece, near_piece, feat_grad))
    far_halves, near_halves = gathered_halves(far_piece), gathered_halves(near_piece)
    weight_grad = widen(core, near_halves, far_halves).reshape(weights.shape)
    return (out_features[None, None], feat_grad[None, None], weight_grad)


def solution(mesh):
    size_x, size_y = mesh.devices.shape
    split = Mesh(mesh.devices.reshape(size_x // 2, 2, size_y), ("gz", "core", "gy"))
    place = P(("gz", "core"), "gy")
    return jax.shard_map(
        shards,
        mesh=split,
        in_specs=(place, P(), place, place, place, place, place, place),
        out_specs=(place, place, P()),
        check_vma=False,
    )
```

```python
import math

import jax
import jax.numpy as jnp
from jax import lax
from jax.experimental import pallas as pl
from jax.experimental.pallas import tpu as pltpu
from jax.sharding import Mesh
from jax.sharding import PartitionSpec as P

DIRECTIONS = ((-1, -1), (-1, 0), (-1, 1), (0, -1), (0, 1), (1, -1), (1, 0), (1, 1))
MIB = 1024 * 1024
ANY = pl.BlockSpec(memory_space=pl.ANY)
HBM = pl.BlockSpec(memory_space=pltpu.HBM)
VMEM = pl.BlockSpec(memory_space=pltpu.VMEM)
SMEM = pl.BlockSpec(memory_space=pltpu.SMEM)


def chunk_of(size, wanted):
    return max(c for c in range(1, wanted + 1) if size % c == 0)


def x_size():
    return lax.axis_size("gz") * lax.axis_size("core")


def travel(packet, step_x, step_y):
    size_x, size_y = x_size(), lax.axis_size("gy")
    pairs = [
        (i * size_y + j, (i + step_x) * size_y + j + step_y)
        for i in range(size_x)
        for j in range(size_y)
        if 0 <= i + step_x < size_x and 0 <= j + step_y < size_y
    ]
    return lax.ppermute(packet, ("gz", "core", "gy"), pairs)


def pack(tiles, lists):
    directions, halo = lists.shape
    _, voxels, channels = tiles.shape

    def kernel(lists_ref, tiles_ref, *packets):
        for d in range(directions):
            for h in range(halo):
                packets[d][h] = tiles_ref[lists_ref[d, h]]

    return pl.pallas_call(
        kernel,
        out_shape=[jax.ShapeDtypeStruct((halo, voxels, channels), tiles.dtype)] * directions,
        in_specs=[SMEM, VMEM],
        out_specs=[VMEM] * directions,
        compiler_params=pltpu.CompilerParams(vmem_limit_bytes=16 * MIB),
        name="pack",
    )(lists, tiles)


def source_table(offsets, inputs, outputs, count, offset_count, tile_slots, empty, after):
    rows, blocks = inputs.shape

    def kernel(offsets_ref, inputs_ref, outputs_ref, count_ref, _, table_ref):
        def clear(k, carry):
            for t in range(tile_slots):
                table_ref[k, t] = empty
            return carry

        lax.fori_loop(0, offset_count, clear, 0)

        def block(n, carry):
            k = offsets_ref[n]
            for q in range(rows):
                table_ref[k, outputs_ref[q, n]] = inputs_ref[q, n]
            return carry

        lax.fori_loop(0, jnp.minimum(count_ref[0], blocks), block, 0)

    return pl.pallas_call(
        kernel,
        out_shape=jax.ShapeDtypeStruct((offset_count, tile_slots + 1), jnp.int32),
        in_specs=[SMEM] * 4 + [ANY],
        out_specs=SMEM,
        cost_estimate=pl.CostEstimate(flops=4 * 10**9, bytes_accessed=MIB, transcendentals=0),
        name="source_table",
    )(offsets, inputs, outputs, count, after)


def turn_weights(weights):
    def kernel(w_ref, out_ref):
        for k in range(w_ref.shape[0]):
            out_ref[k] = w_ref[k].astype(jnp.float32).T.astype(out_ref.dtype)

    offset_count, channels, _ = weights.shape
    step = chunk_of(offset_count, 3)
    spec = pl.BlockSpec((step, channels, channels), lambda k: (k, 0, 0))
    return pl.pallas_call(
        kernel,
        grid=(offset_count // step,),
        out_shape=jax.ShapeDtypeStruct(weights.shape, weights.dtype),
        in_specs=[spec],
        out_specs=spec,
        compiler_params=pltpu.CompilerParams(vmem_limit_bytes=16 * MIB),
        cost_estimate=pl.CostEstimate(flops=8 * 10**9, bytes_accessed=7 * MIB, transcendentals=0),
        name="turn_weights",
    )(weights)


def gathered(table_ref, ext, k, first, count):
    return jnp.concatenate([ext[table_ref[k, first + t]] for t in range(count)], axis=0)


def add_weight_terms(table_ref, core_ref, ext, turned_ref, keep_ref, send_ref, first, count, scale):
    _, part, channels = keep_ref.shape
    tile_slots = table_ref.shape[1] - 1

    def turn(k, carry):
        terms = jnp.dot(
            turned_ref[...],
            gathered(table_ref, ext, first + k, 0, tile_slots),
            preferred_element_type=jnp.float32,
        )
        terms = terms.T * scale
        for h in range(channels // part):
            place = 2 * k + h
            half = (place >= count).astype(jnp.int32)
            rest = place - half * count
            values = terms[h * part : (h + 1) * part]

            @pl.when(half == core_ref[0])
            def _():
                keep_ref[rest] = values

            @pl.when(half != core_ref[0])
            def _():
                send_ref[rest] = values

        return carry

    lax.fori_loop(0, count, turn, 0)


def forward_and_terms(table, core, tiles, halos, weights, cotangent, count, scale, after):
    tile_slots, voxels, channels = tiles.shape
    offset_count = weights.shape[0]
    directions, halo = len(halos), halos[0].shape[0]
    empty = tile_slots + directions * halo
    group = chunk_of(tile_slots, 8)
    groups = tile_slots // group
    rows = group * voxels
    deep = chunk_of(offset_count, 9)

    def kernel(table_ref, core_ref, tiles_ref, *refs):
        halo_refs, refs = refs[:directions], refs[directions:]
        w_hbm, cot_hbm, _, out_ref, grad, turned_ref, ext, keep_ref, send_ref = refs[:9]
        w_ref, cot_ref, acc, sems = refs[9:]
        copies = [
            pltpu.make_async_copy(tiles_ref, ext.at[pl.ds(0, tile_slots)], sems.at[0]),
            pltpu.make_async_copy(w_hbm, w_ref, sems.at[1]),
            pltpu.make_async_copy(cot_hbm, cot_ref, sems.at[2]),
        ]
        for d, halo_ref in enumerate(halo_refs):
            place = ext.at[pl.ds(tile_slots + d * halo, halo)]
            copies.append(pltpu.make_async_copy(halo_ref, place, sems.at[d + 3]))
        for copy in copies:
            copy.start()
        ext[empty] = jnp.zeros((voxels, channels), ext.dtype)
        acc[...] = jnp.zeros_like(acc)
        for copy in copies:
            copy.wait()

        def turn(step, carry):
            mats = w_ref[pl.ds(step * deep, deep)].reshape(deep * channels, channels)
            for g in range(groups):
                lhs = jnp.concatenate(
                    [
                        gathered(table_ref, ext, step * deep + j, g * group, group)
                        for j in range(deep)
                    ],
                    axis=1,
                )
                acc[g] += jnp.dot(lhs, mats, preferred_element_type=jnp.float32)
            return carry

        lax.fori_loop(0, offset_count // deep, turn, 0)

        def finish(t, carry):
            pre = acc[t // group, pl.ds(pl.multiple_of((t % group) * voxels, voxels), voxels), :]
            sigma = jax.nn.sigmoid(pre)
            out_ref[t] = (ext[t].astype(jnp.float32) + pre * sigma).astype(out_ref.dtype)
            incoming = cot_ref[t].astype(jnp.float32)
            grad[t] = (incoming * sigma * (1.0 + pre * (1.0 - sigma))).astype(grad.dtype)
            return carry

        lax.fori_loop(0, tile_slots, finish, 0)
        for g in range(groups):
            part = grad[pl.ds(g * group, group)].reshape(rows, channels)
            turned_ref[:, pl.ds(g * rows, rows)] = part.astype(jnp.float32).T.astype(jnp.bfloat16)
        add_weight_terms(table_ref, core_ref, ext, turned_ref, keep_ref, send_ref, 0, count, scale)

    flops = 2 * (offset_count + count) * tile_slots * voxels * channels * channels
    half = jax.ShapeDtypeStruct((count, channels // 2, channels), jnp.float32)
    return pl.pallas_call(
        kernel,
        out_shape=[
            jax.ShapeDtypeStruct(tiles.shape, jnp.bfloat16),
            jax.ShapeDtypeStruct(tiles.shape, jnp.bfloat16),
            jax.ShapeDtypeStruct((channels, tile_slots * voxels), jnp.bfloat16),
            jax.ShapeDtypeStruct((empty + 1, voxels, channels), jnp.bfloat16),
            half,
            half,
        ],
        in_specs=[SMEM, SMEM] + [HBM] * (directions + 4),
        out_specs=[VMEM] * 6,
        scratch_shapes=[
            pltpu.VMEM(weights.shape, jnp.bfloat16),
            pltpu.VMEM(tiles.shape, jnp.bfloat16),
            pltpu.VMEM((groups, rows, channels), jnp.float32),
            pltpu.SemaphoreType.DMA((directions + 3,)),
        ],
        compiler_params=pltpu.CompilerParams(vmem_limit_bytes=28 * MIB),
        cost_estimate=pl.CostEstimate(flops=flops, bytes_accessed=20 * MIB, transcendentals=0),
        name="forward_and_terms",
    )(table, core, tiles, *halos, weights, cotangent, after)


def weight_terms(table, core, ext, turned, first, count, scale):
    channels = ext.shape[2]

    def kernel(table_ref, core_ref, ext_ref, turned_ref, keep_ref, send_ref):
        add_weight_terms(
            table_ref, core_ref, ext_ref, turned_ref, keep_ref, send_ref, first, count, scale
        )

    flops = 2 * count * turned.shape[1] * channels * channels
    return pl.pallas_call(
        kernel,
        out_shape=[jax.ShapeDtypeStruct((count, channels // 2, channels), jnp.float32)] * 2,
        in_specs=[SMEM, SMEM, VMEM, VMEM],
        out_specs=[VMEM, VMEM],
        compiler_params=pltpu.CompilerParams(vmem_limit_bytes=16 * MIB),
        cost_estimate=pl.CostEstimate(flops=flops, bytes_accessed=6 * MIB, transcendentals=0),
        name="weight_terms",
    )(table, core, ext, turned)


def input_grad(table, pre_grad, turned_weights, directions, halo):
    tile_slots, voxels, channels = pre_grad.shape
    offset_count = turned_weights.shape[0]
    empty = tile_slots + directions * halo
    group = chunk_of(tile_slots, 8)
    groups = tile_slots // group
    rows = group * voxels
    unroll = chunk_of(offset_count, 3)

    def kernel(table_ref, grad_hbm, wt_hbm, own_ref, *refs):
        adjoints = refs[:directions]
        even, odd, grad, wt_ref, sems = refs[directions:]
        copies = [
            pltpu.make_async_copy(grad_hbm, grad, sems.at[0]),
            pltpu.make_async_copy(wt_hbm, wt_ref, sems.at[1]),
        ]
        for copy in copies:
            copy.start()
        for one in (even, odd):
            one[...] = jnp.zeros_like(one)
        for copy in copies:
            copy.wait()

        def turn(step, carry):
            for j in range(unroll):
                k = step * unroll + j
                for g in range(groups):
                    back = jnp.dot(
                        grad[pl.ds(g * group, group)].reshape(rows, channels),
                        wt_ref[k],
                        preferred_element_type=jnp.float32,
                    )
                    for t in range(group):
                        slot = table_ref[k, g * group + t]
                        sums = (even, odd)[t % 2]
                        sums[slot] += back[t * voxels : (t + 1) * voxels]
            return carry

        lax.fori_loop(0, offset_count // unroll, turn, 0)

        def own(t, carry):
            own_ref[t] = even[t] + odd[t]
            return carry

        lax.fori_loop(0, tile_slots, own, 0)
        for d in range(directions):
            for h in range(halo):
                slot = tile_slots + d * halo + h
                adjoints[d][h] = (even[slot] + odd[slot]).astype(jnp.bfloat16)

    flops = 2 * offset_count * tile_slots * voxels * channels * channels
    return pl.pallas_call(
        kernel,
        out_shape=[jax.ShapeDtypeStruct(pre_grad.shape, jnp.float32)]
        + [jax.ShapeDtypeStruct((halo, voxels, channels), jnp.bfloat16)] * directions,
        in_specs=[SMEM, HBM, HBM],
        out_specs=[VMEM] * (directions + 1),
        scratch_shapes=[pltpu.VMEM((empty + 1, voxels, channels), jnp.float32)] * 2
        + [
            pltpu.VMEM(pre_grad.shape, jnp.bfloat16),
            pltpu.VMEM(turned_weights.shape, jnp.bfloat16),
            pltpu.SemaphoreType.DMA((2,)),
        ],
        compiler_params=pltpu.CompilerParams(vmem_limit_bytes=32 * MIB),
        cost_estimate=pl.CostEstimate(flops=flops, bytes_accessed=12 * MIB, transcendentals=0),
        name="input_grad",
    )(table, pre_grad, turned_weights)


def to_other_core(x):
    return lax.ppermute(x, "core", [(0, 1), (1, 0)])


def along(axis):
    size = lax.axis_size(axis)

    def move(x, by):
        return lax.ppermute(x, axis, [(i, (i + by) % size) for i in range(size)])

    return size, lax.axis_index(axis), move


def given_out(total, ring, kind):
    size, place, _ = ring
    blocks = total.reshape(size, total.shape[0] // size, total.shape[1])
    parts = [
        lax.dynamic_index_in_dim(blocks, (place + s) % size, keepdims=False) for s in range(size)
    ]
    return parts[0], [one.astype(kind) for one in parts[1:]]


def handed(parts, ring):
    return [ring[2](one, s + 1) for s, one in enumerate(parts)]


def added(mine, arrived):
    for one in arrived:
        mine = mine + one.astype(jnp.float32)
    return mine


def fetched(piece, ring):
    return [ring[2](piece, -s) for s in range(1, ring[0])]


def in_order(piece, others, ring):
    size, place, _ = ring
    whole = jnp.zeros((size,) + piece.shape, piece.dtype)
    for s, one in enumerate([piece, *others]):
        whole = lax.dynamic_update_index_in_dim(whole, one, (place + s) % size, 0)
    return whole.reshape(size * piece.shape[0], piece.shape[1])


def together(*values):
    return lax.optimization_barrier(values)


def widen(core, far, near):
    step, channels = near[0].shape

    def kernel(core_ref, far_own, far_other, near_own, near_other, out_ref):
        turn = pl.program_id(0)
        half = jnp.where(turn < 2, turn, (turn - 2) // 2)
        mine = half == core_ref[0]
        for late, own_ref, other_ref in ((True, far_own, far_other), (False, near_own, near_other)):
            here = (turn >= 2) == late

            @pl.when(here & mine)
            def _():
                out_ref[...] = own_ref[...].astype(jnp.float32)

            @pl.when(here & jnp.logical_not(mine))
            def _():
                out_ref[...] = other_ref[...].astype(jnp.float32)

    far_spec = pl.BlockSpec((step, channels), lambda i: (jnp.where(i < 2, 0, i % 2), 0))
    near_spec = pl.BlockSpec((step, channels), lambda i: (0, 0))
    return pl.pallas_call(
        kernel,
        grid=(6,),
        out_shape=jax.ShapeDtypeStruct((6 * step, channels), jnp.float32),
        in_specs=[SMEM, far_spec, far_spec, near_spec, near_spec],
        out_specs=pl.BlockSpec((step, channels), lambda i: (i, 0)),
        compiler_params=pltpu.CompilerParams(vmem_limit_bytes=24 * MIB),
        name="widen",
    )(core, *far, *near)


def combine(lists, own, cotangent, returned):
    directions, halo = lists.shape
    tile_slots, voxels, channels = own.shape

    def kernel(lists_ref, own_ref, cot_ref, *refs):
        returned_refs = refs[:directions]
        out_ref, acc = refs[directions:]

        def start(t, carry):
            acc[t] = own_ref[t] + cot_ref[t].astype(jnp.float32)
            return carry

        lax.fori_loop(0, tile_slots, start, 0)
        for d in range(directions):
            for h in range(halo):
                acc[lists_ref[d, h]] += returned_refs[d][h].astype(jnp.float32)

        def finish(t, carry):
            out_ref[t] = acc[t].astype(out_ref.dtype)
            return carry

        lax.fori_loop(0, tile_slots, finish, 0)

    return pl.pallas_call(
        kernel,
        out_shape=jax.ShapeDtypeStruct(own.shape, jnp.bfloat16),
        in_specs=[SMEM] + [VMEM] * (directions + 2),
        out_specs=VMEM,
        scratch_shapes=[pltpu.VMEM(own.shape, jnp.float32)],
        compiler_params=pltpu.CompilerParams(vmem_limit_bytes=32 * MIB),
        name="combine",
    )(lists, own, cotangent, *returned)


def shards(
    features, weights, cotangent, send_lists, block_offset, block_input, block_output, block_count
):
    tiles = features[0, 0]
    incoming = cotangent[0, 0]
    lists = send_lists[0, 0]
    tile_slots, voxels, channels = tiles.shape
    directions, halo = lists.shape
    device_total = x_size() * lax.axis_size("gy")
    scale = 1.0 / math.sqrt(voxels * tile_slots * device_total)
    offset_count = weights.shape[0]
    core = lax.axis_index("core").astype(jnp.int32)[None]

    order = sorted(range(directions), key=lambda d: DIRECTIONS[d][1] == 0)
    early = order[: directions // 2]
    packets = pack(tiles, lists)
    table = source_table(
        block_offset[0, 0],
        block_input[0, 0].T,
        block_output[0, 0].T,
        block_count[0],
        offset_count,
        tile_slots,
        tile_slots + directions * halo,
        packets[0],
    )
    turned_weights = turn_weights(weights)
    arrived = {d: travel(packets[d], *DIRECTIONS[d]) for d in order}
    halos = [arrived[d] for d in range(directions)]

    near = offset_count // 3
    far = offset_count - near
    chips, columns = along("gz"), along("gy")
    out_features, pre_grad, turned, ext, near_keep, near_send = forward_and_terms(
        table, core, tiles, halos, weights, incoming, near, scale, turned_weights
    )
    near_half = near_keep + to_other_core(near_send)
    far_keep, far_send = weight_terms(table, core, ext, turned, near, far, scale)
    far_half = far_keep + to_other_core(far_send)
    near_own, near_out = given_out(near_half.reshape(-1, channels), chips, jnp.bfloat16)
    far_own, far_out = given_out(far_half.reshape(-1, channels), columns, jnp.bfloat16)

    pre_grad, *out = together(pre_grad, *near_out, *far_out)
    near_in, far_in = handed(out[: len(near_out)], chips), handed(out[len(near_out) :], columns)
    own, *adjoints = input_grad(table, pre_grad, turned_weights, directions, halo)
    adjoints[0], *moved = together(adjoints[0], *near_in, *far_in)
    back = {d: travel(adjoints[d], -DIRECTIONS[d][0], -DIRECTIONS[d][1]) for d in order}
    near_sum = added(near_own, moved[: len(near_in)])
    far_sum = added(far_own, moved[len(near_in) :])

    near_own, near_out = given_out(near_sum, columns, jnp.float32)
    far_own, far_out = given_out(far_sum, chips, jnp.float32)
    near_piece = added(near_own, handed(near_out, columns)).astype(jnp.bfloat16)
    far_piece = added(far_own, handed(far_out, chips)).astype(jnp.bfloat16)

    near_piece = in_order(near_piece, fetched(near_piece, columns), columns)
    far_piece = in_order(far_piece, fetched(far_piece, chips), chips)
    near_piece, far_piece, *halfway = together(near_piece, far_piece, *[back[d] for d in early])
    back.update(zip(early, halfway))
    near_piece = in_order(near_piece, fetched(near_piece, chips), chips)
    far_piece = in_order(far_piece, fetched(far_piece, columns), columns)
    late = order[len(early) :]
    near_piece, far_piece, *rest = together(near_piece, far_piece, *[back[d] for d in late])
    back.update(zip(late, rest))
    halves = [(one, to_other_core(one)) for one in (far_piece, near_piece)]
    weight_grad = widen(core, *halves).reshape(weights.shape)
    feat_grad = combine(lists, own, incoming, [back[d] for d in range(directions)])
    return (out_features[None, None], feat_grad[None, None], weight_grad)


def solution(mesh):
    size_x, size_y = mesh.devices.shape
    split = Mesh(mesh.devices.reshape(size_x // 2, 2, size_y), ("gz", "core", "gy"))
    place = P(("gz", "core"), "gy")
    return jax.shard_map(
        shards,
        mesh=split,
        in_specs=(place, P(), place, place, place, place, place, place),
        out_specs=(place, place, P()),
        check_vma=False,
    )
```

```python
import math

import jax
import jax.numpy as jnp
from jax import lax
from jax.experimental import pallas as pl
from jax.experimental.pallas import tpu as pltpu
from jax.sharding import Mesh
from jax.sharding import PartitionSpec as P

DIRECTIONS = ((-1, -1), (-1, 0), (-1, 1), (0, -1), (0, 1), (1, -1), (1, 0), (1, 1))
BUNDLES = (
    ((-1, -1), (0, -1), (1, -1)),
    ((-1, 1), (0, 1), (1, 1)),
    ((-1, 0),),
    ((1, 0),),
)
MIB = 1024 * 1024
ANY = pl.BlockSpec(memory_space=pl.ANY)
HBM = pl.BlockSpec(memory_space=pltpu.HBM)
VMEM = pl.BlockSpec(memory_space=pltpu.VMEM)
SMEM = pl.BlockSpec(memory_space=pltpu.SMEM)


def chunk_of(size, wanted):
    return max(c for c in range(1, wanted + 1) if size % c == 0)


def x_size():
    return lax.axis_size("gz") * lax.axis_size("core")


def travel(packet, step_x, step_y):
    size_x, size_y = x_size(), lax.axis_size("gy")
    pairs = [
        (i * size_y + j, (i + step_x) * size_y + j + step_y)
        for i in range(size_x)
        for j in range(size_y)
        if 0 <= i + step_x < size_x and 0 <= j + step_y < size_y
    ]
    return lax.ppermute(packet, ("gz", "core", "gy"), pairs)


def pack(tiles, lists):
    directions, halo = lists.shape
    _, voxels, channels = tiles.shape

    def kernel(lists_ref, tiles_ref, *packets):
        for d in range(directions):
            for h in range(halo):
                packets[d][h] = tiles_ref[lists_ref[d, h]]

    return pl.pallas_call(
        kernel,
        out_shape=[jax.ShapeDtypeStruct((halo, voxels, channels), tiles.dtype)] * directions,
        in_specs=[SMEM, VMEM],
        out_specs=[VMEM] * directions,
        compiler_params=pltpu.CompilerParams(vmem_limit_bytes=16 * MIB),
        name="pack",
    )(lists, tiles)


def source_table(offsets, inputs, outputs, count, offset_count, tile_slots, empty, after):
    rows, blocks = inputs.shape

    def kernel(offsets_ref, inputs_ref, outputs_ref, count_ref, _, table_ref):
        def clear(k, carry):
            for t in range(tile_slots):
                table_ref[k, t] = empty
            return carry

        lax.fori_loop(0, offset_count, clear, 0)

        def block(n, carry):
            k = offsets_ref[n]
            for q in range(rows):
                table_ref[k, outputs_ref[q, n]] = inputs_ref[q, n]
            return carry

        lax.fori_loop(0, jnp.minimum(count_ref[0], blocks), block, 0)

    return pl.pallas_call(
        kernel,
        out_shape=jax.ShapeDtypeStruct((offset_count, tile_slots + 1), jnp.int32),
        in_specs=[SMEM] * 4 + [ANY],
        out_specs=SMEM,
        cost_estimate=pl.CostEstimate(flops=4 * 10**9, bytes_accessed=MIB, transcendentals=0),
        name="source_table",
    )(offsets, inputs, outputs, count, after)


def gathered(table_ref, ext, k, first, count):
    return jnp.concatenate([ext[table_ref[k, first + t]] for t in range(count)], axis=0)


def forward_and_input_grad(table, tiles, halos, weights, cotangent):
    tile_slots, voxels, channels = tiles.shape
    offset_count = weights.shape[0]
    directions, halo = len(halos), halos[0].shape[0]
    empty = tile_slots + directions * halo
    group = chunk_of(tile_slots, 8)
    groups = tile_slots // group
    rows = group * voxels
    deep = chunk_of(offset_count, 9)
    unroll = chunk_of(offset_count, 3)
    bundles = len(BUNDLES)

    def kernel(table_ref, tiles_ref, *refs):
        halo_refs, refs = refs[:directions], refs[directions:]
        w_hbm, cot_hbm, out_ref, turned_ref, ext, own_ref = refs[:6]
        adjoints, refs = refs[6 : 6 + bundles], refs[6 + bundles :]
        w_ref, cot_ref, grad, acc, even, odd, sems = refs
        copies = [
            pltpu.make_async_copy(tiles_ref, ext.at[pl.ds(0, tile_slots)], sems.at[0]),
            pltpu.make_async_copy(w_hbm, w_ref, sems.at[1]),
            pltpu.make_async_copy(cot_hbm, cot_ref, sems.at[2]),
        ]
        for d, halo_ref in enumerate(halo_refs):
            place = ext.at[pl.ds(tile_slots + d * halo, halo)]
            copies.append(pltpu.make_async_copy(halo_ref, place, sems.at[d + 3]))
        for copy in copies:
            copy.start()
        ext[empty] = jnp.zeros((voxels, channels), ext.dtype)
        for one in (acc, even, odd):
            one[...] = jnp.zeros_like(one)
        for copy in copies:
            copy.wait()

        def turn(step, carry):
            mats = w_ref[pl.ds(step * deep, deep)].reshape(deep * channels, channels)
            for g in range(groups):
                lhs = jnp.concatenate(
                    [
                        gathered(table_ref, ext, step * deep + j, g * group, group)
                        for j in range(deep)
                    ],
                    axis=1,
                )
                acc[g] += jnp.dot(lhs, mats, preferred_element_type=jnp.float32)
            return carry

        lax.fori_loop(0, offset_count // deep, turn, 0)

        def finish(t, carry):
            pre = acc[t // group, pl.ds(pl.multiple_of((t % group) * voxels, voxels), voxels), :]
            sigma = jax.nn.sigmoid(pre)
            out_ref[t] = (ext[t].astype(jnp.float32) + pre * sigma).astype(out_ref.dtype)
            incoming = cot_ref[t].astype(jnp.float32)
            grad[t] = (incoming * sigma * (1.0 + pre * (1.0 - sigma))).astype(grad.dtype)
            return carry

        lax.fori_loop(0, tile_slots, finish, 0)
        for g in range(groups):
            part = grad[pl.ds(g * group, group)].reshape(rows, channels)
            turned_ref[:, pl.ds(g * rows, rows)] = part.astype(jnp.float32).T.astype(jnp.bfloat16)

        def back_turn(step, carry):
            for j in range(unroll):
                k = step * unroll + j
                mat = w_ref[k].astype(jnp.float32).T.astype(jnp.bfloat16)
                for g in range(groups):
                    back = jnp.dot(
                        grad[pl.ds(g * group, group)].reshape(rows, channels),
                        mat,
                        preferred_element_type=jnp.float32,
                    )
                    for t in range(group):
                        slot = table_ref[k, g * group + t]
                        sums = (even, odd)[t % 2]
                        sums[slot] += back[t * voxels : (t + 1) * voxels]
            return carry

        lax.fori_loop(0, offset_count // unroll, back_turn, 0)

        def own(t, carry):
            own_ref[t] = even[t] + odd[t]
            return carry

        lax.fori_loop(0, tile_slots, own, 0)
        for bundle, adjoint in zip(BUNDLES, adjoints):
            for n, pair in enumerate(bundle):
                for h in range(halo):
                    slot = tile_slots + DIRECTIONS.index(pair) * halo + h
                    adjoint[n * halo + h] = (even[slot] + odd[slot]).astype(jnp.bfloat16)

    flops = 4 * offset_count * tile_slots * voxels * channels * channels
    return pl.pallas_call(
        kernel,
        out_shape=[
            jax.ShapeDtypeStruct(tiles.shape, jnp.bfloat16),
            jax.ShapeDtypeStruct((channels, tile_slots * voxels), jnp.bfloat16),
            jax.ShapeDtypeStruct((empty + 1, voxels, channels), jnp.bfloat16),
            jax.ShapeDtypeStruct(tiles.shape, jnp.float32),
        ]
        + [
            jax.ShapeDtypeStruct((len(bundle) * halo, voxels, channels), jnp.bfloat16)
            for bundle in BUNDLES
        ],
        in_specs=[SMEM, HBM] + [ANY] * directions + [HBM, HBM],
        out_specs=[VMEM] * (4 + bundles),
        scratch_shapes=[
            pltpu.VMEM(weights.shape, jnp.bfloat16),
            pltpu.VMEM(tiles.shape, jnp.bfloat16),
            pltpu.VMEM(tiles.shape, jnp.bfloat16),
            pltpu.VMEM((groups, rows, channels), jnp.float32),
            pltpu.VMEM((empty + 1, voxels, channels), jnp.float32),
            pltpu.VMEM((empty + 1, voxels, channels), jnp.float32),
            pltpu.SemaphoreType.DMA((directions + 3,)),
        ],
        compiler_params=pltpu.CompilerParams(vmem_limit_bytes=44 * MIB),
        cost_estimate=pl.CostEstimate(flops=flops, bytes_accessed=20 * MIB, transcendentals=0),
        name="forward_and_input_grad",
    )(table, tiles, *halos, weights, cotangent)


def weight_terms(table, half, ext, turned, offset_count, scale):
    channels = ext.shape[2]
    tile_slots = table.shape[1] - 1
    part = channels // 2
    count = (offset_count + 1) // 2
    first = offset_count - count

    def kernel(table_ref, half_ref, ext_ref, turned_ref, out_ref):
        late = half_ref[0]

        def turn(j, carry):
            k = late * first + j
            terms = jnp.dot(
                turned_ref[...],
                gathered(table_ref, ext_ref, k, 0, tile_slots),
                preferred_element_type=jnp.float32,
            )
            terms = terms.T * scale
            for b in range(2):
                place = 2 * k + b - late * offset_count

                @pl.when((place >= 0) & (place < offset_count))
                def _():
                    out_ref[place] = terms[b * part : (b + 1) * part]

            return carry

        lax.fori_loop(0, count, turn, 0)

    flops = 2 * count * turned.shape[1] * channels * channels
    return pl.pallas_call(
        kernel,
        out_shape=jax.ShapeDtypeStruct((offset_count, part, channels), jnp.float32),
        in_specs=[SMEM, SMEM, VMEM, VMEM],
        out_specs=VMEM,
        compiler_params=pltpu.CompilerParams(vmem_limit_bytes=16 * MIB),
        cost_estimate=pl.CostEstimate(flops=flops, bytes_accessed=6 * MIB, transcendentals=0),
        name="weight_terms",
    )(table, half, ext, turned)


def to_other_core(x):
    return lax.ppermute(x, "core", [(0, 1), (1, 0)])


def ring(first):
    chips, columns = lax.axis_size("gz"), lax.axis_size("gy")
    crossed = chips == columns

    def upright(core):
        return (core == 0 or not crossed) == first

    def move(x, by):
        pairs = []
        for z in range(chips):
            for core in range(2):
                for y in range(columns):
                    to_z, to_y = (z, (y + by) % columns) if upright(core) else ((z + by) % chips, y)
                    pairs.append(((2 * z + core) * columns + y, (2 * to_z + core) * columns + to_y))
        return lax.ppermute(x, ("gz", "core", "gy"), pairs)

    column, chip = lax.axis_index("gy"), lax.axis_index("gz")
    places = [column if upright(core) else chip for core in range(2)]
    size = columns if upright(0) else chips
    return size, jnp.where(lax.axis_index("core") == 0, *places), move


def given_out(total, ring):
    size, place, _ = ring
    blocks = total.reshape(size, total.shape[0] // size, total.shape[1])
    parts = [
        lax.dynamic_index_in_dim(blocks, (place + s) % size, keepdims=False) for s in range(size)
    ]
    return parts[0], [one.astype(jnp.bfloat16) for one in parts[1:]]


def handed(parts, ring):
    return [ring[2](one, s + 1) for s, one in enumerate(parts)]


def added(mine, arrived):
    for one in arrived:
        mine = mine + one.astype(jnp.float32)
    return mine


def fetched(piece, ring):
    return [ring[2](piece, -s) for s in range(1, ring[0])]


def in_order(piece, others, ring):
    size, place, _ = ring
    whole = jnp.zeros((size,) + piece.shape, piece.dtype)
    for s, one in enumerate([piece, *others]):
        whole = lax.dynamic_update_index_in_dim(whole, one, (place + s) % size, 0)
    return whole.reshape(size * piece.shape[0], piece.shape[1])


def together(*values):
    return lax.optimization_barrier(values)


def widen(core, own_half, other_half):
    rows, channels = own_half.shape
    turns = chunk_of(rows // 16, 3)
    step = rows // turns

    def kernel(core_ref, own_ref, other_ref, out_ref):
        mine = pl.program_id(0) // turns == core_ref[0]

        @pl.when(mine)
        def _():
            out_ref[...] = own_ref[...].astype(jnp.float32)

        @pl.when(jnp.logical_not(mine))
        def _():
            out_ref[...] = other_ref[...].astype(jnp.float32)

    half_spec = pl.BlockSpec((step, channels), lambda i: (i % turns, 0))
    return pl.pallas_call(
        kernel,
        grid=(2 * turns,),
        out_shape=jax.ShapeDtypeStruct((2 * rows, channels), jnp.float32),
        in_specs=[SMEM, half_spec, half_spec],
        out_specs=pl.BlockSpec((step, channels), lambda i: (i, 0)),
        compiler_params=pltpu.CompilerParams(vmem_limit_bytes=24 * MIB),
        name="widen",
    )(core, own_half, other_half)


def combine(lists, own, cotangent, returned):
    halo = lists.shape[1]
    tile_slots = own.shape[0]
    arrays = [array for array, _ in returned]

    def kernel(lists_ref, own_ref, cot_ref, *refs):
        out_ref, acc = refs[len(arrays) :]

        def start(t, carry):
            acc[t] = own_ref[t] + cot_ref[t].astype(jnp.float32)
            return carry

        lax.fori_loop(0, tile_slots, start, 0)
        for ref, (_, pairs) in zip(refs, returned):
            for n, pair in enumerate(pairs):
                if pair is not None:
                    for h in range(halo):
                        tile = lists_ref[DIRECTIONS.index(pair), h]
                        acc[tile] += ref[n * halo + h].astype(jnp.float32)

        def finish(t, carry):
            out_ref[t] = acc[t].astype(out_ref.dtype)
            return carry

        lax.fori_loop(0, tile_slots, finish, 0)

    return pl.pallas_call(
        kernel,
        out_shape=jax.ShapeDtypeStruct(own.shape, jnp.bfloat16),
        in_specs=[SMEM] + [VMEM] * (len(arrays) + 2),
        out_specs=VMEM,
        scratch_shapes=[pltpu.VMEM(own.shape, jnp.float32)],
        compiler_params=pltpu.CompilerParams(vmem_limit_bytes=32 * MIB),
        name="combine",
    )(lists, own, cotangent, *arrays)


def shards(
    features, weights, cotangent, send_lists, block_offset, block_input, block_output, block_count
):
    tiles = features[0, 0]
    incoming = cotangent[0, 0]
    lists = send_lists[0, 0]
    tile_slots, voxels, channels = tiles.shape
    directions, halo = lists.shape
    device_total = x_size() * lax.axis_size("gy")
    scale = 1.0 / math.sqrt(voxels * tile_slots * device_total)
    offset_count = weights.shape[0]
    core = lax.axis_index("core").astype(jnp.int32)[None]

    order = sorted(range(directions), key=lambda d: DIRECTIONS[d][1] == 0)
    packets = pack(tiles, lists)
    table = source_table(
        block_offset[0, 0],
        block_input[0, 0].T,
        block_output[0, 0].T,
        block_count[0],
        offset_count,
        tile_slots,
        tile_slots + directions * halo,
        packets[0],
    )
    arrived = {d: travel(packets[d], *DIRECTIONS[d]) for d in order}
    halos = [arrived[d] for d in range(directions)]
    out_features, turned, ext, own, low, high, back, ahead = forward_and_input_grad(
        table, tiles, halos, weights, incoming
    )
    low, high = travel(low, 0, 1), travel(high, 0, -1)

    send = weight_terms(table, 1 - core, ext, turned, offset_count, scale)
    received = to_other_core(send)
    keep = weight_terms(table, core, ext, turned, offset_count, scale)
    half = (keep + received).reshape(-1, channels)
    levels = ring(True), ring(False)
    mine, out = given_out(half, levels[0])
    low, high, *moved = together(low, high, *handed(out, levels[0]))

    back = jnp.concatenate([back, low[:halo], high[:halo]])
    ahead = jnp.concatenate([ahead, low[2 * halo :], high[2 * halo :]])
    back, ahead = travel(back, 1, 0), travel(ahead, -1, 0)

    mine, out = given_out(added(mine, moved), levels[1])
    piece = added(mine, handed(out, levels[1])).astype(jnp.bfloat16)
    piece = in_order(piece, fetched(piece, levels[1]), levels[1])
    back, ahead, piece = together(back, ahead, piece)
    own_half = in_order(piece, fetched(piece, levels[0]), levels[0])
    weight_grad = widen(core, own_half, to_other_core(own_half)).reshape(weights.shape)
    feat_grad = combine(
        lists,
        own,
        incoming,
        [
            (low, (None, (0, -1), None)),
            (high, (None, (0, 1), None)),
            (back, ((-1, 0), (-1, -1), (-1, 1))),
            (ahead, ((1, 0), (1, -1), (1, 1))),
        ],
    )
    return (out_features[None, None], feat_grad[None, None], weight_grad)


def solution(mesh):
    size_x, size_y = mesh.devices.shape
    split = Mesh(mesh.devices.reshape(size_x // 2, 2, size_y), ("gz", "core", "gy"))
    place = P(("gz", "core"), "gy")
    return jax.shard_map(
        shards,
        mesh=split,
        in_specs=(place, P(), place, place, place, place, place, place),
        out_specs=(place, place, P()),
        check_vma=False,
    )
```

```python
import math

import jax
import jax.numpy as jnp
from jax import lax
from jax.experimental import pallas as pl
from jax.experimental.pallas import tpu as pltpu
from jax.sharding import Mesh
from jax.sharding import PartitionSpec as P

DIRECTIONS = ((-1, -1), (-1, 0), (-1, 1), (0, -1), (0, 1), (1, -1), (1, 0), (1, 1))
BUNDLES = (
    ((0, -1),),
    ((0, 1),),
    ((-1, -1), (1, -1)),
    ((-1, 1), (1, 1)),
    ((-1, 0),),
    ((1, 0),),
)
MIB = 1024 * 1024
ANY = pl.BlockSpec(memory_space=pl.ANY)
HBM = pl.BlockSpec(memory_space=pltpu.HBM)
VMEM = pl.BlockSpec(memory_space=pltpu.VMEM)
SMEM = pl.BlockSpec(memory_space=pltpu.SMEM)


def chunk_of(size, wanted):
    return max(c for c in range(1, wanted + 1) if size % c == 0)


def x_size():
    return lax.axis_size("gz") * lax.axis_size("core")


def travel(packet, step_x, step_y):
    size_x, size_y = x_size(), lax.axis_size("gy")
    pairs = [
        (i * size_y + j, (i + step_x) * size_y + j + step_y)
        for i in range(size_x)
        for j in range(size_y)
        if 0 <= i + step_x < size_x and 0 <= j + step_y < size_y
    ]
    return lax.ppermute(packet, ("gz", "core", "gy"), pairs)


def pack(tiles, lists):
    directions, halo = lists.shape
    _, voxels, channels = tiles.shape

    def kernel(lists_ref, tiles_ref, *packets):
        for d in range(directions):
            for h in range(halo):
                packets[d][h] = tiles_ref[lists_ref[d, h]]

    return pl.pallas_call(
        kernel,
        out_shape=[jax.ShapeDtypeStruct((halo, voxels, channels), tiles.dtype)] * directions,
        in_specs=[SMEM, VMEM],
        out_specs=[VMEM] * directions,
        compiler_params=pltpu.CompilerParams(vmem_limit_bytes=16 * MIB),
        name="pack",
    )(lists, tiles)


def source_table(offsets, inputs, outputs, count, offset_count, tile_slots, empty, after):
    rows, blocks = inputs.shape

    def kernel(offsets_ref, inputs_ref, outputs_ref, count_ref, _, table_ref):
        def clear(k, carry):
            for t in range(tile_slots):
                table_ref[k, t] = empty
            return carry

        lax.fori_loop(0, offset_count, clear, 0)

        def block(n, carry):
            k = offsets_ref[n]
            for q in range(rows):
                table_ref[k, outputs_ref[q, n]] = inputs_ref[q, n]
            return carry

        lax.fori_loop(0, jnp.minimum(count_ref[0], blocks), block, 0)

    return pl.pallas_call(
        kernel,
        out_shape=jax.ShapeDtypeStruct((offset_count, tile_slots + 1), jnp.int32),
        in_specs=[SMEM] * 4 + [ANY],
        out_specs=SMEM,
        cost_estimate=pl.CostEstimate(flops=4 * 10**9, bytes_accessed=MIB, transcendentals=0),
        name="source_table",
    )(offsets, inputs, outputs, count, after)


def gathered(table_ref, ext, k, first, count):
    return jnp.concatenate([ext[table_ref[k, first + t]] for t in range(count)], axis=0)


def write_half(table_ref, late, ext, turned_ref, out_ref, scale):
    offset_count, part, _ = out_ref.shape
    tile_slots = table_ref.shape[1] - 1
    count = (offset_count + 1) // 2

    def turn(j, carry):
        k = late * (offset_count - count) + j
        terms = jnp.dot(
            turned_ref[...],
            gathered(table_ref, ext, k, 0, tile_slots),
            preferred_element_type=jnp.float32,
        )
        terms = terms.T * scale
        for b in range(2):
            place = 2 * k + b - late * offset_count

            @pl.when((place >= 0) & (place < offset_count))
            def _():
                out_ref[place] = terms[b * part : (b + 1) * part]

        return carry

    lax.fori_loop(0, count, turn, 0)


def forward_and_terms(table, half, tiles, halos, weights, cotangent, scale):
    tile_slots, voxels, channels = tiles.shape
    offset_count = weights.shape[0]
    directions, halo = len(halos), halos[0].shape[0]
    empty = tile_slots + directions * halo
    group = chunk_of(tile_slots, 16)
    groups = tile_slots // group
    rows = group * voxels
    deep = chunk_of(offset_count, 9)

    def kernel(table_ref, half_ref, tiles_ref, *refs):
        halo_refs, refs = refs[:directions], refs[directions:]
        w_hbm, cot_hbm, out_ref, grad, turned_ref, ext, half_out, w_ref, cot_ref, acc, sems = refs
        copies = [
            pltpu.make_async_copy(tiles_ref, ext.at[pl.ds(0, tile_slots)], sems.at[0]),
            pltpu.make_async_copy(w_hbm, w_ref, sems.at[1]),
            pltpu.make_async_copy(cot_hbm, cot_ref, sems.at[2]),
        ]
        for d, halo_ref in enumerate(halo_refs):
            place = ext.at[pl.ds(tile_slots + d * halo, halo)]
            copies.append(pltpu.make_async_copy(halo_ref, place, sems.at[d + 3]))
        for copy in copies:
            copy.start()
        ext[empty] = jnp.zeros((voxels, channels), ext.dtype)
        acc[...] = jnp.zeros_like(acc)
        for copy in copies:
            copy.wait()

        def turn(step, carry):
            mats = w_ref[pl.ds(step * deep, deep)].reshape(deep * channels, channels)
            for g in range(groups):
                lhs = jnp.concatenate(
                    [
                        gathered(table_ref, ext, step * deep + j, g * group, group)
                        for j in range(deep)
                    ],
                    axis=1,
                )
                acc[g] += jnp.dot(lhs, mats, preferred_element_type=jnp.float32)
            return carry

        lax.fori_loop(0, offset_count // deep, turn, 0)

        def finish(t, carry):
            pre = acc[t // group, pl.ds(pl.multiple_of((t % group) * voxels, voxels), voxels), :]
            sigma = jax.nn.sigmoid(pre)
            out_ref[t] = (ext[t].astype(jnp.float32) + pre * sigma).astype(out_ref.dtype)
            incoming = cot_ref[t].astype(jnp.float32)
            grad[t] = (incoming * sigma * (1.0 + pre * (1.0 - sigma))).astype(grad.dtype)
            return carry

        lax.fori_loop(0, tile_slots, finish, 0)
        for g in range(groups):
            part = grad[pl.ds(g * group, group)].reshape(rows, channels)
            turned_ref[:, pl.ds(g * rows, rows)] = part.astype(jnp.float32).T.astype(jnp.bfloat16)
        write_half(table_ref, half_ref[0], ext, turned_ref, half_out, scale)

    flops = 3 * offset_count * tile_slots * voxels * channels * channels
    return pl.pallas_call(
        kernel,
        out_shape=[
            jax.ShapeDtypeStruct(tiles.shape, jnp.bfloat16),
            jax.ShapeDtypeStruct(tiles.shape, jnp.bfloat16),
            jax.ShapeDtypeStruct((channels, tile_slots * voxels), jnp.bfloat16),
            jax.ShapeDtypeStruct((empty + 1, voxels, channels), jnp.bfloat16),
            jax.ShapeDtypeStruct((offset_count, channels // 2, channels), jnp.float32),
        ],
        in_specs=[SMEM, SMEM, HBM] + [ANY] * directions + [HBM, HBM],
        out_specs=[VMEM] * 5,
        scratch_shapes=[
            pltpu.VMEM(weights.shape, jnp.bfloat16),
            pltpu.VMEM(tiles.shape, jnp.bfloat16),
            pltpu.VMEM((groups, rows, channels), jnp.float32),
            pltpu.SemaphoreType.DMA((directions + 3,)),
        ],
        compiler_params=pltpu.CompilerParams(vmem_limit_bytes=28 * MIB),
        cost_estimate=pl.CostEstimate(flops=flops, bytes_accessed=20 * MIB, transcendentals=0),
        name="forward_and_terms",
    )(table, half, tiles, *halos, weights, cotangent)


def weight_terms(table, half, ext, turned, offset_count, scale):
    channels = ext.shape[2]

    def kernel(table_ref, half_ref, ext_ref, turned_ref, out_ref):
        write_half(table_ref, half_ref[0], ext_ref, turned_ref, out_ref, scale)

    flops = offset_count * turned.shape[1] * channels * channels
    return pl.pallas_call(
        kernel,
        out_shape=jax.ShapeDtypeStruct((offset_count, channels // 2, channels), jnp.float32),
        in_specs=[SMEM, SMEM, VMEM, VMEM],
        out_specs=VMEM,
        compiler_params=pltpu.CompilerParams(vmem_limit_bytes=16 * MIB),
        cost_estimate=pl.CostEstimate(flops=flops, bytes_accessed=6 * MIB, transcendentals=0),
        name="weight_terms",
    )(table, half, ext, turned)


def input_grad(table, pre_grad, weights, halo):
    tile_slots, voxels, channels = pre_grad.shape
    offset_count = weights.shape[0]
    empty = tile_slots + len(DIRECTIONS) * halo
    group = chunk_of(tile_slots, 8)
    groups = tile_slots // group
    rows = group * voxels
    unroll = chunk_of(offset_count, 3)
    bundles = len(BUNDLES)

    def kernel(table_ref, grad_any, w_hbm, own_ref, *refs):
        adjoints = refs[:bundles]
        even, odd, grad, w_ref, sems = refs[bundles:]
        copies = [
            pltpu.make_async_copy(grad_any, grad, sems.at[0]),
            pltpu.make_async_copy(w_hbm, w_ref, sems.at[1]),
        ]
        for copy in copies:
            copy.start()
        for one in (even, odd):
            one[...] = jnp.zeros_like(one)
        for copy in copies:
            copy.wait()

        def turn(step, carry):
            for j in range(unroll):
                k = step * unroll + j
                mat = w_ref[k].astype(jnp.float32).T.astype(jnp.bfloat16)
                for g in range(groups):
                    back = jnp.dot(
                        grad[pl.ds(g * group, group)].reshape(rows, channels),
                        mat,
                        preferred_element_type=jnp.float32,
                    )
                    for t in range(group):
                        slot = table_ref[k, g * group + t]
                        sums = (even, odd)[t % 2]
                        sums[slot] += back[t * voxels : (t + 1) * voxels]
            return carry

        lax.fori_loop(0, offset_count // unroll, turn, 0)

        def own(t, carry):
            own_ref[t] = even[t] + odd[t]
            return carry

        lax.fori_loop(0, tile_slots, own, 0)
        for bundle, adjoint in zip(BUNDLES, adjoints):
            for n, pair in enumerate(bundle):
                for h in range(halo):
                    slot = tile_slots + DIRECTIONS.index(pair) * halo + h
                    adjoint[n * halo + h] = (even[slot] + odd[slot]).astype(jnp.bfloat16)

    flops = 2 * offset_count * tile_slots * voxels * channels * channels
    return pl.pallas_call(
        kernel,
        out_shape=[jax.ShapeDtypeStruct(pre_grad.shape, jnp.float32)]
        + [
            jax.ShapeDtypeStruct((len(bundle) * halo, voxels, channels), jnp.bfloat16)
            for bundle in BUNDLES
        ],
        in_specs=[SMEM, ANY, HBM],
        out_specs=[VMEM] * (bundles + 1),
        scratch_shapes=[pltpu.VMEM((empty + 1, voxels, channels), jnp.float32)] * 2
        + [
            pltpu.VMEM(pre_grad.shape, jnp.bfloat16),
            pltpu.VMEM(weights.shape, jnp.bfloat16),
            pltpu.SemaphoreType.DMA((2,)),
        ],
        compiler_params=pltpu.CompilerParams(vmem_limit_bytes=28 * MIB),
        cost_estimate=pl.CostEstimate(flops=flops, bytes_accessed=12 * MIB, transcendentals=0),
        name="input_grad",
    )(table, pre_grad, weights)


def to_other_core(x):
    return lax.ppermute(x, "core", [(0, 1), (1, 0)])


def ring(first):
    chips, columns = lax.axis_size("gz"), lax.axis_size("gy")
    crossed = chips == columns

    def upright(core):
        return (core == 0 or not crossed) == first

    def move(x, by):
        pairs = []
        for z in range(chips):
            for core in range(2):
                for y in range(columns):
                    to_z, to_y = (z, (y + by) % columns) if upright(core) else ((z + by) % chips, y)
                    pairs.append(((2 * z + core) * columns + y, (2 * to_z + core) * columns + to_y))
        return lax.ppermute(x, ("gz", "core", "gy"), pairs)

    column, chip = lax.axis_index("gy"), lax.axis_index("gz")
    places = [column if upright(core) else chip for core in range(2)]
    size = columns if upright(0) else chips
    return size, jnp.where(lax.axis_index("core") == 0, *places), move


def given_out(terms, ring):
    size, place, _ = ring
    parts = []
    for s in range(size):
        blocks = [
            lax.dynamic_index_in_dim(
                one.reshape(size, one.shape[0] // size, one.shape[1]), (place + s) % size, keepdims=False
            )
            for one in terms
        ]
        parts.append(sum(blocks[1:], blocks[0]))
    return parts[0], [one.astype(jnp.bfloat16) for one in parts[1:]]


def handed(parts, ring):
    return [ring[2](one, s + 1) for s, one in enumerate(parts)]


def added(mine, arrived):
    for one in arrived:
        mine = mine + one.astype(jnp.float32)
    return mine


def fetched(piece, ring):
    return [ring[2](piece, -s) for s in range(1, ring[0])]


def in_order(piece, others, ring):
    size, place, _ = ring
    whole = jnp.zeros((size,) + piece.shape, piece.dtype)
    for s, one in enumerate([piece, *others]):
        whole = lax.dynamic_update_index_in_dim(whole, one, (place + s) % size, 0)
    return whole.reshape(size * piece.shape[0], piece.shape[1])


def together(*values):
    return lax.optimization_barrier(values)


def widen(core, own_half, other_half):
    rows, channels = own_half.shape
    turns = chunk_of(rows // 16, 3)
    step = rows // turns

    def kernel(core_ref, own_ref, other_ref, out_ref):
        mine = pl.program_id(0) // turns == core_ref[0]

        @pl.when(mine)
        def _():
            out_ref[...] = own_ref[...].astype(jnp.float32)

        @pl.when(jnp.logical_not(mine))
        def _():
            out_ref[...] = other_ref[...].astype(jnp.float32)

    half_spec = pl.BlockSpec((step, channels), lambda i: (i % turns, 0))
    return pl.pallas_call(
        kernel,
        grid=(2 * turns,),
        out_shape=jax.ShapeDtypeStruct((2 * rows, channels), jnp.float32),
        in_specs=[SMEM, half_spec, half_spec],
        out_specs=pl.BlockSpec((step, channels), lambda i: (i, 0)),
        compiler_params=pltpu.CompilerParams(vmem_limit_bytes=24 * MIB),
        name="widen",
    )(core, own_half, other_half)


def combine(lists, own, cotangent, returned):
    halo = lists.shape[1]
    tile_slots = own.shape[0]
    arrays = [array for array, _ in returned]

    def kernel(lists_ref, own_ref, cot_ref, *refs):
        out_ref, acc = refs[len(arrays) :]

        def start(t, carry):
            acc[t] = own_ref[t] + cot_ref[t].astype(jnp.float32)
            return carry

        lax.fori_loop(0, tile_slots, start, 0)
        for ref, (_, pairs) in zip(refs, returned):
            for n, pair in enumerate(pairs):
                for h in range(halo):
                    tile = lists_ref[DIRECTIONS.index(pair), h]
                    acc[tile] += ref[n * halo + h].astype(jnp.float32)

        def finish(t, carry):
            out_ref[t] = acc[t].astype(out_ref.dtype)
            return carry

        lax.fori_loop(0, tile_slots, finish, 0)

    return pl.pallas_call(
        kernel,
        out_shape=jax.ShapeDtypeStruct(own.shape, jnp.bfloat16),
        in_specs=[SMEM] + [VMEM] * (len(arrays) + 2),
        out_specs=VMEM,
        scratch_shapes=[pltpu.VMEM(own.shape, jnp.float32)],
        compiler_params=pltpu.CompilerParams(vmem_limit_bytes=32 * MIB),
        name="combine",
    )(lists, own, cotangent, *arrays)


def shards(
    features, weights, cotangent, send_lists, block_offset, block_input, block_output, block_count
):
    tiles = features[0, 0]
    incoming = cotangent[0, 0]
    lists = send_lists[0, 0]
    tile_slots, voxels, channels = tiles.shape
    directions, halo = lists.shape
    device_total = x_size() * lax.axis_size("gy")
    scale = 1.0 / math.sqrt(voxels * tile_slots * device_total)
    offset_count = weights.shape[0]
    core = lax.axis_index("core").astype(jnp.int32)[None]

    order = sorted(range(directions), key=lambda d: DIRECTIONS[d][1] == 0)
    packets = pack(tiles, lists)
    table = source_table(
        block_offset[0, 0],
        block_input[0, 0].T,
        block_output[0, 0].T,
        block_count[0],
        offset_count,
        tile_slots,
        tile_slots + directions * halo,
        packets[0],
    )
    arrived = {d: travel(packets[d], *DIRECTIONS[d]) for d in order}
    halos = [arrived[d] for d in range(directions)]
    out_features, pre_grad, turned, ext, send = forward_and_terms(
        table, 1 - core, tiles, halos, weights, incoming, scale
    )
    received = to_other_core(send)
    keep = weight_terms(table, core, ext, turned, offset_count, scale)
    levels = ring(True), ring(False)
    mine, out = given_out([keep.reshape(-1, channels), received.reshape(-1, channels)], levels[0])

    pre_grad, *out = together(pre_grad, *out)
    moved = handed(out, levels[0])
    own, low, high, low_both, high_both, back, ahead = input_grad(table, pre_grad, weights, halo)
    low, *moved = together(low, *moved)
    low, high = travel(low, 0, 1), travel(high, 0, -1)
    low_both, high_both = travel(low_both, 0, 1), travel(high_both, 0, -1)

    mine, out = given_out([added(mine, moved)], levels[1])
    piece = added(mine, handed(out, levels[1])).astype(jnp.bfloat16)
    low, high, piece = together(low, high, piece)
    piece = in_order(piece, fetched(piece, levels[1]), levels[1])
    low_both, high_both, piece = together(low_both, high_both, piece)
    back = jnp.concatenate([back, low_both[:halo], high_both[:halo]])
    ahead = jnp.concatenate([ahead, low_both[halo:], high_both[halo:]])
    back, ahead = travel(back, 1, 0), travel(ahead, -1, 0)
    own_half = in_order(piece, fetched(piece, levels[0]), levels[0])
    back, ahead, own_half = together(back, ahead, own_half)
    weight_grad = widen(core, own_half, to_other_core(own_half)).reshape(weights.shape)
    feat_grad = combine(
        lists,
        own,
        incoming,
        [
            (low, ((0, -1),)),
            (high, ((0, 1),)),
            (back, ((-1, 0), (-1, -1), (-1, 1))),
            (ahead, ((1, 0), (1, -1), (1, 1))),
        ],
    )
    return (out_features[None, None], feat_grad[None, None], weight_grad)


def solution(mesh):
    size_x, size_y = mesh.devices.shape
    split = Mesh(mesh.devices.reshape(size_x // 2, 2, size_y), ("gz", "core", "gy"))
    place = P(("gz", "core"), "gy")
    return jax.shard_map(
        shards,
        mesh=split,
        in_specs=(place, P(), place, place, place, place, place, place),
        out_specs=(place, place, P()),
        check_vma=False,
    )
```

```python
import math

import jax
import jax.numpy as jnp
from jax import lax
from jax.experimental import pallas as pl
from jax.experimental.pallas import tpu as pltpu
from jax.sharding import Mesh
from jax.sharding import PartitionSpec as P

DIRECTIONS = ((-1, -1), (-1, 0), (-1, 1), (0, -1), (0, 1), (1, -1), (1, 0), (1, 1))
PACKETS = (
    ((-1, -1), (-1, 0), (-1, 1)),
    ((1, -1), (1, 0), (1, 1)),
    ((0, -1),),
    ((0, 1),),
)
BUNDLES = (
    ((0, -1),),
    ((0, 1),),
    ((-1, -1), (1, -1)),
    ((-1, 1), (1, 1)),
    ((-1, 0),),
    ((1, 0),),
)
MIB = 1024 * 1024
ANY = pl.BlockSpec(memory_space=pl.ANY)
HBM = pl.BlockSpec(memory_space=pltpu.HBM)
VMEM = pl.BlockSpec(memory_space=pltpu.VMEM)
SMEM = pl.BlockSpec(memory_space=pltpu.SMEM)


def chunk_of(size, wanted):
    return max(c for c in range(1, wanted + 1) if size % c == 0)


def x_size():
    return lax.axis_size("gz") * lax.axis_size("core")


def travel(packet, step_x, step_y):
    size_x, size_y = x_size(), lax.axis_size("gy")
    pairs = [
        (i * size_y + j, (i + step_x) * size_y + j + step_y)
        for i in range(size_x)
        for j in range(size_y)
        if 0 <= i + step_x < size_x and 0 <= j + step_y < size_y
    ]
    return lax.ppermute(packet, ("gz", "core", "gy"), pairs)


def pack(tiles, lists):
    halo = lists.shape[1]
    _, voxels, channels = tiles.shape

    def kernel(lists_ref, tiles_ref, *packets):
        for packet, pairs in zip(packets, PACKETS):
            for n, pair in enumerate(pairs):
                for h in range(halo):
                    packet[n * halo + h] = tiles_ref[lists_ref[DIRECTIONS.index(pair), h]]

    return pl.pallas_call(
        kernel,
        out_shape=[
            jax.ShapeDtypeStruct((len(pairs) * halo, voxels, channels), tiles.dtype)
            for pairs in PACKETS
        ],
        in_specs=[SMEM, VMEM],
        out_specs=[VMEM] * len(PACKETS),
        compiler_params=pltpu.CompilerParams(vmem_limit_bytes=16 * MIB),
        name="pack",
    )(lists, tiles)


def source_table(offsets, inputs, outputs, count, offset_count, tile_slots, empty, after):
    rows, blocks = inputs.shape

    def kernel(offsets_ref, inputs_ref, outputs_ref, count_ref, _, table_ref):
        def clear(k, carry):
            for t in range(tile_slots):
                table_ref[k, t] = empty
            return carry

        lax.fori_loop(0, offset_count, clear, 0)

        def block(n, carry):
            k = offsets_ref[n]
            for q in range(rows):
                table_ref[k, outputs_ref[q, n]] = inputs_ref[q, n]
            return carry

        lax.fori_loop(0, jnp.minimum(count_ref[0], blocks), block, 0)

    return pl.pallas_call(
        kernel,
        out_shape=jax.ShapeDtypeStruct((offset_count, tile_slots + 1), jnp.int32),
        in_specs=[SMEM] * 4 + [ANY],
        out_specs=SMEM,
        cost_estimate=pl.CostEstimate(flops=4 * 10**9, bytes_accessed=MIB, transcendentals=0),
        name="source_table",
    )(offsets, inputs, outputs, count, after)


def gathered(table_ref, ext, k, first, count):
    return jnp.concatenate([ext[table_ref[k, first + t]] for t in range(count)], axis=0)


def write_half(table_ref, late, ext, turned_ref, out_ref, scale):
    offset_count, part, _ = out_ref.shape
    tile_slots = table_ref.shape[1] - 1
    count = (offset_count + 1) // 2

    def turn(j, carry):
        k = late * (offset_count - count) + j
        terms = jnp.dot(
            turned_ref[...],
            gathered(table_ref, ext, k, 0, tile_slots),
            preferred_element_type=jnp.float32,
        )
        terms = terms.T * scale
        for b in range(2):
            place = 2 * k + b - late * offset_count

            @pl.when((place >= 0) & (place < offset_count))
            def _():
                out_ref[place] = terms[b * part : (b + 1) * part]

        return carry

    lax.fori_loop(0, count, turn, 0)


def forward_and_terms(table, half, tiles, halos, weights, cotangent, scale):
    tile_slots, voxels, channels = tiles.shape
    offset_count = weights.shape[0]
    arrays = [array for array, _ in halos]
    blocks = [
        (source, n, DIRECTIONS.index(pair))
        for source, (_, pairs) in enumerate(halos)
        for n, pair in enumerate(pairs)
        if pair is not None
    ]
    halo = arrays[0].shape[0] // len(halos[0][1])
    empty = tile_slots + len(blocks) * halo
    group = chunk_of(tile_slots, 8)
    groups = tile_slots // group
    rows = group * voxels
    deep = chunk_of(offset_count, 9)

    def kernel(table_ref, half_ref, tiles_ref, *refs):
        halo_refs, refs = refs[: len(arrays)], refs[len(arrays) :]
        w_hbm, cot_hbm, out_hbm, grad_hbm, turned_hbm, ext_hbm, half_out = refs[:7]
        w_ref, cot_ref, out_ref, grad, turned_ref, ext, acc, sems = refs[7:]
        copies = [
            pltpu.make_async_copy(tiles_ref, ext.at[pl.ds(0, tile_slots)], sems.at[0]),
            pltpu.make_async_copy(w_hbm, w_ref, sems.at[1]),
        ]
        for n, (source, place, d) in enumerate(blocks):
            copies.append(
                pltpu.make_async_copy(
                    halo_refs[source].at[pl.ds(place * halo, halo)],
                    ext.at[pl.ds(tile_slots + d * halo, halo)],
                    sems.at[n + 7],
                )
            )
        load_cot = pltpu.make_async_copy(cot_hbm, cot_ref, sems.at[2])
        for copy in copies + [load_cot]:
            copy.start()
        ext[empty] = jnp.zeros((voxels, channels), ext.dtype)
        acc[...] = jnp.zeros_like(acc)
        for copy in copies:
            copy.wait()
        saves = [pltpu.make_async_copy(ext, ext_hbm, sems.at[3])]
        saves[0].start()

        def turn(step, carry):
            mats = w_ref[pl.ds(step * deep, deep)].reshape(deep * channels, channels)
            for g in range(groups):
                lhs = jnp.concatenate(
                    [
                        gathered(table_ref, ext, step * deep + j, g * group, group)
                        for j in range(deep)
                    ],
                    axis=1,
                )
                acc[g] += jnp.dot(lhs, mats, preferred_element_type=jnp.float32)
            return carry

        lax.fori_loop(0, offset_count // deep, turn, 0)
        load_cot.wait()

        def finish(t, carry):
            pre = acc[t // group, pl.ds(pl.multiple_of((t % group) * voxels, voxels), voxels), :]
            sigma = jax.nn.sigmoid(pre)
            out_ref[t] = (ext[t].astype(jnp.float32) + pre * sigma).astype(out_ref.dtype)
            incoming = cot_ref[t].astype(jnp.float32)
            grad[t] = (incoming * sigma * (1.0 + pre * (1.0 - sigma))).astype(grad.dtype)
            return carry

        lax.fori_loop(0, tile_slots, finish, 0)
        for g in range(groups):
            part = grad[pl.ds(g * group, group)].reshape(rows, channels)
            turned_ref[:, pl.ds(g * rows, rows)] = part.astype(jnp.float32).T.astype(jnp.bfloat16)
        saves += [
            pltpu.make_async_copy(out_ref, out_hbm, sems.at[4]),
            pltpu.make_async_copy(grad, grad_hbm, sems.at[5]),
            pltpu.make_async_copy(turned_ref, turned_hbm, sems.at[6]),
        ]
        for save in saves[1:]:
            save.start()
        write_half(table_ref, half_ref[0], ext, turned_ref, half_out, scale)
        for save in saves:
            save.wait()

    flops = 3 * offset_count * tile_slots * voxels * channels * channels
    out_shape = [
        jax.ShapeDtypeStruct(tiles.shape, jnp.bfloat16),
        jax.ShapeDtypeStruct(tiles.shape, jnp.bfloat16),
        jax.ShapeDtypeStruct((channels, tile_slots * voxels), jnp.bfloat16),
        jax.ShapeDtypeStruct((empty + 1, voxels, channels), jnp.bfloat16),
        jax.ShapeDtypeStruct((offset_count, channels // 2, channels), jnp.float32),
    ]
    return pl.pallas_call(
        kernel,
        out_shape=out_shape,
        in_specs=[SMEM, SMEM, HBM] + [ANY] * len(arrays) + [HBM, HBM],
        out_specs=[HBM] * 4 + [VMEM],
        scratch_shapes=[
            pltpu.VMEM(weights.shape, jnp.bfloat16),
            pltpu.VMEM(tiles.shape, jnp.bfloat16),
        ]
        + [pltpu.VMEM(one.shape, one.dtype) for one in out_shape[:4]]
        + [
            pltpu.VMEM((groups, rows, channels), jnp.float32),
            pltpu.SemaphoreType.DMA((len(blocks) + 7,)),
        ],
        compiler_params=pltpu.CompilerParams(vmem_limit_bytes=28 * MIB),
        cost_estimate=pl.CostEstimate(flops=flops, bytes_accessed=20 * MIB, transcendentals=0),
        name="forward_and_terms",
    )(table, half, tiles, *arrays, weights, cotangent)


def weight_terms(table, half, ext, turned, offset_count, scale):
    channels = ext.shape[2]

    def kernel(table_ref, half_ref, ext_hbm, turned_hbm, out_ref, ext_ref, turned_ref, sems):
        cut = ext_ref.shape[0] // 2
        copies = [
            pltpu.make_async_copy(ext_hbm.at[pl.ds(0, cut)], ext_ref.at[pl.ds(0, cut)], sems.at[0]),
            pltpu.make_async_copy(
                ext_hbm.at[pl.ds(cut, ext_ref.shape[0] - cut)],
                ext_ref.at[pl.ds(cut, ext_ref.shape[0] - cut)],
                sems.at[1],
            ),
            pltpu.make_async_copy(turned_hbm, turned_ref, sems.at[2]),
        ]
        for copy in copies:
            copy.start()
        for copy in copies:
            copy.wait()
        write_half(table_ref, half_ref[0], ext_ref, turned_ref, out_ref, scale)

    flops = offset_count * turned.shape[1] * channels * channels
    return pl.pallas_call(
        kernel,
        out_shape=jax.ShapeDtypeStruct((offset_count, channels // 2, channels), jnp.float32),
        in_specs=[SMEM, SMEM, HBM, HBM],
        out_specs=VMEM,
        scratch_shapes=[
            pltpu.VMEM(ext.shape, ext.dtype),
            pltpu.VMEM(turned.shape, turned.dtype),
            pltpu.SemaphoreType.DMA((3,)),
        ],
        compiler_params=pltpu.CompilerParams(vmem_limit_bytes=20 * MIB),
        cost_estimate=pl.CostEstimate(flops=flops, bytes_accessed=6 * MIB, transcendentals=0),
        name="weight_terms",
    )(table, half, ext, turned)


def input_grad(table, pre_grad, weights, halo):
    tile_slots, voxels, channels = pre_grad.shape
    offset_count = weights.shape[0]
    empty = tile_slots + len(DIRECTIONS) * halo
    group = chunk_of(tile_slots, 8)
    groups = tile_slots // group
    rows = group * voxels
    unroll = chunk_of(offset_count, 3)
    bundles = len(BUNDLES)

    def kernel(table_ref, grad_hbm, w_hbm, own_ref, *refs):
        adjoints = refs[:bundles]
        even, odd, grad, w_ref, sems = refs[bundles:]
        copies = [
            pltpu.make_async_copy(grad_hbm, grad, sems.at[0]),
            pltpu.make_async_copy(w_hbm, w_ref, sems.at[1]),
        ]
        for copy in copies:
            copy.start()
        for one in (even, odd):
            one[...] = jnp.zeros_like(one)
        for copy in copies:
            copy.wait()

        def turn(step, carry):
            for j in range(unroll):
                k = step * unroll + j
                mat = w_ref[k].astype(jnp.float32).T.astype(jnp.bfloat16)
                for g in range(groups):
                    back = jnp.dot(
                        grad[pl.ds(g * group, group)].reshape(rows, channels),
                        mat,
                        preferred_element_type=jnp.float32,
                    )
                    for t in range(group):
                        slot = table_ref[k, g * group + t]
                        sums = (even, odd)[t % 2]
                        sums[slot] += back[t * voxels : (t + 1) * voxels]
            return carry

        lax.fori_loop(0, offset_count // unroll, turn, 0)

        def own(t, carry):
            own_ref[t] = even[t] + odd[t]
            return carry

        lax.fori_loop(0, tile_slots, own, 0)
        for bundle, adjoint in zip(BUNDLES, adjoints):
            for n, pair in enumerate(bundle):
                for h in range(halo):
                    slot = tile_slots + DIRECTIONS.index(pair) * halo + h
                    adjoint[n * halo + h] = (even[slot] + odd[slot]).astype(jnp.bfloat16)

    flops = 2 * offset_count * tile_slots * voxels * channels * channels
    return pl.pallas_call(
        kernel,
        out_shape=[jax.ShapeDtypeStruct(pre_grad.shape, jnp.float32)]
        + [
            jax.ShapeDtypeStruct((len(bundle) * halo, voxels, channels), jnp.bfloat16)
            for bundle in BUNDLES
        ],
        in_specs=[SMEM, HBM, HBM],
        out_specs=[VMEM] * (bundles + 1),
        scratch_shapes=[pltpu.VMEM((empty + 1, voxels, channels), jnp.float32)] * 2
        + [
            pltpu.VMEM(pre_grad.shape, jnp.bfloat16),
            pltpu.VMEM(weights.shape, jnp.bfloat16),
            pltpu.SemaphoreType.DMA((2,)),
        ],
        compiler_params=pltpu.CompilerParams(vmem_limit_bytes=28 * MIB),
        cost_estimate=pl.CostEstimate(flops=flops, bytes_accessed=12 * MIB, transcendentals=0),
        name="input_grad",
    )(table, pre_grad, weights)


def to_other_core(x):
    return lax.ppermute(x, "core", [(0, 1), (1, 0)])


def ring(first):
    chips, columns = lax.axis_size("gz"), lax.axis_size("gy")
    crossed = chips == columns

    def upright(core):
        return (core == 0 or not crossed) == first

    def move(x, by):
        pairs = []
        for z in range(chips):
            for core in range(2):
                for y in range(columns):
                    to_z, to_y = (z, (y + by) % columns) if upright(core) else ((z + by) % chips, y)
                    pairs.append(((2 * z + core) * columns + y, (2 * to_z + core) * columns + to_y))
        return lax.ppermute(x, ("gz", "core", "gy"), pairs)

    column, chip = lax.axis_index("gy"), lax.axis_index("gz")
    places = [column if upright(core) else chip for core in range(2)]
    size = columns if upright(0) else chips
    return size, jnp.where(lax.axis_index("core") == 0, *places), move


def given_out(terms, ring):
    size, place, _ = ring
    parts = []
    for s in range(size):
        blocks = [
            lax.dynamic_index_in_dim(
                one.reshape(size, one.shape[0] // size, one.shape[1]), (place + s) % size, keepdims=False
            )
            for one in terms
        ]
        parts.append(sum(blocks[1:], blocks[0]))
    return parts[0], [one.astype(jnp.bfloat16) for one in parts[1:]]


def handed(parts, ring):
    return [ring[2](one, s + 1) for s, one in enumerate(parts)]


def added(mine, arrived):
    for one in arrived:
        mine = mine + one.astype(jnp.float32)
    return mine


def fetched(piece, ring):
    return [ring[2](piece, -s) for s in range(1, ring[0])]


def in_order(piece, others, ring):
    size, place, _ = ring
    whole = jnp.zeros((size,) + piece.shape, piece.dtype)
    for s, one in enumerate([piece, *others]):
        whole = lax.dynamic_update_index_in_dim(whole, one, (place + s) % size, 0)
    return whole.reshape(size * piece.shape[0], piece.shape[1])


def together(*values):
    return lax.optimization_barrier(values)


def widen(core, own_half, other_half):
    rows, channels = own_half.shape
    turns = chunk_of(rows // 16, 3)
    step = rows // turns

    def kernel(core_ref, own_ref, other_ref, out_ref):
        mine = pl.program_id(0) // turns == core_ref[0]

        @pl.when(mine)
        def _():
            out_ref[...] = own_ref[...].astype(jnp.float32)

        @pl.when(jnp.logical_not(mine))
        def _():
            out_ref[...] = other_ref[...].astype(jnp.float32)

    half_spec = pl.BlockSpec((step, channels), lambda i: (i % turns, 0))
    return pl.pallas_call(
        kernel,
        grid=(2 * turns,),
        out_shape=jax.ShapeDtypeStruct((2 * rows, channels), jnp.float32),
        in_specs=[SMEM, half_spec, half_spec],
        out_specs=pl.BlockSpec((step, channels), lambda i: (i, 0)),
        compiler_params=pltpu.CompilerParams(vmem_limit_bytes=24 * MIB),
        name="widen",
    )(core, own_half, other_half)


def combine(lists, own, cotangent, returned):
    halo = lists.shape[1]
    tile_slots = own.shape[0]
    arrays = [array for array, _ in returned]

    def kernel(lists_ref, own_ref, cot_ref, *refs):
        out_ref, acc = refs[len(arrays) :]

        def start(t, carry):
            acc[t] = own_ref[t] + cot_ref[t].astype(jnp.float32)
            return carry

        lax.fori_loop(0, tile_slots, start, 0)
        for ref, (_, pairs) in zip(refs, returned):
            for n, pair in enumerate(pairs):
                for h in range(halo):
                    tile = lists_ref[DIRECTIONS.index(pair), h]
                    acc[tile] += ref[n * halo + h].astype(jnp.float32)

        def finish(t, carry):
            out_ref[t] = acc[t].astype(out_ref.dtype)
            return carry

        lax.fori_loop(0, tile_slots, finish, 0)

    return pl.pallas_call(
        kernel,
        out_shape=jax.ShapeDtypeStruct(own.shape, jnp.bfloat16),
        in_specs=[SMEM] + [VMEM] * (len(arrays) + 2),
        out_specs=VMEM,
        scratch_shapes=[pltpu.VMEM(own.shape, jnp.float32)],
        compiler_params=pltpu.CompilerParams(vmem_limit_bytes=32 * MIB),
        name="combine",
    )(lists, own, cotangent, *arrays)


def shards(
    features, weights, cotangent, send_lists, block_offset, block_input, block_output, block_count
):
    tiles = features[0, 0]
    incoming = cotangent[0, 0]
    lists = send_lists[0, 0]
    tile_slots, voxels, channels = tiles.shape
    directions, halo = lists.shape
    device_total = x_size() * lax.axis_size("gy")
    scale = 1.0 / math.sqrt(voxels * tile_slots * device_total)
    offset_count = weights.shape[0]
    core = lax.axis_index("core").astype(jnp.int32)[None]

    behind, ahead, low, high = packets = pack(tiles, lists)
    table = source_table(
        block_offset[0, 0],
        block_input[0, 0].T,
        block_output[0, 0].T,
        block_count[0],
        offset_count,
        tile_slots,
        tile_slots + directions * halo,
        packets[0],
    )
    low, high = travel(low, 0, -1), travel(high, 0, 1)
    behind, ahead = travel(behind, -1, 0), travel(ahead, 1, 0)
    low, high, behind, ahead = together(low, high, behind, ahead)
    low_both = travel(jnp.concatenate([behind[:halo], ahead[:halo]]), 0, -1)
    high_both = travel(jnp.concatenate([behind[2 * halo :], ahead[2 * halo :]]), 0, 1)
    halos = [
        (behind, (None, (-1, 0), None)),
        (ahead, (None, (1, 0), None)),
        (low, ((0, -1),)),
        (high, ((0, 1),)),
        (low_both, ((-1, -1), (1, -1))),
        (high_both, ((-1, 1), (1, 1))),
    ]
    out_features, pre_grad, turned, ext, send = forward_and_terms(
        table, 1 - core, tiles, halos, weights, incoming, scale
    )
    received = to_other_core(send)
    own, low, high, low_both, high_both, behind, ahead = input_grad(table, pre_grad, weights, halo)
    ext, low, high, low_both, high_both = together(ext, low, high, low_both, high_both)
    low, high = travel(low, 0, 1), travel(high, 0, -1)
    low_both, high_both = travel(low_both, 0, 1), travel(high_both, 0, -1)
    keep = weight_terms(table, core, ext, turned, offset_count, scale)

    levels = ring(True), ring(False)
    mine, out = given_out([keep.reshape(-1, channels), received.reshape(-1, channels)], levels[0])
    moved = handed(out, levels[0])
    low, high, low_both, high_both, *moved = together(low, high, low_both, high_both, *moved)
    behind = jnp.concatenate([behind, low_both[:halo], high_both[:halo]])
    ahead = jnp.concatenate([ahead, low_both[halo:], high_both[halo:]])
    behind, ahead = travel(behind, 1, 0), travel(ahead, -1, 0)

    mine, out = given_out([added(mine, moved)], levels[1])
    piece = added(mine, handed(out, levels[1])).astype(jnp.bfloat16)
    piece = in_order(piece, fetched(piece, levels[1]), levels[1])
    behind, ahead, piece = together(behind, ahead, piece)
    own_half = in_order(piece, fetched(piece, levels[0]), levels[0])
    feat_grad = combine(
        lists,
        own,
        incoming,
        [
            (low, ((0, -1),)),
            (high, ((0, 1),)),
            (behind, ((-1, 0), (-1, -1), (-1, 1))),
            (ahead, ((1, 0), (1, -1), (1, 1))),
        ],
    )
    feat_grad, own_half = together(feat_grad, own_half)
    weight_grad = widen(core, own_half, to_other_core(own_half)).reshape(weights.shape)
    return (out_features[None, None], feat_grad[None, None], weight_grad)


def solution(mesh):
    size_x, size_y = mesh.devices.shape
    split = Mesh(mesh.devices.reshape(size_x // 2, 2, size_y), ("gz", "core", "gy"))
    place = P(("gz", "core"), "gy")
    return jax.shard_map(
        shards,
        mesh=split,
        in_specs=(place, P(), place, place, place, place, place, place),
        out_specs=(place, place, P()),
        check_vma=False,
    )
```

```python
import math

import jax
import jax.numpy as jnp
from jax import lax
from jax.experimental import pallas as pl
from jax.experimental.pallas import tpu as pltpu
from jax.sharding import Mesh
from jax.sharding import PartitionSpec as P

DIRECTIONS = ((-1, -1), (-1, 0), (-1, 1), (0, -1), (0, 1), (1, -1), (1, 0), (1, 1))
BUNDLES = (
    ((0, -1),),
    ((0, 1),),
    ((-1, -1), (1, -1)),
    ((-1, 1), (1, 1)),
    ((-1, 0),),
    ((1, 0),),
)
MIB = 1024 * 1024
ANY = pl.BlockSpec(memory_space=pl.ANY)
HBM = pl.BlockSpec(memory_space=pltpu.HBM)
VMEM = pl.BlockSpec(memory_space=pltpu.VMEM)
SMEM = pl.BlockSpec(memory_space=pltpu.SMEM)


def chunk_of(size, wanted):
    return max(c for c in range(1, wanted + 1) if size % c == 0)


def x_size():
    return lax.axis_size("gz") * lax.axis_size("core")


def travel(packet, step_x, step_y):
    size_x, size_y = x_size(), lax.axis_size("gy")
    pairs = [
        (i * size_y + j, (i + step_x) * size_y + j + step_y)
        for i in range(size_x)
        for j in range(size_y)
        if 0 <= i + step_x < size_x and 0 <= j + step_y < size_y
    ]
    return lax.ppermute(packet, ("gz", "core", "gy"), pairs)


def pack(tiles, lists):
    halo = lists.shape[1]
    _, voxels, channels = tiles.shape

    def kernel(lists_ref, tiles_ref, *packets):
        for d, packet in enumerate(packets):
            for h in range(halo):
                packet[h] = tiles_ref[lists_ref[d, h]]

    return pl.pallas_call(
        kernel,
        out_shape=[jax.ShapeDtypeStruct((halo, voxels, channels), tiles.dtype)] * len(DIRECTIONS),
        in_specs=[SMEM, VMEM],
        out_specs=[VMEM] * len(DIRECTIONS),
        compiler_params=pltpu.CompilerParams(vmem_limit_bytes=16 * MIB),
        name="pack",
    )(lists, tiles)


def source_table(offsets, inputs, outputs, count, offset_count, tile_slots, empty, after):
    rows, blocks = inputs.shape

    def kernel(offsets_ref, inputs_ref, outputs_ref, count_ref, _, table_ref):
        def clear(k, carry):
            for t in range(tile_slots):
                table_ref[k, t] = empty
            return carry

        lax.fori_loop(0, offset_count, clear, 0)

        def block(n, carry):
            k = offsets_ref[n]
            for q in range(rows):
                table_ref[k, outputs_ref[q, n]] = inputs_ref[q, n]
            return carry

        lax.fori_loop(0, jnp.minimum(count_ref[0], blocks), block, 0)

    return pl.pallas_call(
        kernel,
        out_shape=jax.ShapeDtypeStruct((offset_count, tile_slots + 1), jnp.int32),
        in_specs=[SMEM] * 4 + [ANY],
        out_specs=SMEM,
        cost_estimate=pl.CostEstimate(flops=4 * 10**9, bytes_accessed=MIB, transcendentals=0),
        name="source_table",
    )(offsets, inputs, outputs, count, after)


def gathered(table_ref, ext, k, first, count):
    return jnp.concatenate([ext[table_ref[k, first + t]] for t in range(count)], axis=0)


def write_half(table_ref, late, ext, turned_ref, out_ref, scale):
    offset_count, part, _ = out_ref.shape
    tile_slots = table_ref.shape[1] - 1
    count = (offset_count + 1) // 2

    def turn(j, carry):
        k = late * (offset_count - count) + j
        terms = jnp.dot(
            turned_ref[...],
            gathered(table_ref, ext, k, 0, tile_slots),
            preferred_element_type=jnp.float32,
        )
        terms = terms.T * scale
        for b in range(2):
            place = 2 * k + b - late * offset_count

            @pl.when((place >= 0) & (place < offset_count))
            def _():
                out_ref[place] = terms[b * part : (b + 1) * part]

        return carry

    lax.fori_loop(0, count, turn, 0)


def forward_and_terms(table, half, tiles, halos, weights, cotangent, scale):
    tile_slots, voxels, channels = tiles.shape
    offset_count = weights.shape[0]
    directions, halo = len(halos), halos[0].shape[0]
    empty = tile_slots + directions * halo
    group = chunk_of(tile_slots, 8)
    groups = tile_slots // group
    rows = group * voxels
    deep = chunk_of(offset_count, 9)

    def kernel(table_ref, half_ref, tiles_ref, *refs):
        halo_refs, refs = refs[:directions], refs[directions:]
        w_hbm, cot_hbm, out_hbm, grad_hbm, turned_hbm, ext_hbm, half_out = refs[:7]
        w_ref, cot_ref, out_ref, grad, turned_ref, ext, acc, sems, w_sems = refs[7:]
        copies = [pltpu.make_async_copy(tiles_ref, ext.at[pl.ds(0, tile_slots)], sems.at[0])]
        for d, halo_ref in enumerate(halo_refs):
            place = ext.at[pl.ds(tile_slots + d * halo, halo)]
            copies.append(pltpu.make_async_copy(halo_ref, place, sems.at[d + 6]))

        def load_mats(step):
            part = pl.ds(step * deep, deep)
            return pltpu.make_async_copy(w_hbm.at[part], w_ref.at[part], w_sems.at[step])

        load_cot = pltpu.make_async_copy(cot_hbm, cot_ref, sems.at[1])
        for copy in copies + [load_mats(n) for n in range(offset_count // deep)] + [load_cot]:
            copy.start()
        ext[empty] = jnp.zeros((voxels, channels), ext.dtype)
        acc[...] = jnp.zeros_like(acc)
        for copy in copies:
            copy.wait()
        saves = [pltpu.make_async_copy(ext, ext_hbm, sems.at[2])]
        saves[0].start()

        def turn(step, carry):
            load_mats(step).wait()
            mats = w_ref[pl.ds(step * deep, deep)].reshape(deep * channels, channels)
            for g in range(groups):
                lhs = jnp.concatenate(
                    [
                        gathered(table_ref, ext, step * deep + j, g * group, group)
                        for j in range(deep)
                    ],
                    axis=1,
                )
                acc[g] += jnp.dot(lhs, mats, preferred_element_type=jnp.float32)
            return carry

        lax.fori_loop(0, offset_count // deep, turn, 0)
        load_cot.wait()

        def finish(t, carry):
            pre = acc[t // group, pl.ds(pl.multiple_of((t % group) * voxels, voxels), voxels), :]
            sigma = jax.nn.sigmoid(pre)
            out_ref[t] = (ext[t].astype(jnp.float32) + pre * sigma).astype(out_ref.dtype)
            incoming = cot_ref[t].astype(jnp.float32)
            grad[t] = (incoming * sigma * (1.0 + pre * (1.0 - sigma))).astype(grad.dtype)
            return carry

        lax.fori_loop(0, tile_slots, finish, 0)
        for g in range(groups):
            part = grad[pl.ds(g * group, group)].reshape(rows, channels)
            turned_ref[:, pl.ds(g * rows, rows)] = part.astype(jnp.float32).T.astype(jnp.bfloat16)
        saves += [
            pltpu.make_async_copy(out_ref, out_hbm, sems.at[3]),
            pltpu.make_async_copy(grad, grad_hbm, sems.at[4]),
            pltpu.make_async_copy(turned_ref, turned_hbm, sems.at[5]),
        ]
        for save in saves[1:]:
            save.start()
        write_half(table_ref, half_ref[0], ext, turned_ref, half_out, scale)
        for save in saves:
            save.wait()

    flops = 3 * offset_count * tile_slots * voxels * channels * channels
    out_shape = [
        jax.ShapeDtypeStruct(tiles.shape, jnp.bfloat16),
        jax.ShapeDtypeStruct(tiles.shape, jnp.bfloat16),
        jax.ShapeDtypeStruct((channels, tile_slots * voxels), jnp.bfloat16),
        jax.ShapeDtypeStruct((empty + 1, voxels, channels), jnp.bfloat16),
        jax.ShapeDtypeStruct((offset_count, channels // 2, channels), jnp.float32),
    ]
    return pl.pallas_call(
        kernel,
        out_shape=out_shape,
        in_specs=[SMEM, SMEM, HBM] + [ANY] * directions + [HBM, HBM],
        out_specs=[HBM] * 4 + [VMEM],
        scratch_shapes=[
            pltpu.VMEM(weights.shape, jnp.bfloat16),
            pltpu.VMEM(tiles.shape, jnp.bfloat16),
        ]
        + [pltpu.VMEM(one.shape, one.dtype) for one in out_shape[:4]]
        + [
            pltpu.VMEM((groups, rows, channels), jnp.float32),
            pltpu.SemaphoreType.DMA((directions + 6,)),
            pltpu.SemaphoreType.DMA((offset_count // deep,)),
        ],
        compiler_params=pltpu.CompilerParams(vmem_limit_bytes=60 * MIB),
        cost_estimate=pl.CostEstimate(flops=flops, bytes_accessed=20 * MIB, transcendentals=0),
        name="forward_and_terms",
    )(table, half, tiles, *halos, weights, cotangent)


def weight_terms(table, half, ext, turned, offset_count, scale):
    channels = ext.shape[2]

    def kernel(table_ref, half_ref, ext_hbm, turned_hbm, out_ref, ext_ref, turned_ref, sems):
        cut = ext_ref.shape[0] // 2
        copies = [
            pltpu.make_async_copy(ext_hbm.at[pl.ds(0, cut)], ext_ref.at[pl.ds(0, cut)], sems.at[0]),
            pltpu.make_async_copy(
                ext_hbm.at[pl.ds(cut, ext_ref.shape[0] - cut)],
                ext_ref.at[pl.ds(cut, ext_ref.shape[0] - cut)],
                sems.at[1],
            ),
            pltpu.make_async_copy(turned_hbm, turned_ref, sems.at[2]),
        ]
        for copy in copies:
            copy.start()
        for copy in copies:
            copy.wait()
        write_half(table_ref, half_ref[0], ext_ref, turned_ref, out_ref, scale)

    flops = offset_count * turned.shape[1] * channels * channels
    return pl.pallas_call(
        kernel,
        out_shape=jax.ShapeDtypeStruct((offset_count, channels // 2, channels), jnp.float32),
        in_specs=[SMEM, SMEM, HBM, HBM],
        out_specs=VMEM,
        scratch_shapes=[
            pltpu.VMEM(ext.shape, ext.dtype),
            pltpu.VMEM(turned.shape, turned.dtype),
            pltpu.SemaphoreType.DMA((3,)),
        ],
        compiler_params=pltpu.CompilerParams(vmem_limit_bytes=60 * MIB),
        cost_estimate=pl.CostEstimate(flops=flops, bytes_accessed=6 * MIB, transcendentals=0),
        name="weight_terms",
    )(table, half, ext, turned)


def input_grad(table, pre_grad, weights, halo):
    tile_slots, voxels, channels = pre_grad.shape
    offset_count = weights.shape[0]
    empty = tile_slots + len(DIRECTIONS) * halo
    group = chunk_of(tile_slots, 8)
    groups = tile_slots // group
    rows = group * voxels
    unroll = chunk_of(offset_count, 3)
    bundles = len(BUNDLES)

    def kernel(table_ref, grad_hbm, w_hbm, own_ref, *refs):
        adjoints = refs[:bundles]
        even, odd, grad, w_ref, sems = refs[bundles:]
        copies = [
            pltpu.make_async_copy(grad_hbm, grad, sems.at[0]),
            pltpu.make_async_copy(w_hbm, w_ref, sems.at[1]),
        ]
        for copy in copies:
            copy.start()
        for one in (even, odd):
            one[...] = jnp.zeros_like(one)
        for copy in copies:
            copy.wait()

        def turn(step, carry):
            for j in range(unroll):
                k = step * unroll + j
                mat = w_ref[k].astype(jnp.float32).T.astype(jnp.bfloat16)
                for g in range(groups):
                    back = jnp.dot(
                        grad[pl.ds(g * group, group)].reshape(rows, channels),
                        mat,
                        preferred_element_type=jnp.float32,
                    )
                    for t in range(group):
                        slot = table_ref[k, g * group + t]
                        sums = (even, odd)[t % 2]
                        sums[slot] += back[t * voxels : (t + 1) * voxels]
            return carry

        lax.fori_loop(0, offset_count // unroll, turn, 0)

        def own(t, carry):
            own_ref[t] = even[t] + odd[t]
            return carry

        lax.fori_loop(0, tile_slots, own, 0)
        for bundle, adjoint in zip(BUNDLES, adjoints):
            for n, pair in enumerate(bundle):
                for h in range(halo):
                    slot = tile_slots + DIRECTIONS.index(pair) * halo + h
                    adjoint[n * halo + h] = (even[slot] + odd[slot]).astype(jnp.bfloat16)

    flops = 2 * offset_count * tile_slots * voxels * channels * channels
    return pl.pallas_call(
        kernel,
        out_shape=[jax.ShapeDtypeStruct(pre_grad.shape, jnp.float32)]
        + [
            jax.ShapeDtypeStruct((len(bundle) * halo, voxels, channels), jnp.bfloat16)
            for bundle in BUNDLES
        ],
        in_specs=[SMEM, HBM, HBM],
        out_specs=[VMEM] * (bundles + 1),
        scratch_shapes=[pltpu.VMEM((empty + 1, voxels, channels), jnp.float32)] * 2
        + [
            pltpu.VMEM(pre_grad.shape, jnp.bfloat16),
            pltpu.VMEM(weights.shape, jnp.bfloat16),
            pltpu.SemaphoreType.DMA((2,)),
        ],
        compiler_params=pltpu.CompilerParams(vmem_limit_bytes=60 * MIB),
        cost_estimate=pl.CostEstimate(flops=flops, bytes_accessed=12 * MIB, transcendentals=0),
        name="input_grad",
    )(table, pre_grad, weights)


def to_other_core(x):
    return lax.ppermute(x, "core", [(0, 1), (1, 0)])


def ring(first):
    chips, columns = lax.axis_size("gz"), lax.axis_size("gy")
    crossed = chips == columns

    def upright(core):
        return (core == 0 or not crossed) == first

    def move(x, by):
        pairs = []
        for z in range(chips):
            for core in range(2):
                for y in range(columns):
                    to_z, to_y = (z, (y + by) % columns) if upright(core) else ((z + by) % chips, y)
                    pairs.append(((2 * z + core) * columns + y, (2 * to_z + core) * columns + to_y))
        return lax.ppermute(x, ("gz", "core", "gy"), pairs)

    column, chip = lax.axis_index("gy"), lax.axis_index("gz")
    places = [column if upright(core) else chip for core in range(2)]
    size = columns if upright(0) else chips
    return size, jnp.where(lax.axis_index("core") == 0, *places), move


def given_out(terms, ring):
    size, place, _ = ring
    parts = []
    for s in range(size):
        blocks = [
            lax.dynamic_index_in_dim(
                one.reshape(size, one.shape[0] // size, one.shape[1]), (place + s) % size, keepdims=False
            )
            for one in terms
        ]
        parts.append(sum(blocks[1:], blocks[0]))
    return parts[0], [one.astype(jnp.bfloat16) for one in parts[1:]]


def handed(parts, ring):
    return [ring[2](one, s + 1) for s, one in enumerate(parts)]


def added(mine, arrived):
    for one in arrived:
        mine = mine + one.astype(jnp.float32)
    return mine


def fetched(piece, ring):
    return [ring[2](piece, -s) for s in range(1, ring[0])]


def in_order(piece, others, ring):
    size, place, _ = ring
    whole = jnp.zeros((size,) + piece.shape, piece.dtype)
    for s, one in enumerate([piece, *others]):
        whole = lax.dynamic_update_index_in_dim(whole, one, (place + s) % size, 0)
    return whole.reshape(size * piece.shape[0], piece.shape[1])


def together(*values):
    return lax.optimization_barrier(values)


def widen(core, own_half, other_half):
    rows, channels = own_half.shape
    turns = chunk_of(rows // 16, 3)
    step = rows // turns

    def kernel(core_ref, own_ref, other_ref, out_ref):
        mine = pl.program_id(0) // turns == core_ref[0]

        @pl.when(mine)
        def _():
            out_ref[...] = own_ref[...].astype(jnp.float32)

        @pl.when(jnp.logical_not(mine))
        def _():
            out_ref[...] = other_ref[...].astype(jnp.float32)

    half_spec = pl.BlockSpec((step, channels), lambda i: (i % turns, 0))
    return pl.pallas_call(
        kernel,
        grid=(2 * turns,),
        out_shape=jax.ShapeDtypeStruct((2 * rows, channels), jnp.float32),
        in_specs=[SMEM, half_spec, half_spec],
        out_specs=pl.BlockSpec((step, channels), lambda i: (i, 0)),
        compiler_params=pltpu.CompilerParams(vmem_limit_bytes=24 * MIB),
        name="widen",
    )(core, own_half, other_half)


def combine(lists, own, cotangent, returned):
    halo = lists.shape[1]
    tile_slots = own.shape[0]
    arrays = [array for array, _ in returned]

    def kernel(lists_ref, own_ref, cot_ref, *refs):
        out_ref, acc = refs[len(arrays) :]

        def start(t, carry):
            acc[t] = own_ref[t] + cot_ref[t].astype(jnp.float32)
            return carry

        lax.fori_loop(0, tile_slots, start, 0)
        for ref, (_, pairs) in zip(refs, returned):
            for n, pair in enumerate(pairs):
                for h in range(halo):
                    tile = lists_ref[DIRECTIONS.index(pair), h]
                    acc[tile] += ref[n * halo + h].astype(jnp.float32)

        def finish(t, carry):
            out_ref[t] = acc[t].astype(out_ref.dtype)
            return carry

        lax.fori_loop(0, tile_slots, finish, 0)

    return pl.pallas_call(
        kernel,
        out_shape=jax.ShapeDtypeStruct(own.shape, jnp.bfloat16),
        in_specs=[SMEM] + [VMEM] * (len(arrays) + 2),
        out_specs=VMEM,
        scratch_shapes=[pltpu.VMEM(own.shape, jnp.float32)],
        compiler_params=pltpu.CompilerParams(vmem_limit_bytes=60 * MIB),
        name="combine",
    )(lists, own, cotangent, *arrays)


def shards(
    features, weights, cotangent, send_lists, block_offset, block_input, block_output, block_count
):
    tiles = features[0, 0]
    incoming = cotangent[0, 0]
    lists = send_lists[0, 0]
    tile_slots, voxels, channels = tiles.shape
    directions, halo = lists.shape
    device_total = x_size() * lax.axis_size("gy")
    scale = 1.0 / math.sqrt(voxels * tile_slots * device_total)
    offset_count = weights.shape[0]
    core = lax.axis_index("core").astype(jnp.int32)[None]

    packets = pack(tiles, lists)
    table = source_table(
        block_offset[0, 0],
        block_input[0, 0].T,
        block_output[0, 0].T,
        block_count[0],
        offset_count,
        tile_slots,
        tile_slots + directions * halo,
        packets[0],
    )
    order = sorted(range(directions), key=lambda d: DIRECTIONS[d][1] == 0)
    arrived = {d: travel(packets[d], *DIRECTIONS[d]) for d in order}
    halos = [arrived[d] for d in range(directions)]
    out_features, pre_grad, turned, ext, send = forward_and_terms(
        table, 1 - core, tiles, halos, weights, incoming, scale
    )
    received = to_other_core(send)
    keep = weight_terms(table, core, ext, turned, offset_count, scale)
    levels = ring(True), ring(False)
    mine, out = given_out([keep.reshape(-1, channels), received.reshape(-1, channels)], levels[0])

    pre_grad, *out = together(pre_grad, *out)
    moved = handed(out, levels[0])
    own, low, high, low_both, high_both, behind, ahead = input_grad(table, pre_grad, weights, halo)
    low, *moved = together(low, *moved)
    low, high = travel(low, 0, 1), travel(high, 0, -1)
    low_both, high_both = travel(low_both, 0, 1), travel(high_both, 0, -1)

    mine, out = given_out([added(mine, moved)], levels[1])
    piece = added(mine, handed(out, levels[1])).astype(jnp.bfloat16)
    low, high, piece = together(low, high, piece)
    piece = in_order(piece, fetched(piece, levels[1]), levels[1])
    low_both, high_both, piece = together(low_both, high_both, piece)
    behind = jnp.concatenate([behind, low_both[:halo], high_both[:halo]])
    ahead = jnp.concatenate([ahead, low_both[halo:], high_both[halo:]])
    behind, ahead = travel(behind, 1, 0), travel(ahead, -1, 0)
    own_half = in_order(piece, fetched(piece, levels[0]), levels[0])
    behind, ahead, own_half = together(behind, ahead, own_half)
    feat_grad = combine(
        lists,
        own,
        incoming,
        [
            (low, ((0, -1),)),
            (high, ((0, 1),)),
            (behind, ((-1, 0), (-1, -1), (-1, 1))),
            (ahead, ((1, 0), (1, -1), (1, 1))),
        ],
    )
    weight_grad = widen(core, own_half, to_other_core(own_half)).reshape(weights.shape)
    return (out_features[None, None], feat_grad[None, None], weight_grad)


def solution(mesh):
    size_x, size_y = mesh.devices.shape
    split = Mesh(mesh.devices.reshape(size_x // 2, 2, size_y), ("gz", "core", "gy"))
    place = P(("gz", "core"), "gy")
    return jax.shard_map(
        shards,
        mesh=split,
        in_specs=(place, P(), place, place, place, place, place, place),
        out_specs=(place, place, P()),
        check_vma=False,
    )
```

```python
import math

import jax
import jax.numpy as jnp
from jax import lax
from jax.experimental import pallas as pl
from jax.experimental.pallas import tpu as pltpu
from jax.sharding import Mesh
from jax.sharding import PartitionSpec as P

DIRECTIONS = ((-1, -1), (-1, 0), (-1, 1), (0, -1), (0, 1), (1, -1), (1, 0), (1, 1))
BUNDLES = (
    ((0, -1),),
    ((0, 1),),
    ((-1, -1), (1, -1)),
    ((-1, 1), (1, 1)),
    ((-1, 0),),
    ((1, 0),),
)
MIB = 1024 * 1024
ANY = pl.BlockSpec(memory_space=pl.ANY)
HBM = pl.BlockSpec(memory_space=pltpu.HBM)
VMEM = pl.BlockSpec(memory_space=pltpu.VMEM)
SMEM = pl.BlockSpec(memory_space=pltpu.SMEM)


def chunk_of(size, wanted):
    return max(c for c in range(1, wanted + 1) if size % c == 0)


def x_size():
    return lax.axis_size("gz") * lax.axis_size("core")


def travel(packet, step_x, step_y):
    size_x, size_y = x_size(), lax.axis_size("gy")
    pairs = [
        (i * size_y + j, (i + step_x) * size_y + j + step_y)
        for i in range(size_x)
        for j in range(size_y)
        if 0 <= i + step_x < size_x and 0 <= j + step_y < size_y
    ]
    return lax.ppermute(packet, ("gz", "core", "gy"), pairs)


def pack(tiles, lists):
    halo = lists.shape[1]
    _, voxels, channels = tiles.shape

    def kernel(lists_ref, tiles_ref, *packets):
        for d, packet in enumerate(packets):
            for h in range(halo):
                packet[h] = tiles_ref[lists_ref[d, h]]

    return pl.pallas_call(
        kernel,
        out_shape=[jax.ShapeDtypeStruct((halo, voxels, channels), tiles.dtype)] * len(DIRECTIONS),
        in_specs=[SMEM, VMEM],
        out_specs=[VMEM] * len(DIRECTIONS),
        compiler_params=pltpu.CompilerParams(vmem_limit_bytes=16 * MIB),
        name="pack",
    )(lists, tiles)


def source_table(offsets, inputs, outputs, count, offset_count, tile_slots, empty, after):
    rows, blocks = inputs.shape

    def kernel(offsets_ref, inputs_ref, outputs_ref, count_ref, _, table_ref):
        def clear(k, carry):
            for t in range(tile_slots):
                table_ref[k, t] = empty
            return carry

        lax.fori_loop(0, offset_count, clear, 0)

        def block(n, carry):
            k = offsets_ref[n]
            for q in range(rows):
                table_ref[k, outputs_ref[q, n]] = inputs_ref[q, n]
            return carry

        lax.fori_loop(0, jnp.minimum(count_ref[0], blocks), block, 0)

    return pl.pallas_call(
        kernel,
        out_shape=jax.ShapeDtypeStruct((offset_count, tile_slots + 1), jnp.int32),
        in_specs=[SMEM] * 4 + [ANY],
        out_specs=SMEM,
        cost_estimate=pl.CostEstimate(flops=4 * 10**9, bytes_accessed=MIB, transcendentals=0),
        name="source_table",
    )(offsets, inputs, outputs, count, after)


def gathered(table_ref, ext, k, first, count):
    return jnp.concatenate([ext[table_ref[k, first + t]] for t in range(count)], axis=0)


def write_half(table_ref, late, ext, turned_ref, out_ref, scale):
    offset_count, part, _ = out_ref.shape
    tile_slots = table_ref.shape[1] - 1
    count = (offset_count + 1) // 2

    def turn(j, carry):
        k = late * (offset_count - count) + j
        terms = jnp.dot(
            turned_ref[...],
            gathered(table_ref, ext, k, 0, tile_slots),
            preferred_element_type=jnp.float32,
        )
        terms = terms.T * scale
        for b in range(2):
            place = 2 * k + b - late * offset_count

            @pl.when((place >= 0) & (place < offset_count))
            def _():
                out_ref[place] = terms[b * part : (b + 1) * part]

        return carry

    lax.fori_loop(0, count, turn, 0)


def forward_and_terms(table, half, tiles, halos, weights, cotangent, scale):
    tile_slots, voxels, channels = tiles.shape
    offset_count = weights.shape[0]
    directions, halo = len(halos), halos[0].shape[0]
    empty = tile_slots + directions * halo
    group = chunk_of(tile_slots, 8)
    groups = tile_slots // group
    rows = group * voxels
    deep = chunk_of(offset_count, 9)

    def kernel(table_ref, half_ref, tiles_ref, *refs):
        halo_refs, refs = refs[:directions], refs[directions:]
        w_hbm, cot_hbm, out_hbm, grad_hbm, turned_hbm, ext_hbm, half_out = refs[:7]
        w_ref, cot_ref, out_ref, grad, turned_ref, ext, acc, sems, w_sems = refs[7:]
        copies = [pltpu.make_async_copy(tiles_ref, ext.at[pl.ds(0, tile_slots)], sems.at[0])]
        for d, halo_ref in enumerate(halo_refs):
            place = ext.at[pl.ds(tile_slots + d * halo, halo)]
            copies.append(pltpu.make_async_copy(halo_ref, place, sems.at[d + 6]))

        def load_mats(step):
            part = pl.ds(step * deep, deep)
            return pltpu.make_async_copy(w_hbm.at[part], w_ref.at[part], w_sems.at[step])

        load_cot = pltpu.make_async_copy(cot_hbm, cot_ref, sems.at[1])
        for copy in copies + [load_mats(n) for n in range(offset_count // deep)] + [load_cot]:
            copy.start()
        ext[empty] = jnp.zeros((voxels, channels), ext.dtype)
        acc[...] = jnp.zeros_like(acc)
        for copy in copies:
            copy.wait()
        saves = [pltpu.make_async_copy(ext, ext_hbm, sems.at[2])]
        saves[0].start()

        def turn(step, carry):
            load_mats(step).wait()
            mats = w_ref[pl.ds(step * deep, deep)].reshape(deep * channels, channels)
            for g in range(groups):
                lhs = jnp.concatenate(
                    [
                        gathered(table_ref, ext, step * deep + j, g * group, group)
                        for j in range(deep)
                    ],
                    axis=1,
                )
                acc[g] += jnp.dot(lhs, mats, preferred_element_type=jnp.float32)
            return carry

        lax.fori_loop(0, offset_count // deep, turn, 0)
        load_cot.wait()

        def finish(t, carry):
            pre = acc[t // group, pl.ds(pl.multiple_of((t % group) * voxels, voxels), voxels), :]
            sigma = jax.nn.sigmoid(pre)
            out_ref[t] = (ext[t].astype(jnp.float32) + pre * sigma).astype(out_ref.dtype)
            incoming = cot_ref[t].astype(jnp.float32)
            grad[t] = (incoming * sigma * (1.0 + pre * (1.0 - sigma))).astype(grad.dtype)
            return carry

        lax.fori_loop(0, tile_slots, finish, 0)
        for g in range(groups):
            part = grad[pl.ds(g * group, group)].reshape(rows, channels)
            turned_ref[:, pl.ds(g * rows, rows)] = part.astype(jnp.float32).T.astype(jnp.bfloat16)
        saves += [
            pltpu.make_async_copy(out_ref, out_hbm, sems.at[3]),
            pltpu.make_async_copy(grad, grad_hbm, sems.at[4]),
            pltpu.make_async_copy(turned_ref, turned_hbm, sems.at[5]),
        ]
        for save in saves[1:]:
            save.start()
        write_half(table_ref, half_ref[0], ext, turned_ref, half_out, scale)
        for save in saves:
            save.wait()

    flops = 3 * offset_count * tile_slots * voxels * channels * channels
    out_shape = [
        jax.ShapeDtypeStruct(tiles.shape, jnp.bfloat16),
        jax.ShapeDtypeStruct(tiles.shape, jnp.bfloat16),
        jax.ShapeDtypeStruct((channels, tile_slots * voxels), jnp.bfloat16),
        jax.ShapeDtypeStruct((empty + 1, voxels, channels), jnp.bfloat16),
        jax.ShapeDtypeStruct((offset_count, channels // 2, channels), jnp.float32),
    ]
    return pl.pallas_call(
        kernel,
        out_shape=out_shape,
        in_specs=[SMEM, SMEM, HBM] + [ANY] * directions + [HBM, HBM],
        out_specs=[HBM] * 4 + [VMEM],
        scratch_shapes=[
            pltpu.VMEM(weights.shape, jnp.bfloat16),
            pltpu.VMEM(tiles.shape, jnp.bfloat16),
        ]
        + [pltpu.VMEM(one.shape, one.dtype) for one in out_shape[:4]]
        + [
            pltpu.VMEM((groups, rows, channels), jnp.float32),
            pltpu.SemaphoreType.DMA((directions + 6,)),
            pltpu.SemaphoreType.DMA((offset_count // deep,)),
        ],
        compiler_params=pltpu.CompilerParams(vmem_limit_bytes=60 * MIB),
        cost_estimate=pl.CostEstimate(flops=flops, bytes_accessed=20 * MIB, transcendentals=0),
        name="forward_and_terms",
    )(table, half, tiles, *halos, weights, cotangent)


def weight_terms(table, half, ext, turned, offset_count, scale):
    channels = ext.shape[2]

    def kernel(table_ref, half_ref, ext_hbm, turned_hbm, out_ref, ext_ref, turned_ref, sems):
        cut = ext_ref.shape[0] // 2
        copies = [
            pltpu.make_async_copy(ext_hbm.at[pl.ds(0, cut)], ext_ref.at[pl.ds(0, cut)], sems.at[0]),
            pltpu.make_async_copy(
                ext_hbm.at[pl.ds(cut, ext_ref.shape[0] - cut)],
                ext_ref.at[pl.ds(cut, ext_ref.shape[0] - cut)],
                sems.at[1],
            ),
            pltpu.make_async_copy(turned_hbm, turned_ref, sems.at[2]),
        ]
        for copy in copies:
            copy.start()
        for copy in copies:
            copy.wait()
        write_half(table_ref, half_ref[0], ext_ref, turned_ref, out_ref, scale)

    flops = offset_count * turned.shape[1] * channels * channels
    return pl.pallas_call(
        kernel,
        out_shape=jax.ShapeDtypeStruct((offset_count, channels // 2, channels), jnp.float32),
        in_specs=[SMEM, SMEM, HBM, HBM],
        out_specs=VMEM,
        scratch_shapes=[
            pltpu.VMEM(ext.shape, ext.dtype),
            pltpu.VMEM(turned.shape, turned.dtype),
            pltpu.SemaphoreType.DMA((3,)),
        ],
        compiler_params=pltpu.CompilerParams(vmem_limit_bytes=60 * MIB),
        cost_estimate=pl.CostEstimate(flops=flops, bytes_accessed=6 * MIB, transcendentals=0),
        name="weight_terms",
    )(table, half, ext, turned)


def input_grad(table, pre_grad, weights, halo):
    tile_slots, voxels, channels = pre_grad.shape
    offset_count = weights.shape[0]
    empty = tile_slots + len(DIRECTIONS) * halo
    group = chunk_of(tile_slots, 8)
    groups = tile_slots // group
    rows = group * voxels
    unroll = chunk_of(offset_count, 3)
    bundles = len(BUNDLES)

    def kernel(table_ref, grad_hbm, w_hbm, own_ref, *refs):
        adjoints = refs[:bundles]
        even, odd, grad, w_ref, sems = refs[bundles:]
        copies = [
            pltpu.make_async_copy(grad_hbm, grad, sems.at[0]),
            pltpu.make_async_copy(w_hbm, w_ref, sems.at[1]),
        ]
        for copy in copies:
            copy.start()
        for one in (even, odd):
            one[...] = jnp.zeros_like(one)
        for copy in copies:
            copy.wait()

        def turn(step, carry):
            for j in range(unroll):
                k = step * unroll + j
                mat = w_ref[k].astype(jnp.float32).T.astype(jnp.bfloat16)
                for g in range(groups):
                    back = jnp.dot(
                        grad[pl.ds(g * group, group)].reshape(rows, channels),
                        mat,
                        preferred_element_type=jnp.float32,
                    )
                    for t in range(group):
                        slot = table_ref[k, g * group + t]
                        sums = (even, odd)[t % 2]
                        sums[slot] += back[t * voxels : (t + 1) * voxels]
            return carry

        lax.fori_loop(0, offset_count // unroll, turn, 0)

        def own(t, carry):
            own_ref[t] = even[t] + odd[t]
            return carry

        lax.fori_loop(0, tile_slots, own, 0)
        for bundle, adjoint in zip(BUNDLES, adjoints):
            for n, pair in enumerate(bundle):
                for h in range(halo):
                    slot = tile_slots + DIRECTIONS.index(pair) * halo + h
                    adjoint[n * halo + h] = (even[slot] + odd[slot]).astype(jnp.bfloat16)

    flops = 2 * offset_count * tile_slots * voxels * channels * channels
    return pl.pallas_call(
        kernel,
        out_shape=[jax.ShapeDtypeStruct(pre_grad.shape, jnp.float32)]
        + [
            jax.ShapeDtypeStruct((len(bundle) * halo, voxels, channels), jnp.bfloat16)
            for bundle in BUNDLES
        ],
        in_specs=[SMEM, HBM, HBM],
        out_specs=[VMEM] * (bundles + 1),
        scratch_shapes=[pltpu.VMEM((empty + 1, voxels, channels), jnp.float32)] * 2
        + [
            pltpu.VMEM(pre_grad.shape, jnp.bfloat16),
            pltpu.VMEM(weights.shape, jnp.bfloat16),
            pltpu.SemaphoreType.DMA((2,)),
        ],
        compiler_params=pltpu.CompilerParams(vmem_limit_bytes=60 * MIB),
        cost_estimate=pl.CostEstimate(flops=flops, bytes_accessed=12 * MIB, transcendentals=0),
        name="input_grad",
    )(table, pre_grad, weights)


def to_other_core(x):
    return lax.ppermute(x, "core", [(0, 1), (1, 0)])


def ring(first):
    chips, columns = lax.axis_size("gz"), lax.axis_size("gy")
    crossed = chips == columns

    def upright(core):
        return (core == 0 or not crossed) == first

    def move(x, by):
        pairs = []
        for z in range(chips):
            for core in range(2):
                for y in range(columns):
                    to_z, to_y = (z, (y + by) % columns) if upright(core) else ((z + by) % chips, y)
                    pairs.append(((2 * z + core) * columns + y, (2 * to_z + core) * columns + to_y))
        return lax.ppermute(x, ("gz", "core", "gy"), pairs)

    column, chip = lax.axis_index("gy"), lax.axis_index("gz")
    places = [column if upright(core) else chip for core in range(2)]
    size = columns if upright(0) else chips
    return size, jnp.where(lax.axis_index("core") == 0, *places), move


def given_out(terms, ring):
    size, place, _ = ring
    parts = []
    for s in range(size):
        blocks = [
            lax.dynamic_index_in_dim(
                one.reshape(size, one.shape[0] // size, one.shape[1]), (place + s) % size, keepdims=False
            )
            for one in terms
        ]
        parts.append(sum(blocks[1:], blocks[0]))
    return parts[0], [one.astype(jnp.bfloat16) for one in parts[1:]]


def handed(parts, ring):
    return [ring[2](one, s + 1) for s, one in enumerate(parts)]


def added(mine, arrived):
    for one in arrived:
        mine = mine + one.astype(jnp.float32)
    return mine


def fetched(piece, ring):
    return [ring[2](piece, -s) for s in range(1, ring[0])]


def in_order(piece, others, ring):
    size, place, _ = ring
    whole = jnp.zeros((size,) + piece.shape, piece.dtype)
    for s, one in enumerate([piece, *others]):
        whole = lax.dynamic_update_index_in_dim(whole, one, (place + s) % size, 0)
    return whole.reshape(size * piece.shape[0], piece.shape[1])


def together(*values):
    return lax.optimization_barrier(values)


def widen(core, own_half, other_half):
    rows, channels = own_half.shape
    turns = chunk_of(rows // 16, 3)
    step = rows // turns

    def kernel(core_ref, own_ref, other_ref, out_ref):
        mine = pl.program_id(0) // turns == core_ref[0]

        @pl.when(mine)
        def _():
            out_ref[...] = own_ref[...].astype(jnp.float32)

        @pl.when(jnp.logical_not(mine))
        def _():
            out_ref[...] = other_ref[...].astype(jnp.float32)

    half_spec = pl.BlockSpec((step, channels), lambda i: (i % turns, 0))
    return pl.pallas_call(
        kernel,
        grid=(2 * turns,),
        out_shape=jax.ShapeDtypeStruct((2 * rows, channels), jnp.float32),
        in_specs=[SMEM, half_spec, half_spec],
        out_specs=pl.BlockSpec((step, channels), lambda i: (i, 0)),
        compiler_params=pltpu.CompilerParams(vmem_limit_bytes=24 * MIB),
        name="widen",
    )(core, own_half, other_half)


def combine(lists, own, cotangent, returned):
    halo = lists.shape[1]
    tile_slots = own.shape[0]
    arrays = [array for array, _ in returned]

    def kernel(lists_ref, own_ref, cot_ref, *refs):
        out_ref, acc = refs[len(arrays) :]

        def start(t, carry):
            acc[t] = own_ref[t] + cot_ref[t].astype(jnp.float32)
            return carry

        lax.fori_loop(0, tile_slots, start, 0)
        for ref, (_, pairs) in zip(refs, returned):
            for n, pair in enumerate(pairs):
                for h in range(halo):
                    tile = lists_ref[DIRECTIONS.index(pair), h]
                    acc[tile] += ref[n * halo + h].astype(jnp.float32)

        def finish(t, carry):
            out_ref[t] = acc[t].astype(out_ref.dtype)
            return carry

        lax.fori_loop(0, tile_slots, finish, 0)

    return pl.pallas_call(
        kernel,
        out_shape=jax.ShapeDtypeStruct(own.shape, jnp.bfloat16),
        in_specs=[SMEM] + [VMEM] * (len(arrays) + 2),
        out_specs=VMEM,
        scratch_shapes=[pltpu.VMEM(own.shape, jnp.float32)],
        compiler_params=pltpu.CompilerParams(vmem_limit_bytes=60 * MIB),
        name="combine",
    )(lists, own, cotangent, *arrays)


def shards(
    features, weights, cotangent, send_lists, block_offset, block_input, block_output, block_count
):
    tiles = features[0, 0]
    incoming = cotangent[0, 0]
    lists = send_lists[0, 0]
    tile_slots, voxels, channels = tiles.shape
    directions, halo = lists.shape
    device_total = x_size() * lax.axis_size("gy")
    scale = 1.0 / math.sqrt(voxels * tile_slots * device_total)
    offset_count = weights.shape[0]
    core = lax.axis_index("core").astype(jnp.int32)[None]

    packets = pack(tiles, lists)
    table = source_table(
        block_offset[0, 0],
        block_input[0, 0].T,
        block_output[0, 0].T,
        block_count[0],
        offset_count,
        tile_slots,
        tile_slots + directions * halo,
        packets[0],
    )
    order = sorted(range(directions), key=lambda d: DIRECTIONS[d][1] == 0)
    arrived = {d: travel(packets[d], *DIRECTIONS[d]) for d in order}
    halos = [arrived[d] for d in range(directions)]
    out_features, pre_grad, turned, ext, send = forward_and_terms(
        table, 1 - core, tiles, halos, weights, incoming, scale
    )
    received = to_other_core(send)
    keep = weight_terms(table, core, ext, turned, offset_count, scale)
    levels = ring(True), ring(False)
    mine, out = given_out([keep.reshape(-1, channels), received.reshape(-1, channels)], levels[0])

    pre_grad, *out = together(pre_grad, *out)
    moved = handed(out, levels[0])
    own, low, high, low_both, high_both, behind, ahead = input_grad(table, pre_grad, weights, halo)
    low, *moved = together(low, *moved)
    low, high = travel(low, 0, 1), travel(high, 0, -1)
    low_both, high_both = travel(low_both, 0, 1), travel(high_both, 0, -1)

    mine, out = given_out([added(mine, moved)], levels[1])
    piece = added(mine, handed(out, levels[1])).astype(jnp.bfloat16)
    low, high, piece = together(low, high, piece)
    piece = in_order(piece, fetched(piece, levels[1]), levels[1])
    others = fetched(piece, levels[0])
    low_both, high_both, *others = together(low_both, high_both, *others)
    own_half = in_order(piece, others, levels[0])
    behind = jnp.concatenate([behind, low_both[:halo], high_both[:halo]])
    ahead = jnp.concatenate([ahead, low_both[halo:], high_both[halo:]])
    behind, ahead = travel(behind, 1, 0), travel(ahead, -1, 0)
    weight_grad = widen(core, own_half, to_other_core(own_half)).reshape(weights.shape)
    behind, ahead, weight_grad = together(behind, ahead, weight_grad)
    feat_grad = combine(
        lists,
        own,
        incoming,
        [
            (low, ((0, -1),)),
            (high, ((0, 1),)),
            (behind, ((-1, 0), (-1, -1), (-1, 1))),
            (ahead, ((1, 0), (1, -1), (1, 1))),
        ],
    )
    return (out_features[None, None], feat_grad[None, None], weight_grad)


def solution(mesh):
    size_x, size_y = mesh.devices.shape
    split = Mesh(mesh.devices.reshape(size_x // 2, 2, size_y), ("gz", "core", "gy"))
    place = P(("gz", "core"), "gy")
    return jax.shard_map(
        shards,
        mesh=split,
        in_specs=(place, P(), place, place, place, place, place, place),
        out_specs=(place, place, P()),
        check_vma=False,
    )
```

```python
import math

import jax
import jax.numpy as jnp
from jax import lax
from jax.experimental import pallas as pl
from jax.experimental.pallas import tpu as pltpu
from jax.sharding import Mesh
from jax.sharding import PartitionSpec as P

DIRECTIONS = ((-1, -1), (-1, 0), (-1, 1), (0, -1), (0, 1), (1, -1), (1, 0), (1, 1))
BUNDLES = (
    ((0, -1),),
    ((0, 1),),
    ((-1, -1), (1, -1)),
    ((-1, 1), (1, 1)),
    ((-1, 0),),
    ((1, 0),),
)
MIB = 1024 * 1024
ANY = pl.BlockSpec(memory_space=pl.ANY)
HBM = pl.BlockSpec(memory_space=pltpu.HBM)
VMEM = pl.BlockSpec(memory_space=pltpu.VMEM)
SMEM = pl.BlockSpec(memory_space=pltpu.SMEM)


def chunk_of(size, wanted):
    return max(c for c in range(1, wanted + 1) if size % c == 0)


def x_size():
    return lax.axis_size("gz") * lax.axis_size("core")


def travel(packet, step_x, step_y):
    size_x, size_y = x_size(), lax.axis_size("gy")
    pairs = [
        (i * size_y + j, (i + step_x) * size_y + j + step_y)
        for i in range(size_x)
        for j in range(size_y)
        if 0 <= i + step_x < size_x and 0 <= j + step_y < size_y
    ]
    return lax.ppermute(packet, ("gz", "core", "gy"), pairs)


def pack(tiles, lists):
    halo = lists.shape[1]
    _, voxels, channels = tiles.shape

    def kernel(lists_ref, tiles_ref, *packets):
        for d, packet in enumerate(packets):
            for h in range(halo):
                packet[h] = tiles_ref[lists_ref[d, h]]

    return pl.pallas_call(
        kernel,
        out_shape=[jax.ShapeDtypeStruct((halo, voxels, channels), tiles.dtype)] * len(DIRECTIONS),
        in_specs=[SMEM, VMEM],
        out_specs=[VMEM] * len(DIRECTIONS),
        compiler_params=pltpu.CompilerParams(vmem_limit_bytes=16 * MIB),
        name="pack",
    )(lists, tiles)


def source_table(offsets, inputs, outputs, count, offset_count, tile_slots, empty, after):
    rows, blocks = inputs.shape

    def kernel(offsets_ref, inputs_ref, outputs_ref, count_ref, _, table_ref):
        def clear(k, carry):
            for t in range(tile_slots):
                table_ref[k, t] = empty
            return carry

        lax.fori_loop(0, offset_count, clear, 0)

        def block(n, carry):
            k = offsets_ref[n]
            for q in range(rows):
                table_ref[k, outputs_ref[q, n]] = inputs_ref[q, n]
            return carry

        lax.fori_loop(0, jnp.minimum(count_ref[0], blocks), block, 0)

    return pl.pallas_call(
        kernel,
        out_shape=jax.ShapeDtypeStruct((offset_count, tile_slots + 1), jnp.int32),
        in_specs=[SMEM] * 4 + [ANY],
        out_specs=SMEM,
        cost_estimate=pl.CostEstimate(flops=4 * 10**9, bytes_accessed=MIB, transcendentals=0),
        name="source_table",
    )(offsets, inputs, outputs, count, after)


def gathered(table_ref, ext, k, first, count):
    return jnp.concatenate([ext[table_ref[k, first + t]] for t in range(count)], axis=0)


def write_half(table_ref, late, ext, turned_ref, out_ref, scale):
    offset_count, part, _ = out_ref.shape
    tile_slots = table_ref.shape[1] - 1
    count = (offset_count + 1) // 2

    def turn(j, carry):
        k = late * (offset_count - count) + j
        terms = jnp.dot(
            turned_ref[...],
            gathered(table_ref, ext, k, 0, tile_slots),
            preferred_element_type=jnp.float32,
        )
        terms = terms.T * scale
        for b in range(2):
            place = 2 * k + b - late * offset_count

            @pl.when((place >= 0) & (place < offset_count))
            def _():
                out_ref[place] = terms[b * part : (b + 1) * part]

        return carry

    lax.fori_loop(0, count, turn, 0)


def forward_and_terms(table, half, tiles, halos, weights, cotangent, scale):
    tile_slots, voxels, channels = tiles.shape
    offset_count = weights.shape[0]
    directions, halo = len(halos), halos[0].shape[0]
    empty = tile_slots + directions * halo
    group = chunk_of(tile_slots, 8)
    groups = tile_slots // group
    rows = group * voxels
    deep = chunk_of(offset_count, 9)

    def kernel(table_ref, half_ref, tiles_ref, *refs):
        halo_refs, refs = refs[:directions], refs[directions:]
        w_hbm, cot_hbm, out_hbm, grad_hbm, turned_hbm, ext_hbm, half_out = refs[:7]
        w_ref, cot_ref, out_ref, grad, turned_ref, ext, acc, sems, w_sems = refs[7:]
        copies = [pltpu.make_async_copy(tiles_ref, ext.at[pl.ds(0, tile_slots)], sems.at[0])]
        for d, halo_ref in enumerate(halo_refs):
            place = ext.at[pl.ds(tile_slots + d * halo, halo)]
            copies.append(pltpu.make_async_copy(halo_ref, place, sems.at[d + 6]))

        def load_mats(step):
            part = pl.ds(step * deep, deep)
            return pltpu.make_async_copy(w_hbm.at[part], w_ref.at[part], w_sems.at[step])

        load_cot = pltpu.make_async_copy(cot_hbm, cot_ref, sems.at[1])
        for copy in copies + [load_mats(n) for n in range(offset_count // deep)] + [load_cot]:
            copy.start()
        ext[empty] = jnp.zeros((voxels, channels), ext.dtype)
        acc[...] = jnp.zeros_like(acc)
        for copy in copies:
            copy.wait()
        saves = [pltpu.make_async_copy(ext, ext_hbm, sems.at[2])]
        saves[0].start()

        def turn(step, carry):
            load_mats(step).wait()
            mats = w_ref[pl.ds(step * deep, deep)].reshape(deep * channels, channels)
            for g in range(groups):
                lhs = jnp.concatenate(
                    [
                        gathered(table_ref, ext, step * deep + j, g * group, group)
                        for j in range(deep)
                    ],
                    axis=1,
                )
                acc[g] += jnp.dot(lhs, mats, preferred_element_type=jnp.float32)
            return carry

        lax.fori_loop(0, offset_count // deep, turn, 0)
        load_cot.wait()

        def finish(t, carry):
            pre = acc[t // group, pl.ds(pl.multiple_of((t % group) * voxels, voxels), voxels), :]
            sigma = jax.nn.sigmoid(pre)
            out_ref[t] = (ext[t].astype(jnp.float32) + pre * sigma).astype(out_ref.dtype)
            incoming = cot_ref[t].astype(jnp.float32)
            grad[t] = (incoming * sigma * (1.0 + pre * (1.0 - sigma))).astype(grad.dtype)
            return carry

        lax.fori_loop(0, tile_slots, finish, 0)
        for g in range(groups):
            part = grad[pl.ds(g * group, group)].reshape(rows, channels)
            turned_ref[:, pl.ds(g * rows, rows)] = part.astype(jnp.float32).T.astype(jnp.bfloat16)
        saves += [
            pltpu.make_async_copy(out_ref, out_hbm, sems.at[3]),
            pltpu.make_async_copy(grad, grad_hbm, sems.at[4]),
            pltpu.make_async_copy(turned_ref, turned_hbm, sems.at[5]),
        ]
        for save in saves[1:]:
            save.start()
        write_half(table_ref, half_ref[0], ext, turned_ref, half_out, scale)
        for save in saves:
            save.wait()

    flops = 3 * offset_count * tile_slots * voxels * channels * channels
    out_shape = [
        jax.ShapeDtypeStruct(tiles.shape, jnp.bfloat16),
        jax.ShapeDtypeStruct(tiles.shape, jnp.bfloat16),
        jax.ShapeDtypeStruct((channels, tile_slots * voxels), jnp.bfloat16),
        jax.ShapeDtypeStruct((empty + 1, voxels, channels), jnp.bfloat16),
        jax.ShapeDtypeStruct((offset_count, channels // 2, channels), jnp.float32),
    ]
    return pl.pallas_call(
        kernel,
        out_shape=out_shape,
        in_specs=[SMEM, SMEM, HBM] + [ANY] * directions + [HBM, HBM],
        out_specs=[HBM] * 4 + [VMEM],
        scratch_shapes=[
            pltpu.VMEM(weights.shape, jnp.bfloat16),
            pltpu.VMEM(tiles.shape, jnp.bfloat16),
        ]
        + [pltpu.VMEM(one.shape, one.dtype) for one in out_shape[:4]]
        + [
            pltpu.VMEM((groups, rows, channels), jnp.float32),
            pltpu.SemaphoreType.DMA((directions + 6,)),
            pltpu.SemaphoreType.DMA((offset_count // deep,)),
        ],
        compiler_params=pltpu.CompilerParams(vmem_limit_bytes=60 * MIB),
        cost_estimate=pl.CostEstimate(flops=flops, bytes_accessed=20 * MIB, transcendentals=0),
        name="forward_and_terms",
    )(table, half, tiles, *halos, weights, cotangent)


def weight_terms(table, half, ext, turned, offset_count, scale):
    channels = ext.shape[2]

    def kernel(table_ref, half_ref, ext_hbm, turned_hbm, out_ref, ext_ref, turned_ref, sems):
        cut = ext_ref.shape[0] // 2
        copies = [
            pltpu.make_async_copy(ext_hbm.at[pl.ds(0, cut)], ext_ref.at[pl.ds(0, cut)], sems.at[0]),
            pltpu.make_async_copy(
                ext_hbm.at[pl.ds(cut, ext_ref.shape[0] - cut)],
                ext_ref.at[pl.ds(cut, ext_ref.shape[0] - cut)],
                sems.at[1],
            ),
            pltpu.make_async_copy(turned_hbm, turned_ref, sems.at[2]),
        ]
        for copy in copies:
            copy.start()
        for copy in copies:
            copy.wait()
        write_half(table_ref, half_ref[0], ext_ref, turned_ref, out_ref, scale)

    flops = offset_count * turned.shape[1] * channels * channels
    return pl.pallas_call(
        kernel,
        out_shape=jax.ShapeDtypeStruct((offset_count, channels // 2, channels), jnp.float32),
        in_specs=[SMEM, SMEM, HBM, HBM],
        out_specs=VMEM,
        scratch_shapes=[
            pltpu.VMEM(ext.shape, ext.dtype),
            pltpu.VMEM(turned.shape, turned.dtype),
            pltpu.SemaphoreType.DMA((3,)),
        ],
        compiler_params=pltpu.CompilerParams(vmem_limit_bytes=60 * MIB),
        cost_estimate=pl.CostEstimate(flops=flops, bytes_accessed=6 * MIB, transcendentals=0),
        name="weight_terms",
    )(table, half, ext, turned)


def input_grad(table, pre_grad, weights, halo):
    tile_slots, voxels, channels = pre_grad.shape
    offset_count = weights.shape[0]
    empty = tile_slots + len(DIRECTIONS) * halo
    group = chunk_of(tile_slots, 8)
    groups = tile_slots // group
    rows = group * voxels
    unroll = chunk_of(offset_count, 3)
    bundles = len(BUNDLES)

    def kernel(table_ref, grad_hbm, w_hbm, own_ref, *refs):
        adjoints = refs[:bundles]
        even, odd, grad, w_ref, sems = refs[bundles:]
        copies = [
            pltpu.make_async_copy(grad_hbm, grad, sems.at[0]),
            pltpu.make_async_copy(w_hbm, w_ref, sems.at[1]),
        ]
        for copy in copies:
            copy.start()
        for one in (even, odd):
            one[...] = jnp.zeros_like(one)
        for copy in copies:
            copy.wait()

        def turn(step, carry):
            for j in range(unroll):
                k = step * unroll + j
                mat = w_ref[k].astype(jnp.float32).T.astype(jnp.bfloat16)
                for g in range(groups):
                    back = jnp.dot(
                        grad[pl.ds(g * group, group)].reshape(rows, channels),
                        mat,
                        preferred_element_type=jnp.float32,
                    )
                    for t in range(group):
                        slot = table_ref[k, g * group + t]
                        sums = (even, odd)[t % 2]
                        sums[slot] += back[t * voxels : (t + 1) * voxels]
            return carry

        lax.fori_loop(0, offset_count // unroll, turn, 0)

        def own(t, carry):
            own_ref[t] = even[t] + odd[t]
            return carry

        lax.fori_loop(0, tile_slots, own, 0)
        for bundle, adjoint in zip(BUNDLES, adjoints):
            for n, pair in enumerate(bundle):
                for h in range(halo):
                    slot = tile_slots + DIRECTIONS.index(pair) * halo + h
                    adjoint[n * halo + h] = (even[slot] + odd[slot]).astype(jnp.bfloat16)

    flops = 2 * offset_count * tile_slots * voxels * channels * channels
    return pl.pallas_call(
        kernel,
        out_shape=[jax.ShapeDtypeStruct(pre_grad.shape, jnp.float32)]
        + [
            jax.ShapeDtypeStruct((len(bundle) * halo, voxels, channels), jnp.bfloat16)
            for bundle in BUNDLES
        ],
        in_specs=[SMEM, HBM, HBM],
        out_specs=[VMEM] * (bundles + 1),
        scratch_shapes=[pltpu.VMEM((empty + 1, voxels, channels), jnp.float32)] * 2
        + [
            pltpu.VMEM(pre_grad.shape, jnp.bfloat16),
            pltpu.VMEM(weights.shape, jnp.bfloat16),
            pltpu.SemaphoreType.DMA((2,)),
        ],
        compiler_params=pltpu.CompilerParams(vmem_limit_bytes=60 * MIB),
        cost_estimate=pl.CostEstimate(flops=flops, bytes_accessed=12 * MIB, transcendentals=0),
        name="input_grad",
    )(table, pre_grad, weights)


def to_other_core(x):
    return lax.ppermute(x, "core", [(0, 1), (1, 0)])


def ring(axis):
    size = lax.axis_size(axis)

    def move(x, by):
        return lax.ppermute(x, axis, [(i, (i + by) % size) for i in range(size)])

    return size, lax.axis_index(axis), move


def given_out(terms, ring):
    size, place, _ = ring
    parts = []
    for s in range(size):
        blocks = [
            lax.dynamic_index_in_dim(
                one.reshape(size, one.shape[0] // size, one.shape[1]), (place + s) % size, keepdims=False
            )
            for one in terms
        ]
        parts.append(sum(blocks[1:], blocks[0]))
    return parts[0], [one.astype(jnp.bfloat16) for one in parts[1:]]


def handed(parts, ring):
    return [ring[2](one, s + 1) for s, one in enumerate(parts)]


def added(mine, arrived):
    for one in arrived:
        mine = mine + one.astype(jnp.float32)
    return mine


def fetched(piece, ring):
    return [ring[2](piece, -s) for s in range(1, ring[0])]


def in_order(piece, others, ring):
    size, place, _ = ring
    whole = jnp.zeros((size,) + piece.shape, piece.dtype)
    for s, one in enumerate([piece, *others]):
        whole = lax.dynamic_update_index_in_dim(whole, one, (place + s) % size, 0)
    return whole.reshape(size * piece.shape[0], piece.shape[1])


def together(*values):
    return lax.optimization_barrier(values)


def widen(core, own_half, other_half):
    rows, channels = own_half.shape
    turns = chunk_of(rows // 16, 3)
    step = rows // turns

    def kernel(core_ref, own_ref, other_ref, out_ref):
        mine = pl.program_id(0) // turns == core_ref[0]

        @pl.when(mine)
        def _():
            out_ref[...] = own_ref[...].astype(jnp.float32)

        @pl.when(jnp.logical_not(mine))
        def _():
            out_ref[...] = other_ref[...].astype(jnp.float32)

    half_spec = pl.BlockSpec((step, channels), lambda i: (i % turns, 0))
    return pl.pallas_call(
        kernel,
        grid=(2 * turns,),
        out_shape=jax.ShapeDtypeStruct((2 * rows, channels), jnp.float32),
        in_specs=[SMEM, half_spec, half_spec],
        out_specs=pl.BlockSpec((step, channels), lambda i: (i, 0)),
        compiler_params=pltpu.CompilerParams(vmem_limit_bytes=24 * MIB),
        name="widen",
    )(core, own_half, other_half)


def combine(lists, own, cotangent, returned):
    halo = lists.shape[1]
    tile_slots = own.shape[0]
    arrays = [array for array, _ in returned]

    def kernel(lists_ref, own_ref, cot_ref, *refs):
        out_ref, acc = refs[len(arrays) :]

        def start(t, carry):
            acc[t] = own_ref[t] + cot_ref[t].astype(jnp.float32)
            return carry

        lax.fori_loop(0, tile_slots, start, 0)
        for ref, (_, pairs) in zip(refs, returned):
            for n, pair in enumerate(pairs):
                for h in range(halo):
                    tile = lists_ref[DIRECTIONS.index(pair), h]
                    acc[tile] += ref[n * halo + h].astype(jnp.float32)

        def finish(t, carry):
            out_ref[t] = acc[t].astype(out_ref.dtype)
            return carry

        lax.fori_loop(0, tile_slots, finish, 0)

    return pl.pallas_call(
        kernel,
        out_shape=jax.ShapeDtypeStruct(own.shape, jnp.bfloat16),
        in_specs=[SMEM] + [VMEM] * (len(arrays) + 2),
        out_specs=VMEM,
        scratch_shapes=[pltpu.VMEM(own.shape, jnp.float32)],
        compiler_params=pltpu.CompilerParams(vmem_limit_bytes=60 * MIB),
        name="combine",
    )(lists, own, cotangent, *arrays)


def shards(
    features, weights, cotangent, send_lists, block_offset, block_input, block_output, block_count
):
    tiles = features[0, 0]
    incoming = cotangent[0, 0]
    lists = send_lists[0, 0]
    tile_slots, voxels, channels = tiles.shape
    directions, halo = lists.shape
    device_total = x_size() * lax.axis_size("gy")
    scale = 1.0 / math.sqrt(voxels * tile_slots * device_total)
    offset_count = weights.shape[0]
    core = lax.axis_index("core").astype(jnp.int32)[None]

    packets = pack(tiles, lists)
    table = source_table(
        block_offset[0, 0],
        block_input[0, 0].T,
        block_output[0, 0].T,
        block_count[0],
        offset_count,
        tile_slots,
        tile_slots + directions * halo,
        packets[0],
    )
    order = sorted(range(directions), key=lambda d: DIRECTIONS[d][1] == 0)
    arrived = {d: travel(packets[d], *DIRECTIONS[d]) for d in order}
    halos = [arrived[d] for d in range(directions)]
    out_features, pre_grad, turned, ext, send = forward_and_terms(
        table, 1 - core, tiles, halos, weights, incoming, scale
    )
    received = to_other_core(send)
    keep = weight_terms(table, core, ext, turned, offset_count, scale)
    levels = ring("gy"), ring("gz")
    mine, out = given_out([keep.reshape(-1, channels), received.reshape(-1, channels)], levels[0])

    pre_grad, *out = together(pre_grad, *out)
    moved = handed(out, levels[0])
    own, low, high, low_both, high_both, behind, ahead = input_grad(table, pre_grad, weights, halo)
    low, *moved = together(low, *moved)
    low, high = travel(low, 0, 1), travel(high, 0, -1)
    low_both, high_both = travel(low_both, 0, 1), travel(high_both, 0, -1)

    mine, out = given_out([added(mine, moved)], levels[1])
    piece = added(mine, handed(out, levels[1])).astype(jnp.bfloat16)
    low, high, piece = together(low, high, piece)
    piece = in_order(piece, fetched(piece, levels[1]), levels[1])
    low_both, high_both, piece = together(low_both, high_both, piece)
    behind = jnp.concatenate([behind, low_both[:halo], high_both[:halo]])
    ahead = jnp.concatenate([ahead, low_both[halo:], high_both[halo:]])
    behind, ahead = travel(behind, 1, 0), travel(ahead, -1, 0)
    own_half = in_order(piece, fetched(piece, levels[0]), levels[0])
    behind, ahead, own_half = together(behind, ahead, own_half)
    feat_grad = combine(
        lists,
        own,
        incoming,
        [
            (low, ((0, -1),)),
            (high, ((0, 1),)),
            (behind, ((-1, 0), (-1, -1), (-1, 1))),
            (ahead, ((1, 0), (1, -1), (1, 1))),
        ],
    )
    weight_grad = widen(core, own_half, to_other_core(own_half)).reshape(weights.shape)
    return (out_features[None, None], feat_grad[None, None], weight_grad)


def solution(mesh):
    size_x, size_y = mesh.devices.shape
    split = Mesh(mesh.devices.reshape(size_x // 2, 2, size_y), ("gz", "core", "gy"))
    place = P(("gz", "core"), "gy")
    return jax.shard_map(
        shards,
        mesh=split,
        in_specs=(place, P(), place, place, place, place, place, place),
        out_specs=(place, place, P()),
        check_vma=False,
    )
```

```python
import math

import jax
import jax.numpy as jnp
from jax import lax
from jax.experimental import pallas as pl
from jax.experimental.pallas import tpu as pltpu
from jax.sharding import Mesh
from jax.sharding import PartitionSpec as P

DIRECTIONS = ((-1, -1), (-1, 0), (-1, 1), (0, -1), (0, 1), (1, -1), (1, 0), (1, 1))
BUNDLES = (
    ((0, -1),),
    ((0, 1),),
    ((-1, -1), (1, -1)),
    ((-1, 1), (1, 1)),
    ((-1, 0),),
    ((1, 0),),
)
MIB = 1024 * 1024
ANY = pl.BlockSpec(memory_space=pl.ANY)
HBM = pl.BlockSpec(memory_space=pltpu.HBM)
VMEM = pl.BlockSpec(memory_space=pltpu.VMEM)
SMEM = pl.BlockSpec(memory_space=pltpu.SMEM)


def chunk_of(size, wanted):
    return max(c for c in range(1, wanted + 1) if size % c == 0)


def x_size():
    return lax.axis_size("gz") * lax.axis_size("core")


def travel(packet, step_x, step_y):
    size_x, size_y = x_size(), lax.axis_size("gy")
    pairs = [
        (i * size_y + j, (i + step_x) * size_y + j + step_y)
        for i in range(size_x)
        for j in range(size_y)
        if 0 <= i + step_x < size_x and 0 <= j + step_y < size_y
    ]
    return lax.ppermute(packet, ("gz", "core", "gy"), pairs)


def pack(tiles, lists):
    halo = lists.shape[1]
    _, voxels, channels = tiles.shape

    def kernel(lists_ref, tiles_ref, *packets):
        for d, packet in enumerate(packets):
            for h in range(halo):
                packet[h] = tiles_ref[lists_ref[d, h]]

    return pl.pallas_call(
        kernel,
        out_shape=[jax.ShapeDtypeStruct((halo, voxels, channels), tiles.dtype)] * len(DIRECTIONS),
        in_specs=[SMEM, VMEM],
        out_specs=[VMEM] * len(DIRECTIONS),
        compiler_params=pltpu.CompilerParams(vmem_limit_bytes=16 * MIB),
        name="pack",
    )(lists, tiles)


def source_table(offsets, inputs, outputs, count, offset_count, tile_slots, empty, after):
    rows, blocks = inputs.shape

    def kernel(offsets_ref, inputs_ref, outputs_ref, count_ref, _, table_ref):
        def clear(k, carry):
            for t in range(tile_slots):
                table_ref[k, t] = empty
            return carry

        lax.fori_loop(0, offset_count, clear, 0)

        def block(n, carry):
            k = offsets_ref[n]
            for q in range(rows):
                table_ref[k, outputs_ref[q, n]] = inputs_ref[q, n]
            return carry

        lax.fori_loop(0, jnp.minimum(count_ref[0], blocks), block, 0)

    return pl.pallas_call(
        kernel,
        out_shape=jax.ShapeDtypeStruct((offset_count, tile_slots + 1), jnp.int32),
        in_specs=[SMEM] * 4 + [ANY],
        out_specs=SMEM,
        cost_estimate=pl.CostEstimate(flops=4 * 10**9, bytes_accessed=MIB, transcendentals=0),
        name="source_table",
    )(offsets, inputs, outputs, count, after)


def gathered(table_ref, ext, k, first, count):
    return jnp.concatenate([ext[table_ref[k, first + t]] for t in range(count)], axis=0)


def write_half(table_ref, late, ext, turned_ref, out_ref, out_hbm, sem, scale):
    offset_count, part, _ = out_ref.shape
    tile_slots = table_ref.shape[1] - 1
    count = (offset_count + 1) // 2

    def turn(j, carry):
        k = late * (offset_count - count) + j
        terms = jnp.dot(
            turned_ref[...],
            gathered(table_ref, ext, k, 0, tile_slots),
            preferred_element_type=jnp.float32,
        )
        terms = terms.T * scale
        for b in range(2):
            place = 2 * k + b - late * offset_count

            @pl.when((place >= 0) & (place < offset_count))
            def _():
                out_ref[place] = terms[b * part : (b + 1) * part]
                pltpu.make_async_copy(out_ref.at[place], out_hbm.at[place], sem).start()

        return carry

    lax.fori_loop(0, count, turn, 0)
    pltpu.make_async_copy(out_ref, out_hbm, sem).wait()


def turn_weights(weights):
    def kernel(w_ref, out_ref):
        for k in range(w_ref.shape[0]):
            out_ref[k] = w_ref[k].astype(jnp.float32).T.astype(out_ref.dtype)

    offset_count, channels, _ = weights.shape
    step = chunk_of(offset_count, 3)
    spec = pl.BlockSpec((step, channels, channels), lambda k: (k, 0, 0))
    return pl.pallas_call(
        kernel,
        grid=(offset_count // step,),
        out_shape=jax.ShapeDtypeStruct(weights.shape, weights.dtype),
        in_specs=[spec],
        out_specs=spec,
        compiler_params=pltpu.CompilerParams(vmem_limit_bytes=60 * MIB),
        cost_estimate=pl.CostEstimate(flops=8 * 10**9, bytes_accessed=7 * MIB, transcendentals=0),
        name="turn_weights",
    )(weights)


def forward_and_terms(table, half, tiles, halos, weights, cotangent, scale, after):
    tile_slots, voxels, channels = tiles.shape
    offset_count = weights.shape[0]
    directions, halo = len(halos), halos[0].shape[0]
    empty = tile_slots + directions * halo
    group = chunk_of(tile_slots, 8)
    groups = tile_slots // group
    rows = group * voxels
    deep = chunk_of(offset_count, 9)

    def kernel(table_ref, half_ref, tiles_ref, *refs):
        halo_refs, refs = refs[:directions], refs[directions:]
        w_hbm, cot_hbm, _, out_hbm, grad_hbm, turned_hbm, ext_hbm, half_hbm = refs[:8]
        w_ref, cot_ref, out_ref, grad, turned_ref, ext, half_out, acc, sems, w_sems = refs[8:]
        copies = [pltpu.make_async_copy(tiles_ref, ext.at[pl.ds(0, tile_slots)], sems.at[0])]
        for d, halo_ref in enumerate(halo_refs):
            place = ext.at[pl.ds(tile_slots + d * halo, halo)]
            copies.append(pltpu.make_async_copy(halo_ref, place, sems.at[d + 6]))

        def load_mats(step):
            part = pl.ds(step * deep, deep)
            return pltpu.make_async_copy(w_hbm.at[part], w_ref.at[part], w_sems.at[step])

        load_cot = pltpu.make_async_copy(cot_hbm, cot_ref, sems.at[1])
        for copy in copies + [load_mats(n) for n in range(offset_count // deep)] + [load_cot]:
            copy.start()
        ext[empty] = jnp.zeros((voxels, channels), ext.dtype)
        acc[...] = jnp.zeros_like(acc)
        for copy in copies:
            copy.wait()
        saves = [pltpu.make_async_copy(ext, ext_hbm, sems.at[2])]
        saves[0].start()

        def turn(step, carry):
            load_mats(step).wait()
            mats = w_ref[pl.ds(step * deep, deep)].reshape(deep * channels, channels)
            for g in range(groups):
                lhs = jnp.concatenate(
                    [
                        gathered(table_ref, ext, step * deep + j, g * group, group)
                        for j in range(deep)
                    ],
                    axis=1,
                )
                acc[g] += jnp.dot(lhs, mats, preferred_element_type=jnp.float32)
            return carry

        lax.fori_loop(0, offset_count // deep, turn, 0)
        load_cot.wait()

        def finish(t, carry):
            pre = acc[t // group, pl.ds(pl.multiple_of((t % group) * voxels, voxels), voxels), :]
            sigma = jax.nn.sigmoid(pre)
            out_ref[t] = (ext[t].astype(jnp.float32) + pre * sigma).astype(out_ref.dtype)
            incoming = cot_ref[t].astype(jnp.float32)
            grad[t] = (incoming * sigma * (1.0 + pre * (1.0 - sigma))).astype(grad.dtype)
            return carry

        lax.fori_loop(0, tile_slots, finish, 0)
        for g in range(groups):
            part = grad[pl.ds(g * group, group)].reshape(rows, channels)
            turned_ref[:, pl.ds(g * rows, rows)] = part.astype(jnp.float32).T.astype(jnp.bfloat16)
        saves += [
            pltpu.make_async_copy(out_ref, out_hbm, sems.at[3]),
            pltpu.make_async_copy(grad, grad_hbm, sems.at[4]),
            pltpu.make_async_copy(turned_ref, turned_hbm, sems.at[5]),
        ]
        for save in saves[1:]:
            save.start()
        write_half(
            table_ref, half_ref[0], ext, turned_ref, half_out, half_hbm, sems.at[directions + 6], scale
        )
        for save in saves:
            save.wait()

    flops = 3 * offset_count * tile_slots * voxels * channels * channels
    out_shape = [
        jax.ShapeDtypeStruct(tiles.shape, jnp.bfloat16),
        jax.ShapeDtypeStruct(tiles.shape, jnp.bfloat16),
        jax.ShapeDtypeStruct((channels, tile_slots * voxels), jnp.bfloat16),
        jax.ShapeDtypeStruct((empty + 1, voxels, channels), jnp.bfloat16),
        jax.ShapeDtypeStruct((offset_count, channels // 2, channels), jnp.float32),
    ]
    return pl.pallas_call(
        kernel,
        out_shape=out_shape,
        in_specs=[SMEM, SMEM, HBM] + [ANY] * directions + [HBM, HBM, ANY],
        out_specs=[HBM] * 5,
        scratch_shapes=[
            pltpu.VMEM(weights.shape, jnp.bfloat16),
            pltpu.VMEM(tiles.shape, jnp.bfloat16),
        ]
        + [pltpu.VMEM(one.shape, one.dtype) for one in out_shape]
        + [
            pltpu.VMEM((groups, rows, channels), jnp.float32),
            pltpu.SemaphoreType.DMA((directions + 7,)),
            pltpu.SemaphoreType.DMA((offset_count // deep,)),
        ],
        compiler_params=pltpu.CompilerParams(vmem_limit_bytes=60 * MIB),
        cost_estimate=pl.CostEstimate(flops=flops, bytes_accessed=20 * MIB, transcendentals=0),
        name="forward_and_terms",
    )(table, half, tiles, *halos, weights, cotangent, after)


def weight_terms(table, half, ext, turned, offset_count, scale):
    channels = ext.shape[2]

    def kernel(table_ref, half_ref, ext_hbm, turned_hbm, out_hbm, ext_ref, turned_ref, out_ref, sems):
        copies = [pltpu.make_async_copy(turned_hbm, turned_ref, sems.at[0])]
        slots = ext_ref.shape[0]
        for n in range(4):
            part = pl.ds(n * slots // 4, (n + 1) * slots // 4 - n * slots // 4)
            copies.append(pltpu.make_async_copy(ext_hbm.at[part], ext_ref.at[part], sems.at[n + 1]))
        for copy in copies:
            copy.start()
        for copy in copies:
            copy.wait()
        write_half(table_ref, half_ref[0], ext_ref, turned_ref, out_ref, out_hbm, sems.at[5], scale)

    flops = offset_count * turned.shape[1] * channels * channels
    out_shape = jax.ShapeDtypeStruct((offset_count, channels // 2, channels), jnp.float32)
    return pl.pallas_call(
        kernel,
        out_shape=out_shape,
        in_specs=[SMEM, SMEM, HBM, HBM],
        out_specs=HBM,
        scratch_shapes=[
            pltpu.VMEM(ext.shape, ext.dtype),
            pltpu.VMEM(turned.shape, turned.dtype),
            pltpu.VMEM(out_shape.shape, out_shape.dtype),
            pltpu.SemaphoreType.DMA((6,)),
        ],
        compiler_params=pltpu.CompilerParams(vmem_limit_bytes=60 * MIB),
        cost_estimate=pl.CostEstimate(flops=flops, bytes_accessed=6 * MIB, transcendentals=0),
        name="weight_terms",
    )(table, half, ext, turned)


def input_grad(table, pre_grad, turned_weights, halo):
    tile_slots, voxels, channels = pre_grad.shape
    offset_count = turned_weights.shape[0]
    empty = tile_slots + len(DIRECTIONS) * halo
    group = chunk_of(tile_slots, 8)
    groups = tile_slots // group
    rows = group * voxels
    unroll = chunk_of(offset_count, 3)
    bundles = len(BUNDLES)

    def kernel(table_ref, grad_hbm, w_hbm, own_hbm, *refs):
        adjoints_hbm, refs = refs[:bundles], refs[bundles:]
        own_ref, adjoints, refs = refs[0], refs[1 : bundles + 1], refs[bundles + 1 :]
        even, odd, grad, w_ref, sems = refs
        copies = [
            pltpu.make_async_copy(grad_hbm, grad, sems.at[0]),
            pltpu.make_async_copy(w_hbm, w_ref, sems.at[1]),
        ]
        for copy in copies:
            copy.start()
        for one in (even, odd):
            one[...] = jnp.zeros_like(one)
        for copy in copies:
            copy.wait()

        def turn(step, carry):
            for j in range(unroll):
                k = step * unroll + j
                for g in range(groups):
                    back = jnp.dot(
                        grad[pl.ds(g * group, group)].reshape(rows, channels),
                        w_ref[k],
                        preferred_element_type=jnp.float32,
                    )
                    for t in range(group):
                        slot = table_ref[k, g * group + t]
                        sums = (even, odd)[t % 2]
                        sums[slot] += back[t * voxels : (t + 1) * voxels]
            return carry

        lax.fori_loop(0, offset_count // unroll, turn, 0)

        saves = []
        for n, (bundle, adjoint) in enumerate(zip(BUNDLES, adjoints)):
            for m, pair in enumerate(bundle):
                for h in range(halo):
                    slot = tile_slots + DIRECTIONS.index(pair) * halo + h
                    adjoint[m * halo + h] = (even[slot] + odd[slot]).astype(jnp.bfloat16)
            saves.append(pltpu.make_async_copy(adjoint, adjoints_hbm[n], sems.at[n + 2]))
            saves[-1].start()

        def own(t, carry):
            own_ref[t] = even[t] + odd[t]
            return carry

        half = tile_slots // 2
        for n in range(2):
            lax.fori_loop(n * half, (n + 1) * half, own, 0)
            part = pl.ds(n * half, half)
            saves.append(
                pltpu.make_async_copy(own_ref.at[part], own_hbm.at[part], sems.at[bundles + 2 + n])
            )
            saves[-1].start()
        for save in saves:
            save.wait()

    flops = 2 * offset_count * tile_slots * voxels * channels * channels
    out_shape = [jax.ShapeDtypeStruct(pre_grad.shape, jnp.float32)] + [
        jax.ShapeDtypeStruct((len(bundle) * halo, voxels, channels), jnp.bfloat16)
        for bundle in BUNDLES
    ]
    return pl.pallas_call(
        kernel,
        out_shape=out_shape,
        in_specs=[SMEM, HBM, HBM],
        out_specs=[HBM] * (bundles + 1),
        scratch_shapes=[pltpu.VMEM(one.shape, one.dtype) for one in out_shape]
        + [pltpu.VMEM((empty + 1, voxels, channels), jnp.float32)] * 2
        + [
            pltpu.VMEM(pre_grad.shape, jnp.bfloat16),
            pltpu.VMEM(turned_weights.shape, jnp.bfloat16),
            pltpu.SemaphoreType.DMA((bundles + 4,)),
        ],
        compiler_params=pltpu.CompilerParams(vmem_limit_bytes=60 * MIB),
        cost_estimate=pl.CostEstimate(flops=flops, bytes_accessed=12 * MIB, transcendentals=0),
        name="input_grad",
    )(table, pre_grad, turned_weights)


def to_other_core(x):
    return lax.ppermute(x, "core", [(0, 1), (1, 0)])


def ring(axis):
    size = lax.axis_size(axis)

    def move(x, by):
        return lax.ppermute(x, axis, [(i, (i + by) % size) for i in range(size)])

    return size, lax.axis_index(axis), move


def given_out(terms, ring):
    size, place, _ = ring
    parts = []
    for s in range(size):
        blocks = [
            lax.dynamic_index_in_dim(
                one.reshape(size, one.shape[0] // size, one.shape[1]), (place + s) % size, keepdims=False
            )
            for one in terms
        ]
        parts.append(sum(blocks[1:], blocks[0]))
    return parts[0], [one.astype(jnp.bfloat16) for one in parts[1:]]


def handed(parts, ring):
    return [ring[2](one, s + 1) for s, one in enumerate(parts)]


def added(mine, arrived):
    for one in arrived:
        mine = mine + one.astype(jnp.float32)
    return mine


def fetched(piece, ring):
    return [ring[2](piece, -s) for s in range(1, ring[0])]


def in_order(piece, others, ring):
    size, place, _ = ring
    whole = jnp.zeros((size,) + piece.shape, piece.dtype)
    for s, one in enumerate([piece, *others]):
        whole = lax.dynamic_update_index_in_dim(whole, one, (place + s) % size, 0)
    return whole.reshape(size * piece.shape[0], piece.shape[1])


def together(*values):
    return lax.optimization_barrier(values)


def widen(place, half, whole):
    rows, channels = half.shape
    turns = chunk_of(rows // 16, 3)
    step = rows // turns

    def kernel(place_ref, half_ref, *refs):
        refs[-1][...] = half_ref[...].astype(jnp.float32)

    given = [] if whole is None else [whole]
    return pl.pallas_call(
        kernel,
        grid_spec=pltpu.PrefetchScalarGridSpec(
            num_scalar_prefetch=1,
            grid=(turns,),
            in_specs=[pl.BlockSpec((step, channels), lambda i, place: (i, 0))] + [ANY] * len(given),
            out_specs=pl.BlockSpec((step, channels), lambda i, place: (place[0] * turns + i, 0)),
        ),
        out_shape=jax.ShapeDtypeStruct((2 * rows, channels), jnp.float32),
        input_output_aliases={2: 0} if given else {},
        compiler_params=pltpu.CompilerParams(vmem_limit_bytes=24 * MIB),
        name="widen",
    )(place, half, *given)


def combine(lists, own, cotangent, returned):
    halo = lists.shape[1]
    tile_slots = own.shape[0]
    arrays = [array for array, _ in returned]

    def kernel(lists_ref, own_ref, cot_ref, *refs):
        out_ref, acc = refs[len(arrays) :]

        def start(t, carry):
            acc[t] = own_ref[t] + cot_ref[t].astype(jnp.float32)
            return carry

        lax.fori_loop(0, tile_slots, start, 0)
        for ref, (_, pairs) in zip(refs, returned):
            for n, pair in enumerate(pairs):
                for h in range(halo):
                    tile = lists_ref[DIRECTIONS.index(pair), h]
                    acc[tile] += ref[n * halo + h].astype(jnp.float32)

        def finish(t, carry):
            out_ref[t] = acc[t].astype(out_ref.dtype)
            return carry

        lax.fori_loop(0, tile_slots, finish, 0)

    return pl.pallas_call(
        kernel,
        out_shape=jax.ShapeDtypeStruct(own.shape, jnp.bfloat16),
        in_specs=[SMEM] + [VMEM] * (len(arrays) + 2),
        out_specs=VMEM,
        scratch_shapes=[pltpu.VMEM(own.shape, jnp.float32)],
        compiler_params=pltpu.CompilerParams(vmem_limit_bytes=16 * MIB),
        name="combine",
    )(lists, own, cotangent, *arrays)


def shards(
    features, weights, cotangent, send_lists, block_offset, block_input, block_output, block_count
):
    tiles = features[0, 0]
    incoming = cotangent[0, 0]
    lists = send_lists[0, 0]
    tile_slots, voxels, channels = tiles.shape
    directions, halo = lists.shape
    device_total = x_size() * lax.axis_size("gy")
    scale = 1.0 / math.sqrt(voxels * tile_slots * device_total)
    offset_count = weights.shape[0]
    core = lax.axis_index("core").astype(jnp.int32)[None]

    packets = pack(tiles, lists)
    table = source_table(
        block_offset[0, 0],
        block_input[0, 0].T,
        block_output[0, 0].T,
        block_count[0],
        offset_count,
        tile_slots,
        tile_slots + directions * halo,
        packets[0],
    )
    turned_weights = turn_weights(weights)
    order = sorted(range(directions), key=lambda d: DIRECTIONS[d][1] == 0)
    arrived = {d: travel(packets[d], *DIRECTIONS[d]) for d in order}
    halos = [arrived[d] for d in range(directions)]
    out_features, pre_grad, turned, ext, send = forward_and_terms(
        table, 1 - core, tiles, halos, weights, incoming, scale, turned_weights
    )
    received = to_other_core(send)
    keep = weight_terms(table, core, ext, turned, offset_count, scale)
    levels = ring("gy"), ring("gz")
    mine, out = given_out([keep.reshape(-1, channels), received.reshape(-1, channels)], levels[0])

    pre_grad, *out = together(pre_grad, *out)
    moved = handed(out, levels[0])
    own, low, high, low_both, high_both, behind, ahead = input_grad(table, pre_grad, turned_weights, halo)
    low, *moved = together(low, *moved)
    low, high = travel(low, 0, 1), travel(high, 0, -1)
    low_both, high_both = travel(low_both, 0, 1), travel(high_both, 0, -1)

    mine, out = given_out([added(mine, moved)], levels[1])
    piece = added(mine, handed(out, levels[1])).astype(jnp.bfloat16)
    low, high, piece = together(low, high, piece)
    piece = in_order(piece, fetched(piece, levels[1]), levels[1])
    low_both, high_both, piece = together(low_both, high_both, piece)
    behind = jnp.concatenate([behind, low_both[:halo], high_both[:halo]])
    ahead = jnp.concatenate([ahead, low_both[halo:], high_both[halo:]])
    behind, ahead = travel(behind, 1, 0), travel(ahead, -1, 0)
    own_half = in_order(piece, fetched(piece, levels[0]), levels[0])
    behind, ahead, own_half = together(behind, ahead, own_half)
    feat_grad = combine(
        lists,
        own,
        incoming,
        [
            (low, ((0, -1),)),
            (high, ((0, 1),)),
            (behind, ((-1, 0), (-1, -1), (-1, 1))),
            (ahead, ((1, 0), (1, -1), (1, 1))),
        ],
    )
    other_half = to_other_core(own_half)
    weight_grad = widen(1 - core, other_half, widen(core, own_half, None)).reshape(weights.shape)
    return (out_features[None, None], feat_grad[None, None], weight_grad)


def solution(mesh):
    size_x, size_y = mesh.devices.shape
    split = Mesh(mesh.devices.reshape(size_x // 2, 2, size_y), ("gz", "core", "gy"))
    place = P(("gz", "core"), "gy")
    return jax.shard_map(
        shards,
        mesh=split,
        in_specs=(place, P(), place, place, place, place, place, place),
        out_specs=(place, place, P()),
        check_vma=False,
    )
```

```python
import math

import jax
import jax.numpy as jnp
from jax import lax
from jax.experimental import pallas as pl
from jax.experimental.pallas import tpu as pltpu
from jax.sharding import Mesh
from jax.sharding import PartitionSpec as P

DIRECTIONS = ((-1, -1), (-1, 0), (-1, 1), (0, -1), (0, 1), (1, -1), (1, 0), (1, 1))
BUNDLES = (
    ((0, -1),),
    ((0, 1),),
    ((-1, -1), (1, -1)),
    ((-1, 1), (1, 1)),
    ((-1, 0),),
    ((1, 0),),
)
MIB = 1024 * 1024
ANY = pl.BlockSpec(memory_space=pl.ANY)
HBM = pl.BlockSpec(memory_space=pltpu.HBM)
VMEM = pl.BlockSpec(memory_space=pltpu.VMEM)
SMEM = pl.BlockSpec(memory_space=pltpu.SMEM)


def chunk_of(size, wanted):
    return max(c for c in range(1, wanted + 1) if size % c == 0)


def x_size():
    return lax.axis_size("gz") * lax.axis_size("core")


def travel(packet, step_x, step_y):
    size_x, size_y = x_size(), lax.axis_size("gy")
    pairs = [
        (i * size_y + j, (i + step_x) * size_y + j + step_y)
        for i in range(size_x)
        for j in range(size_y)
        if 0 <= i + step_x < size_x and 0 <= j + step_y < size_y
    ]
    return lax.ppermute(packet, ("gz", "core", "gy"), pairs)


def pack(tiles, lists):
    halo = lists.shape[1]
    _, voxels, channels = tiles.shape

    def kernel(lists_ref, tiles_ref, *packets):
        for d, packet in enumerate(packets):
            for h in range(halo):
                packet[h] = tiles_ref[lists_ref[d, h]]

    return pl.pallas_call(
        kernel,
        out_shape=[jax.ShapeDtypeStruct((halo, voxels, channels), tiles.dtype)] * len(DIRECTIONS),
        in_specs=[SMEM, VMEM],
        out_specs=[VMEM] * len(DIRECTIONS),
        compiler_params=pltpu.CompilerParams(vmem_limit_bytes=16 * MIB),
        name="pack",
    )(lists, tiles)


def source_table(offsets, inputs, outputs, count, offset_count, tile_slots, empty, after):
    rows, blocks = inputs.shape

    def kernel(offsets_ref, inputs_ref, outputs_ref, count_ref, _, table_ref):
        def clear(k, carry):
            for t in range(tile_slots):
                table_ref[k, t] = empty
            return carry

        lax.fori_loop(0, offset_count, clear, 0)

        def block(n, carry):
            k = offsets_ref[n]
            for q in range(rows):
                table_ref[k, outputs_ref[q, n]] = inputs_ref[q, n]
            return carry

        lax.fori_loop(0, jnp.minimum(count_ref[0], blocks), block, 0)

    return pl.pallas_call(
        kernel,
        out_shape=jax.ShapeDtypeStruct((offset_count, tile_slots + 1), jnp.int32),
        in_specs=[SMEM] * 4 + [ANY],
        out_specs=SMEM,
        cost_estimate=pl.CostEstimate(flops=4 * 10**9, bytes_accessed=MIB, transcendentals=0),
        name="source_table",
    )(offsets, inputs, outputs, count, after)


def gathered(table_ref, ext, k, first, count):
    return jnp.concatenate([ext[table_ref[k, first + t]] for t in range(count)], axis=0)


def write_half(table_ref, late, ext, turned_ref, out_ref, out_hbm, sem, scale):
    offset_count, part, _ = out_ref.shape
    tile_slots = table_ref.shape[1] - 1
    count = (offset_count + 1) // 2

    def turn(j, carry):
        k = late * (offset_count - count) + j
        terms = jnp.dot(
            turned_ref[...],
            gathered(table_ref, ext, k, 0, tile_slots),
            preferred_element_type=jnp.float32,
        )
        terms = terms.T * scale
        for b in range(2):
            place = 2 * k + b - late * offset_count

            @pl.when((place >= 0) & (place < offset_count))
            def _():
                out_ref[place] = terms[b * part : (b + 1) * part]
                pltpu.make_async_copy(out_ref.at[place], out_hbm.at[place], sem).start()

        return carry

    lax.fori_loop(0, count, turn, 0)
    pltpu.make_async_copy(out_ref, out_hbm, sem).wait()


def turn_weights(weights, after):
    def kernel(_, w_ref, out_ref):
        for k in range(w_ref.shape[0]):
            out_ref[k] = w_ref[k].astype(jnp.float32).T.astype(out_ref.dtype)

    offset_count, channels, _ = weights.shape
    step = chunk_of(offset_count, 3)
    spec = pl.BlockSpec((step, channels, channels), lambda k: (k, 0, 0))
    return pl.pallas_call(
        kernel,
        grid=(offset_count // step,),
        out_shape=jax.ShapeDtypeStruct(weights.shape, weights.dtype),
        in_specs=[SMEM, spec],
        out_specs=spec,
        compiler_params=pltpu.CompilerParams(vmem_limit_bytes=16 * MIB),
        cost_estimate=pl.CostEstimate(flops=8 * 10**9, bytes_accessed=7 * MIB, transcendentals=0),
        name="turn_weights",
    )(after, weights)


def forward_and_terms(table, half, tiles, halos, weights, cotangent, scale, after):
    tile_slots, voxels, channels = tiles.shape
    offset_count = weights.shape[0]
    directions, halo = len(halos), halos[0].shape[0]
    empty = tile_slots + directions * halo
    group = chunk_of(tile_slots, 8)
    groups = tile_slots // group
    rows = group * voxels
    deep = chunk_of(offset_count, 9)

    def kernel(table_ref, half_ref, tiles_ref, *refs):
        halo_refs, refs = refs[:directions], refs[directions:]
        w_hbm, cot_hbm, _, out_hbm, grad_hbm, turned_hbm, ext_hbm, half_hbm = refs[:8]
        w_ref, cot_ref, out_ref, grad, turned_ref, ext, half_out, acc, sems, w_sems = refs[8:]
        copies = [pltpu.make_async_copy(tiles_ref, ext.at[pl.ds(0, tile_slots)], sems.at[0])]
        for d, halo_ref in enumerate(halo_refs):
            place = ext.at[pl.ds(tile_slots + d * halo, halo)]
            copies.append(pltpu.make_async_copy(halo_ref, place, sems.at[d + 6]))

        def load_mats(step):
            part = pl.ds(step * deep, deep)
            return pltpu.make_async_copy(w_hbm.at[part], w_ref.at[part], w_sems.at[step])

        load_cot = pltpu.make_async_copy(cot_hbm, cot_ref, sems.at[1])
        for copy in copies + [load_mats(n) for n in range(offset_count // deep)] + [load_cot]:
            copy.start()
        ext[empty] = jnp.zeros((voxels, channels), ext.dtype)
        acc[...] = jnp.zeros_like(acc)
        for copy in copies:
            copy.wait()
        saves = [pltpu.make_async_copy(ext, ext_hbm, sems.at[2])]
        saves[0].start()

        def turn(step, carry):
            load_mats(step).wait()
            mats = w_ref[pl.ds(step * deep, deep)].reshape(deep * channels, channels)
            for g in range(groups):
                lhs = jnp.concatenate(
                    [
                        gathered(table_ref, ext, step * deep + j, g * group, group)
                        for j in range(deep)
                    ],
                    axis=1,
                )
                acc[g] += jnp.dot(lhs, mats, preferred_element_type=jnp.float32)
            return carry

        lax.fori_loop(0, offset_count // deep, turn, 0)
        load_cot.wait()

        def finish(t, carry):
            pre = acc[t // group, pl.ds(pl.multiple_of((t % group) * voxels, voxels), voxels), :]
            sigma = jax.nn.sigmoid(pre)
            out_ref[t] = (ext[t].astype(jnp.float32) + pre * sigma).astype(out_ref.dtype)
            incoming = cot_ref[t].astype(jnp.float32)
            grad[t] = (incoming * sigma * (1.0 + pre * (1.0 - sigma))).astype(grad.dtype)
            return carry

        lax.fori_loop(0, tile_slots, finish, 0)
        for g in range(groups):
            part = grad[pl.ds(g * group, group)].reshape(rows, channels)
            turned_ref[:, pl.ds(g * rows, rows)] = part.astype(jnp.float32).T.astype(jnp.bfloat16)
        saves += [
            pltpu.make_async_copy(out_ref, out_hbm, sems.at[3]),
            pltpu.make_async_copy(grad, grad_hbm, sems.at[4]),
            pltpu.make_async_copy(turned_ref, turned_hbm, sems.at[5]),
        ]
        for save in saves[1:]:
            save.start()
        write_half(
            table_ref, half_ref[0], ext, turned_ref, half_out, half_hbm, sems.at[directions + 6], scale
        )
        for save in saves:
            save.wait()

    flops = 3 * offset_count * tile_slots * voxels * channels * channels
    out_shape = [
        jax.ShapeDtypeStruct(tiles.shape, jnp.bfloat16),
        jax.ShapeDtypeStruct(tiles.shape, jnp.bfloat16),
        jax.ShapeDtypeStruct((channels, tile_slots * voxels), jnp.bfloat16),
        jax.ShapeDtypeStruct((empty + 1, voxels, channels), jnp.bfloat16),
        jax.ShapeDtypeStruct((offset_count, channels // 2, channels), jnp.float32),
    ]
    return pl.pallas_call(
        kernel,
        out_shape=out_shape,
        in_specs=[SMEM, SMEM, HBM] + [ANY] * directions + [HBM, HBM, ANY],
        out_specs=[HBM] * 5,
        scratch_shapes=[
            pltpu.VMEM(weights.shape, jnp.bfloat16),
            pltpu.VMEM(tiles.shape, jnp.bfloat16),
        ]
        + [pltpu.VMEM(one.shape, one.dtype) for one in out_shape]
        + [
            pltpu.VMEM((groups, rows, channels), jnp.float32),
            pltpu.SemaphoreType.DMA((directions + 7,)),
            pltpu.SemaphoreType.DMA((offset_count // deep,)),
        ],
        compiler_params=pltpu.CompilerParams(vmem_limit_bytes=60 * MIB),
        cost_estimate=pl.CostEstimate(flops=flops, bytes_accessed=20 * MIB, transcendentals=0),
        name="forward_and_terms",
    )(table, half, tiles, *halos, weights, cotangent, after)


def weight_terms(table, half, ext, turned, offset_count, scale):
    channels = ext.shape[2]

    def kernel(table_ref, half_ref, ext_hbm, turned_hbm, out_hbm, ext_ref, turned_ref, out_ref, sems):
        copies = [pltpu.make_async_copy(turned_hbm, turned_ref, sems.at[0])]
        slots = ext_ref.shape[0]
        for n in range(4):
            part = pl.ds(n * slots // 4, (n + 1) * slots // 4 - n * slots // 4)
            copies.append(pltpu.make_async_copy(ext_hbm.at[part], ext_ref.at[part], sems.at[n + 1]))
        for copy in copies:
            copy.start()
        for copy in copies:
            copy.wait()
        write_half(table_ref, half_ref[0], ext_ref, turned_ref, out_ref, out_hbm, sems.at[5], scale)

    flops = offset_count * turned.shape[1] * channels * channels
    out_shape = jax.ShapeDtypeStruct((offset_count, channels // 2, channels), jnp.float32)
    return pl.pallas_call(
        kernel,
        out_shape=out_shape,
        in_specs=[SMEM, SMEM, HBM, HBM],
        out_specs=HBM,
        scratch_shapes=[
            pltpu.VMEM(ext.shape, ext.dtype),
            pltpu.VMEM(turned.shape, turned.dtype),
            pltpu.VMEM(out_shape.shape, out_shape.dtype),
            pltpu.SemaphoreType.DMA((6,)),
        ],
        compiler_params=pltpu.CompilerParams(vmem_limit_bytes=60 * MIB),
        cost_estimate=pl.CostEstimate(flops=flops, bytes_accessed=6 * MIB, transcendentals=0),
        name="weight_terms",
    )(table, half, ext, turned)


def input_grad(table, pre_grad, turned_weights, halo):
    tile_slots, voxels, channels = pre_grad.shape
    offset_count = turned_weights.shape[0]
    empty = tile_slots + len(DIRECTIONS) * halo
    group = chunk_of(tile_slots, 8)
    groups = tile_slots // group
    rows = group * voxels
    unroll = chunk_of(offset_count, 3)
    bundles = len(BUNDLES)

    def kernel(table_ref, grad_hbm, w_hbm, own_hbm, *refs):
        adjoints_hbm, refs = refs[:bundles], refs[bundles:]
        own_ref, adjoints, refs = refs[0], refs[1 : bundles + 1], refs[bundles + 1 :]
        even, odd, grad, w_ref, sems = refs
        copies = [
            pltpu.make_async_copy(grad_hbm, grad, sems.at[0]),
            pltpu.make_async_copy(w_hbm, w_ref, sems.at[1]),
        ]
        for copy in copies:
            copy.start()
        for one in (even, odd):
            one[...] = jnp.zeros_like(one)
        for copy in copies:
            copy.wait()

        def turn(step, carry):
            for j in range(unroll):
                k = step * unroll + j
                for g in range(groups):
                    back = jnp.dot(
                        grad[pl.ds(g * group, group)].reshape(rows, channels),
                        w_ref[k],
                        preferred_element_type=jnp.float32,
                    )
                    for t in range(group):
                        slot = table_ref[k, g * group + t]
                        sums = (even, odd)[t % 2]
                        sums[slot] += back[t * voxels : (t + 1) * voxels]
            return carry

        lax.fori_loop(0, offset_count // unroll, turn, 0)

        saves = []
        for n, (bundle, adjoint) in enumerate(zip(BUNDLES, adjoints)):
            for m, pair in enumerate(bundle):
                for h in range(halo):
                    slot = tile_slots + DIRECTIONS.index(pair) * halo + h
                    adjoint[m * halo + h] = (even[slot] + odd[slot]).astype(jnp.bfloat16)
            saves.append(pltpu.make_async_copy(adjoint, adjoints_hbm[n], sems.at[n + 2]))
            saves[-1].start()

        def own(t, carry):
            own_ref[t] = even[t] + odd[t]
            return carry

        half = tile_slots // 2
        for n in range(2):
            lax.fori_loop(n * half, (n + 1) * half, own, 0)
            part = pl.ds(n * half, half)
            saves.append(
                pltpu.make_async_copy(own_ref.at[part], own_hbm.at[part], sems.at[bundles + 2 + n])
            )
            saves[-1].start()
        for save in saves:
            save.wait()

    flops = 2 * offset_count * tile_slots * voxels * channels * channels
    out_shape = [jax.ShapeDtypeStruct(pre_grad.shape, jnp.float32)] + [
        jax.ShapeDtypeStruct((len(bundle) * halo, voxels, channels), jnp.bfloat16)
        for bundle in BUNDLES
    ]
    return pl.pallas_call(
        kernel,
        out_shape=out_shape,
        in_specs=[SMEM, HBM, HBM],
        out_specs=[HBM] * (bundles + 1),
        scratch_shapes=[pltpu.VMEM(one.shape, one.dtype) for one in out_shape]
        + [pltpu.VMEM((empty + 1, voxels, channels), jnp.float32)] * 2
        + [
            pltpu.VMEM(pre_grad.shape, jnp.bfloat16),
            pltpu.VMEM(turned_weights.shape, jnp.bfloat16),
            pltpu.SemaphoreType.DMA((bundles + 4,)),
        ],
        compiler_params=pltpu.CompilerParams(vmem_limit_bytes=60 * MIB),
        cost_estimate=pl.CostEstimate(flops=flops, bytes_accessed=12 * MIB, transcendentals=0),
        name="input_grad",
    )(table, pre_grad, turned_weights)


def to_other_core(x):
    return lax.ppermute(x, "core", [(0, 1), (1, 0)])


def ring(axis):
    size = lax.axis_size(axis)

    def move(x, by):
        return lax.ppermute(x, axis, [(i, (i + by) % size) for i in range(size)])

    return size, lax.axis_index(axis), move


def given_out(terms, ring):
    size, place, _ = ring
    parts = []
    for s in range(size):
        blocks = [
            lax.dynamic_index_in_dim(
                one.reshape(size, one.shape[0] // size, one.shape[1]), (place + s) % size, keepdims=False
            )
            for one in terms
        ]
        parts.append(sum(blocks[1:], blocks[0]))
    return parts[0], [one.astype(jnp.bfloat16) for one in parts[1:]]


def handed(parts, ring):
    return [ring[2](one, s + 1) for s, one in enumerate(parts)]


def added(mine, arrived):
    for one in arrived:
        mine = mine + one.astype(jnp.float32)
    return mine


def fetched(piece, ring):
    return [ring[2](piece, -s) for s in range(1, ring[0])]


def in_order(piece, others, ring):
    size, place, _ = ring
    whole = jnp.zeros((size,) + piece.shape, piece.dtype)
    for s, one in enumerate([piece, *others]):
        whole = lax.dynamic_update_index_in_dim(whole, one, (place + s) % size, 0)
    return whole.reshape(size * piece.shape[0], piece.shape[1])


def together(*values):
    return lax.optimization_barrier(values)


def widen(place, half, whole):
    rows, channels = half.shape
    turns = chunk_of(rows // 16, 3)
    step = rows // turns

    def kernel(place_ref, half_ref, *refs):
        refs[-1][...] = half_ref[...].astype(jnp.float32)

    given = [] if whole is None else [whole]
    return pl.pallas_call(
        kernel,
        grid_spec=pltpu.PrefetchScalarGridSpec(
            num_scalar_prefetch=1,
            grid=(turns,),
            in_specs=[pl.BlockSpec((step, channels), lambda i, place: (i, 0))] + [ANY] * len(given),
            out_specs=pl.BlockSpec((step, channels), lambda i, place: (place[0] * turns + i, 0)),
        ),
        out_shape=jax.ShapeDtypeStruct((2 * rows, channels), jnp.float32),
        input_output_aliases={2: 0} if given else {},
        compiler_params=pltpu.CompilerParams(vmem_limit_bytes=24 * MIB),
        name="widen",
    )(place, half, *given)


def combine(lists, own, cotangent, returned):
    halo = lists.shape[1]
    tile_slots = own.shape[0]
    arrays = [array for array, _ in returned]

    def kernel(lists_ref, own_ref, cot_ref, *refs):
        out_ref, acc = refs[len(arrays) :]

        def start(t, carry):
            acc[t] = own_ref[t] + cot_ref[t].astype(jnp.float32)
            return carry

        lax.fori_loop(0, tile_slots, start, 0)
        for ref, (_, pairs) in zip(refs, returned):
            for n, pair in enumerate(pairs):
                for h in range(halo):
                    tile = lists_ref[DIRECTIONS.index(pair), h]
                    acc[tile] += ref[n * halo + h].astype(jnp.float32)

        def finish(t, carry):
            out_ref[t] = acc[t].astype(out_ref.dtype)
            return carry

        lax.fori_loop(0, tile_slots, finish, 0)

    return pl.pallas_call(
        kernel,
        out_shape=jax.ShapeDtypeStruct(own.shape, jnp.bfloat16),
        in_specs=[SMEM] + [VMEM] * (len(arrays) + 2),
        out_specs=VMEM,
        scratch_shapes=[pltpu.VMEM(own.shape, jnp.float32)],
        compiler_params=pltpu.CompilerParams(vmem_limit_bytes=16 * MIB),
        name="combine",
    )(lists, own, cotangent, *arrays)


def shards(
    features, weights, cotangent, send_lists, block_offset, block_input, block_output, block_count
):
    tiles = features[0, 0]
    incoming = cotangent[0, 0]
    lists = send_lists[0, 0]
    tile_slots, voxels, channels = tiles.shape
    directions, halo = lists.shape
    device_total = x_size() * lax.axis_size("gy")
    scale = 1.0 / math.sqrt(voxels * tile_slots * device_total)
    offset_count = weights.shape[0]
    core = lax.axis_index("core").astype(jnp.int32)[None]

    packets = pack(tiles, lists)
    table = source_table(
        block_offset[0, 0],
        block_input[0, 0].T,
        block_output[0, 0].T,
        block_count[0],
        offset_count,
        tile_slots,
        tile_slots + directions * halo,
        packets[0],
    )
    turned_weights = turn_weights(weights, table)
    order = [
        DIRECTIONS.index(pair)
        for pair in ((-1, -1), (1, 1), (-1, 0), (1, 0), (-1, 1), (1, -1), (0, -1), (0, 1))
    ]
    arrived = {d: travel(packets[d], *DIRECTIONS[d]) for d in order}
    halos = [arrived[d] for d in range(directions)]
    out_features, pre_grad, turned, ext, send = forward_and_terms(
        table, 1 - core, tiles, halos, weights, incoming, scale, turned_weights
    )
    received = to_other_core(send)
    keep = weight_terms(table, core, ext, turned, offset_count, scale)
    levels = ring("gy"), ring("gz")
    mine, out = given_out([keep.reshape(-1, channels), received.reshape(-1, channels)], levels[0])

    pre_grad, *out = together(pre_grad, *out)
    moved = handed(out, levels[0])
    own, low, high, low_both, high_both, behind, ahead = input_grad(table, pre_grad, turned_weights, halo)
    low, high = travel(low, 0, 1), travel(high, 0, -1)
    low, *moved = together(low, *moved)
    low_both, high_both = travel(low_both, 0, 1), travel(high_both, 0, -1)

    mine, out = given_out([added(mine, moved)], levels[1])
    piece = added(mine, handed(out, levels[1])).astype(jnp.bfloat16)
    low, high, piece = together(low, high, piece)
    piece = in_order(piece, fetched(piece, levels[1]), levels[1])
    low_both, high_both, piece = together(low_both, high_both, piece)
    behind = jnp.concatenate([behind, low_both[:halo], high_both[:halo]])
    ahead = jnp.concatenate([ahead, low_both[halo:], high_both[halo:]])
    behind, ahead = travel(behind, 1, 0), travel(ahead, -1, 0)
    own_half = in_order(piece, fetched(piece, levels[0]), levels[0])
    behind, ahead, own_half = together(behind, ahead, own_half)
    feat_grad = combine(
        lists,
        own,
        incoming,
        [
            (low, ((0, -1),)),
            (high, ((0, 1),)),
            (behind, ((-1, 0), (-1, -1), (-1, 1))),
            (ahead, ((1, 0), (1, -1), (1, 1))),
        ],
    )
    other_half = to_other_core(own_half)
    weight_grad = widen(1 - core, other_half, widen(core, own_half, None)).reshape(weights.shape)
    return (out_features[None, None], feat_grad[None, None], weight_grad)


def solution(mesh):
    size_x, size_y = mesh.devices.shape
    split = Mesh(mesh.devices.reshape(size_x // 2, 2, size_y), ("gz", "core", "gy"))
    place = P(("gz", "core"), "gy")
    return jax.shard_map(
        shards,
        mesh=split,
        in_specs=(place, P(), place, place, place, place, place, place),
        out_specs=(place, place, P()),
        check_vma=False,
    )
```

```python
import math

import jax
import jax.numpy as jnp
from jax import lax
from jax.experimental import pallas as pl
from jax.experimental.pallas import tpu as pltpu
from jax.sharding import Mesh
from jax.sharding import PartitionSpec as P

DIRECTIONS = ((-1, -1), (-1, 0), (-1, 1), (0, -1), (0, 1), (1, -1), (1, 0), (1, 1))
BUNDLES = (
    ((0, -1),),
    ((0, 1),),
    ((-1, -1), (1, -1)),
    ((-1, 1), (1, 1)),
    ((-1, 0),),
    ((1, 0),),
)
MIB = 1024 * 1024
ANY = pl.BlockSpec(memory_space=pl.ANY)
HBM = pl.BlockSpec(memory_space=pltpu.HBM)
VMEM = pl.BlockSpec(memory_space=pltpu.VMEM)
SMEM = pl.BlockSpec(memory_space=pltpu.SMEM)


def chunk_of(size, wanted):
    return max(c for c in range(1, wanted + 1) if size % c == 0)


def x_size():
    return lax.axis_size("gz") * lax.axis_size("core")


def travel(packet, step_x, step_y):
    size_x, size_y = x_size(), lax.axis_size("gy")
    pairs = [
        (i * size_y + j, (i + step_x) * size_y + j + step_y)
        for i in range(size_x)
        for j in range(size_y)
        if 0 <= i + step_x < size_x and 0 <= j + step_y < size_y
    ]
    return lax.ppermute(packet, ("gz", "core", "gy"), pairs)


def pack(tiles, lists):
    halo = lists.shape[1]
    _, voxels, channels = tiles.shape

    def kernel(lists_ref, tiles_ref, *packets):
        for d, packet in enumerate(packets):
            for h in range(halo):
                packet[h] = tiles_ref[lists_ref[d, h]]

    return pl.pallas_call(
        kernel,
        out_shape=[jax.ShapeDtypeStruct((halo, voxels, channels), tiles.dtype)] * len(DIRECTIONS),
        in_specs=[SMEM, VMEM],
        out_specs=[VMEM] * len(DIRECTIONS),
        compiler_params=pltpu.CompilerParams(vmem_limit_bytes=16 * MIB),
        name="pack",
    )(lists, tiles)


def source_table(offsets, inputs, outputs, count, offset_count, tile_slots, empty, after):
    rows, blocks = inputs.shape

    def kernel(offsets_ref, inputs_ref, outputs_ref, count_ref, _, table_ref):
        def clear(k, carry):
            for t in range(tile_slots):
                table_ref[k, t] = empty
            return carry

        lax.fori_loop(0, offset_count, clear, 0)

        def block(n, carry):
            k = offsets_ref[n]
            for q in range(rows):
                table_ref[k, outputs_ref[q, n]] = inputs_ref[q, n]
            return carry

        lax.fori_loop(0, jnp.minimum(count_ref[0], blocks), block, 0)

    return pl.pallas_call(
        kernel,
        out_shape=jax.ShapeDtypeStruct((offset_count, tile_slots + 1), jnp.int32),
        in_specs=[SMEM] * 4 + [ANY],
        out_specs=SMEM,
        cost_estimate=pl.CostEstimate(flops=4 * 10**9, bytes_accessed=MIB, transcendentals=0),
        name="source_table",
    )(offsets, inputs, outputs, count, after)


def gathered(table_ref, ext, k, first, count):
    return jnp.concatenate([ext[table_ref[k, first + t]] for t in range(count)], axis=0)


def write_half(table_ref, late, ext, turned_ref, out_ref, out_hbm, sem, scale):
    offset_count, part, _ = out_ref.shape
    tile_slots = table_ref.shape[1] - 1
    count = (offset_count + 1) // 2

    def turn(j, carry):
        k = late * (offset_count - count) + j
        terms = jnp.dot(
            turned_ref[...],
            gathered(table_ref, ext, k, 0, tile_slots),
            preferred_element_type=jnp.float32,
        )
        terms = terms.T * scale
        for b in range(2):
            place = 2 * k + b - late * offset_count

            @pl.when((place >= 0) & (place < offset_count))
            def _():
                out_ref[place] = terms[b * part : (b + 1) * part]
                pltpu.make_async_copy(out_ref.at[place], out_hbm.at[place], sem).start()

        return carry

    lax.fori_loop(0, count, turn, 0)
    pltpu.make_async_copy(out_ref, out_hbm, sem).wait()


def turn_weights(weights, after):
    def kernel(_, w_ref, out_ref):
        for k in range(w_ref.shape[0]):
            out_ref[k] = w_ref[k].astype(jnp.float32).T.astype(out_ref.dtype)

    offset_count, channels, _ = weights.shape
    step = chunk_of(offset_count, 3)
    spec = pl.BlockSpec((step, channels, channels), lambda k: (k, 0, 0))
    return pl.pallas_call(
        kernel,
        grid=(offset_count // step,),
        out_shape=jax.ShapeDtypeStruct(weights.shape, weights.dtype),
        in_specs=[SMEM, spec],
        out_specs=spec,
        compiler_params=pltpu.CompilerParams(vmem_limit_bytes=16 * MIB),
        cost_estimate=pl.CostEstimate(flops=8 * 10**9, bytes_accessed=7 * MIB, transcendentals=0),
        name="turn_weights",
    )(after, weights)


def forward_and_terms(table, half, tiles, halos, weights, cotangent, scale, after):
    tile_slots, voxels, channels = tiles.shape
    offset_count = weights.shape[0]
    directions, halo = len(halos), halos[0].shape[0]
    empty = tile_slots + directions * halo
    group = chunk_of(tile_slots, 8)
    groups = tile_slots // group
    rows = group * voxels
    deep = chunk_of(offset_count, 9)

    def kernel(table_ref, half_ref, tiles_ref, *refs):
        halo_refs, refs = refs[:directions], refs[directions:]
        w_hbm, cot_hbm, _, out_hbm, grad_hbm, turned_hbm, ext_hbm, half_hbm = refs[:8]
        w_ref, cot_ref, out_ref, grad, turned_ref, ext, half_out, acc, sems, w_sems = refs[8:]
        copies = [pltpu.make_async_copy(tiles_ref, ext.at[pl.ds(0, tile_slots)], sems.at[0])]
        for d, halo_ref in enumerate(halo_refs):
            place = ext.at[pl.ds(tile_slots + d * halo, halo)]
            copies.append(pltpu.make_async_copy(halo_ref, place, sems.at[d + 6]))

        def load_mats(step):
            part = pl.ds(step * deep, deep)
            return pltpu.make_async_copy(w_hbm.at[part], w_ref.at[part], w_sems.at[step])

        load_cot = pltpu.make_async_copy(cot_hbm, cot_ref, sems.at[1])
        for copy in copies + [load_mats(n) for n in range(offset_count // deep)] + [load_cot]:
            copy.start()
        ext[empty] = jnp.zeros((voxels, channels), ext.dtype)
        acc[...] = jnp.zeros_like(acc)
        for copy in copies:
            copy.wait()
        saves = [pltpu.make_async_copy(ext, ext_hbm, sems.at[2])]
        saves[0].start()

        def turn(step, carry):
            load_mats(step).wait()
            mats = w_ref[pl.ds(step * deep, deep)].reshape(deep * channels, channels)
            for g in range(groups):
                lhs = jnp.concatenate(
                    [
                        gathered(table_ref, ext, step * deep + j, g * group, group)
                        for j in range(deep)
                    ],
                    axis=1,
                )
                acc[g] += jnp.dot(lhs, mats, preferred_element_type=jnp.float32)
            return carry

        lax.fori_loop(0, offset_count // deep, turn, 0)
        load_cot.wait()

        def finish(t, carry):
            pre = acc[t // group, pl.ds(pl.multiple_of((t % group) * voxels, voxels), voxels), :]
            sigma = jax.nn.sigmoid(pre)
            out_ref[t] = (ext[t].astype(jnp.float32) + pre * sigma).astype(out_ref.dtype)
            incoming = cot_ref[t].astype(jnp.float32)
            grad[t] = (incoming * sigma * (1.0 + pre * (1.0 - sigma))).astype(grad.dtype)
            return carry

        lax.fori_loop(0, tile_slots, finish, 0)
        for g in range(groups):
            part = grad[pl.ds(g * group, group)].reshape(rows, channels)
            turned_ref[:, pl.ds(g * rows, rows)] = part.astype(jnp.float32).T.astype(jnp.bfloat16)
        saves += [
            pltpu.make_async_copy(out_ref, out_hbm, sems.at[3]),
            pltpu.make_async_copy(grad, grad_hbm, sems.at[4]),
            pltpu.make_async_copy(turned_ref, turned_hbm, sems.at[5]),
        ]
        for save in saves[1:]:
            save.start()
        write_half(
            table_ref, half_ref[0], ext, turned_ref, half_out, half_hbm, sems.at[directions + 6], scale
        )
        for save in saves:
            save.wait()

    flops = 3 * offset_count * tile_slots * voxels * channels * channels
    out_shape = [
        jax.ShapeDtypeStruct(tiles.shape, jnp.bfloat16),
        jax.ShapeDtypeStruct(tiles.shape, jnp.bfloat16),
        jax.ShapeDtypeStruct((channels, tile_slots * voxels), jnp.bfloat16),
        jax.ShapeDtypeStruct((empty + 1, voxels, channels), jnp.bfloat16),
        jax.ShapeDtypeStruct((offset_count, channels // 2, channels), jnp.float32),
    ]
    return pl.pallas_call(
        kernel,
        out_shape=out_shape,
        in_specs=[SMEM, SMEM, HBM] + [ANY] * directions + [HBM, HBM, ANY],
        out_specs=[HBM] * 5,
        scratch_shapes=[
            pltpu.VMEM(weights.shape, jnp.bfloat16),
            pltpu.VMEM(tiles.shape, jnp.bfloat16),
        ]
        + [pltpu.VMEM(one.shape, one.dtype) for one in out_shape]
        + [
            pltpu.VMEM((groups, rows, channels), jnp.float32),
            pltpu.SemaphoreType.DMA((directions + 7,)),
            pltpu.SemaphoreType.DMA((offset_count // deep,)),
        ],
        compiler_params=pltpu.CompilerParams(vmem_limit_bytes=60 * MIB),
        cost_estimate=pl.CostEstimate(flops=flops, bytes_accessed=20 * MIB, transcendentals=0),
        name="forward_and_terms",
    )(table, half, tiles, *halos, weights, cotangent, after)


def weight_terms(table, half, ext, turned, offset_count, scale):
    channels = ext.shape[2]

    def kernel(table_ref, half_ref, ext_hbm, turned_hbm, out_hbm, ext_ref, turned_ref, out_ref, sems):
        copies = [pltpu.make_async_copy(turned_hbm, turned_ref, sems.at[0])]
        slots = ext_ref.shape[0]
        for n in range(4):
            part = pl.ds(n * slots // 4, (n + 1) * slots // 4 - n * slots // 4)
            copies.append(pltpu.make_async_copy(ext_hbm.at[part], ext_ref.at[part], sems.at[n + 1]))
        for copy in copies:
            copy.start()
        for copy in copies:
            copy.wait()
        write_half(table_ref, half_ref[0], ext_ref, turned_ref, out_ref, out_hbm, sems.at[5], scale)

    flops = offset_count * turned.shape[1] * channels * channels
    out_shape = jax.ShapeDtypeStruct((offset_count, channels // 2, channels), jnp.float32)
    return pl.pallas_call(
        kernel,
        out_shape=out_shape,
        in_specs=[SMEM, SMEM, HBM, HBM],
        out_specs=HBM,
        scratch_shapes=[
            pltpu.VMEM(ext.shape, ext.dtype),
            pltpu.VMEM(turned.shape, turned.dtype),
            pltpu.VMEM(out_shape.shape, out_shape.dtype),
            pltpu.SemaphoreType.DMA((6,)),
        ],
        compiler_params=pltpu.CompilerParams(vmem_limit_bytes=60 * MIB),
        cost_estimate=pl.CostEstimate(flops=flops, bytes_accessed=6 * MIB, transcendentals=0),
        name="weight_terms",
    )(table, half, ext, turned)


def input_grad(table, pre_grad, turned_weights, halo):
    tile_slots, voxels, channels = pre_grad.shape
    offset_count = turned_weights.shape[0]
    empty = tile_slots + len(DIRECTIONS) * halo
    group = chunk_of(tile_slots, 8)
    groups = tile_slots // group
    rows = group * voxels
    unroll = chunk_of(offset_count, 3)
    bundles = len(BUNDLES)

    def kernel(table_ref, grad_hbm, w_hbm, own_hbm, *refs):
        adjoints_hbm, refs = refs[:bundles], refs[bundles:]
        own_ref, adjoints, refs = refs[0], refs[1 : bundles + 1], refs[bundles + 1 :]
        even, odd, grad, w_ref, sems = refs
        copies = [
            pltpu.make_async_copy(grad_hbm, grad, sems.at[0]),
            pltpu.make_async_copy(w_hbm, w_ref, sems.at[1]),
        ]
        for copy in copies:
            copy.start()
        for one in (even, odd):
            one[...] = jnp.zeros_like(one)
        for copy in copies:
            copy.wait()

        def turn(step, carry):
            for j in range(unroll):
                k = step * unroll + j
                for g in range(groups):
                    back = jnp.dot(
                        grad[pl.ds(g * group, group)].reshape(rows, channels),
                        w_ref[k],
                        preferred_element_type=jnp.float32,
                    )
                    for t in range(group):
                        slot = table_ref[k, g * group + t]
                        sums = (even, odd)[t % 2]
                        sums[slot] += back[t * voxels : (t + 1) * voxels]
            return carry

        lax.fori_loop(0, offset_count // unroll, turn, 0)

        saves = []
        for n, (bundle, adjoint) in enumerate(zip(BUNDLES, adjoints)):
            for m, pair in enumerate(bundle):
                for h in range(halo):
                    slot = tile_slots + DIRECTIONS.index(pair) * halo + h
                    adjoint[m * halo + h] = (even[slot] + odd[slot]).astype(jnp.bfloat16)
            saves.append(pltpu.make_async_copy(adjoint, adjoints_hbm[n], sems.at[n + 2]))
            saves[-1].start()

        def own(t, carry):
            own_ref[t] = even[t] + odd[t]
            return carry

        half = tile_slots // 2
        for n in range(2):
            lax.fori_loop(n * half, (n + 1) * half, own, 0)
            part = pl.ds(n * half, half)
            saves.append(
                pltpu.make_async_copy(own_ref.at[part], own_hbm.at[part], sems.at[bundles + 2 + n])
            )
            saves[-1].start()
        for save in saves:
            save.wait()

    flops = 2 * offset_count * tile_slots * voxels * channels * channels
    out_shape = [jax.ShapeDtypeStruct(pre_grad.shape, jnp.float32)] + [
        jax.ShapeDtypeStruct((len(bundle) * halo, voxels, channels), jnp.bfloat16)
        for bundle in BUNDLES
    ]
    return pl.pallas_call(
        kernel,
        out_shape=out_shape,
        in_specs=[SMEM, HBM, HBM],
        out_specs=[HBM] * (bundles + 1),
        scratch_shapes=[pltpu.VMEM(one.shape, one.dtype) for one in out_shape]
        + [pltpu.VMEM((empty + 1, voxels, channels), jnp.float32)] * 2
        + [
            pltpu.VMEM(pre_grad.shape, jnp.bfloat16),
            pltpu.VMEM(turned_weights.shape, jnp.bfloat16),
            pltpu.SemaphoreType.DMA((bundles + 4,)),
        ],
        compiler_params=pltpu.CompilerParams(vmem_limit_bytes=60 * MIB),
        cost_estimate=pl.CostEstimate(flops=flops, bytes_accessed=12 * MIB, transcendentals=0),
        name="input_grad",
    )(table, pre_grad, turned_weights)


def to_other_core(x):
    return lax.ppermute(x, "core", [(0, 1), (1, 0)])


def ring(axis):
    size = lax.axis_size(axis)

    def move(x, by):
        return lax.ppermute(x, axis, [(i, (i + by) % size) for i in range(size)])

    return size, lax.axis_index(axis), move


def given_out(terms, ring):
    size, place, _ = ring
    parts = []
    for s in range(size):
        blocks = [
            lax.dynamic_index_in_dim(
                one.reshape(size, one.shape[0] // size, one.shape[1]), (place + s) % size, keepdims=False
            )
            for one in terms
        ]
        parts.append(sum(blocks[1:], blocks[0]))
    return parts[0], [one.astype(jnp.bfloat16) for one in parts[1:]]


def handed(parts, ring):
    return [ring[2](one, s + 1) for s, one in enumerate(parts)]


def added(mine, arrived):
    for one in arrived:
        mine = mine + one.astype(jnp.float32)
    return mine


def fetched(piece, ring):
    return [ring[2](piece, -s) for s in range(1, ring[0])]


def in_order(piece, others, ring):
    size, place, _ = ring
    whole = jnp.zeros((size,) + piece.shape, piece.dtype)
    for s, one in enumerate([piece, *others]):
        whole = lax.dynamic_update_index_in_dim(whole, one, (place + s) % size, 0)
    return whole.reshape(size * piece.shape[0], piece.shape[1])


def together(*values):
    return lax.optimization_barrier(values)


def widen(place, half, whole):
    rows, channels = half.shape
    turns = chunk_of(rows // 16, 3)
    step = rows // turns

    def kernel(place_ref, half_ref, *refs):
        refs[-1][...] = half_ref[...].astype(jnp.float32)

    given = [] if whole is None else [whole]
    return pl.pallas_call(
        kernel,
        grid_spec=pltpu.PrefetchScalarGridSpec(
            num_scalar_prefetch=1,
            grid=(turns,),
            in_specs=[pl.BlockSpec((step, channels), lambda i, place: (i, 0))] + [ANY] * len(given),
            out_specs=pl.BlockSpec((step, channels), lambda i, place: (place[0] * turns + i, 0)),
        ),
        out_shape=jax.ShapeDtypeStruct((2 * rows, channels), jnp.float32),
        input_output_aliases={2: 0} if given else {},
        compiler_params=pltpu.CompilerParams(vmem_limit_bytes=24 * MIB),
        name="widen",
    )(place, half, *given)


def combine(lists, own, cotangent, returned):
    halo = lists.shape[1]
    tile_slots = own.shape[0]
    arrays = [array for array, _ in returned]

    def kernel(lists_ref, own_ref, cot_ref, *refs):
        out_ref, acc = refs[len(arrays) :]

        def start(t, carry):
            acc[t] = own_ref[t] + cot_ref[t].astype(jnp.float32)
            return carry

        lax.fori_loop(0, tile_slots, start, 0)
        for ref, (_, pairs) in zip(refs, returned):
            for n, pair in enumerate(pairs):
                for h in range(halo):
                    tile = lists_ref[DIRECTIONS.index(pair), h]
                    acc[tile] += ref[n * halo + h].astype(jnp.float32)

        def finish(t, carry):
            out_ref[t] = acc[t].astype(out_ref.dtype)
            return carry

        lax.fori_loop(0, tile_slots, finish, 0)

    return pl.pallas_call(
        kernel,
        out_shape=jax.ShapeDtypeStruct(own.shape, jnp.bfloat16),
        in_specs=[SMEM] + [VMEM] * (len(arrays) + 2),
        out_specs=VMEM,
        scratch_shapes=[pltpu.VMEM(own.shape, jnp.float32)],
        compiler_params=pltpu.CompilerParams(vmem_limit_bytes=16 * MIB),
        name="combine",
    )(lists, own, cotangent, *arrays)


def shards(
    features, weights, cotangent, send_lists, block_offset, block_input, block_output, block_count
):
    tiles = features[0, 0]
    incoming = cotangent[0, 0]
    lists = send_lists[0, 0]
    tile_slots, voxels, channels = tiles.shape
    directions, halo = lists.shape
    device_total = x_size() * lax.axis_size("gy")
    scale = 1.0 / math.sqrt(voxels * tile_slots * device_total)
    offset_count = weights.shape[0]
    core = lax.axis_index("core").astype(jnp.int32)[None]

    packets = pack(tiles, lists)
    table = source_table(
        block_offset[0, 0],
        block_input[0, 0].T,
        block_output[0, 0].T,
        block_count[0],
        offset_count,
        tile_slots,
        tile_slots + directions * halo,
        packets[0],
    )
    turned_weights = turn_weights(weights, table)
    order = [
        DIRECTIONS.index(pair)
        for pair in ((-1, -1), (1, 1), (-1, 0), (1, 0), (-1, 1), (1, -1), (0, -1), (0, 1))
    ]
    arrived = {d: travel(packets[d], *DIRECTIONS[d]) for d in order}
    halos = [arrived[d] for d in range(directions)]
    out_features, pre_grad, turned, ext, send = forward_and_terms(
        table, 1 - core, tiles, halos, weights, incoming, scale, turned_weights
    )
    received = to_other_core(send)
    keep = weight_terms(table, core, ext, turned, offset_count, scale)
    levels = ring("gy"), ring("gz")
    mine, out = given_out([keep.reshape(-1, channels), received.reshape(-1, channels)], levels[0])

    pre_grad, *out = together(pre_grad, *out)
    moved = handed(out, levels[0])
    own, low, high, low_both, high_both, behind, ahead = input_grad(table, pre_grad, turned_weights, halo)
    low, high = travel(low, 0, 1), travel(high, 0, -1)
    low, high, *moved = together(low, high, *moved)
    low_both, high_both = travel(low_both, 0, 1), travel(high_both, 0, -1)

    mine, out = given_out([added(mine, moved)], levels[1])
    piece = added(mine, handed(out, levels[1])).astype(jnp.bfloat16)
    low_both, piece = together(low_both, piece)
    piece = in_order(piece, fetched(piece, levels[1]), levels[1])
    high_both, piece = together(high_both, piece)
    behind = jnp.concatenate([behind, low_both[:halo], high_both[:halo]])
    ahead = jnp.concatenate([ahead, low_both[halo:], high_both[halo:]])
    behind, ahead = travel(behind, 1, 0), travel(ahead, -1, 0)
    own_half = in_order(piece, fetched(piece, levels[0]), levels[0])
    behind, ahead, own_half = together(behind, ahead, own_half)
    feat_grad = combine(
        lists,
        own,
        incoming,
        [
            (low, ((0, -1),)),
            (high, ((0, 1),)),
            (behind, ((-1, 0), (-1, -1), (-1, 1))),
            (ahead, ((1, 0), (1, -1), (1, 1))),
        ],
    )
    other_half = to_other_core(own_half)
    weight_grad = widen(1 - core, other_half, widen(core, own_half, None)).reshape(weights.shape)
    return (out_features[None, None], feat_grad[None, None], weight_grad)


def solution(mesh):
    size_x, size_y = mesh.devices.shape
    split = Mesh(mesh.devices.reshape(size_x // 2, 2, size_y), ("gz", "core", "gy"))
    place = P(("gz", "core"), "gy")
    return jax.shard_map(
        shards,
        mesh=split,
        in_specs=(place, P(), place, place, place, place, place, place),
        out_specs=(place, place, P()),
        check_vma=False,
    )
```

```python
import math

import jax
import jax.numpy as jnp
from jax import lax
from jax.experimental import pallas as pl
from jax.experimental.pallas import tpu as pltpu
from jax.sharding import Mesh
from jax.sharding import PartitionSpec as P

DIRECTIONS = ((-1, -1), (-1, 0), (-1, 1), (0, -1), (0, 1), (1, -1), (1, 0), (1, 1))
BUNDLES = (
    ((0, -1),),
    ((0, 1),),
    ((-1, -1), (1, -1)),
    ((-1, 1), (1, 1)),
    ((-1, 0),),
    ((1, 0),),
)
MIB = 1024 * 1024
ANY = pl.BlockSpec(memory_space=pl.ANY)
HBM = pl.BlockSpec(memory_space=pltpu.HBM)
VMEM = pl.BlockSpec(memory_space=pltpu.VMEM)
SMEM = pl.BlockSpec(memory_space=pltpu.SMEM)


def chunk_of(size, wanted):
    return max(c for c in range(1, wanted + 1) if size % c == 0)


def x_size():
    return lax.axis_size("gz") * lax.axis_size("core")


def travel(packet, step_x, step_y):
    size_x, size_y = x_size(), lax.axis_size("gy")
    pairs = [
        (i * size_y + j, (i + step_x) * size_y + j + step_y)
        for i in range(size_x)
        for j in range(size_y)
        if 0 <= i + step_x < size_x and 0 <= j + step_y < size_y
    ]
    return lax.ppermute(packet, ("gz", "core", "gy"), pairs)


def pack(tiles, lists):
    halo = lists.shape[1]
    _, voxels, channels = tiles.shape

    def kernel(lists_ref, tiles_ref, *packets):
        for d, packet in enumerate(packets):
            for h in range(halo):
                packet[h] = tiles_ref[lists_ref[d, h]]

    return pl.pallas_call(
        kernel,
        out_shape=[jax.ShapeDtypeStruct((halo, voxels, channels), tiles.dtype)] * len(DIRECTIONS),
        in_specs=[SMEM, VMEM],
        out_specs=[VMEM] * len(DIRECTIONS),
        compiler_params=pltpu.CompilerParams(vmem_limit_bytes=16 * MIB),
        name="pack",
    )(lists, tiles)


def source_table(offsets, inputs, outputs, count, offset_count, tile_slots, empty, after):
    rows, blocks = inputs.shape

    def kernel(offsets_ref, inputs_ref, outputs_ref, count_ref, _, table_ref):
        def clear(k, carry):
            for t in range(tile_slots):
                table_ref[k, t] = empty
            return carry

        lax.fori_loop(0, offset_count, clear, 0)

        def block(n, carry):
            k = offsets_ref[n]
            for q in range(rows):
                table_ref[k, outputs_ref[q, n]] = inputs_ref[q, n]
            return carry

        lax.fori_loop(0, jnp.minimum(count_ref[0], blocks), block, 0)

    return pl.pallas_call(
        kernel,
        out_shape=jax.ShapeDtypeStruct((offset_count, tile_slots + 1), jnp.int32),
        in_specs=[SMEM] * 4 + [ANY],
        out_specs=SMEM,
        cost_estimate=pl.CostEstimate(flops=4 * 10**9, bytes_accessed=MIB, transcendentals=0),
        name="source_table",
    )(offsets, inputs, outputs, count, after)


def gathered(table_ref, ext, k, first, count):
    return jnp.concatenate([ext[table_ref[k, first + t]] for t in range(count)], axis=0)


def write_half(table_ref, late, ext, turned_ref, out_ref, out_hbm, sem, scale):
    offset_count, part, _ = out_ref.shape
    tile_slots = table_ref.shape[1] - 1
    count = (offset_count + 1) // 2

    def turn(j, carry):
        k = late * (offset_count - count) + j
        terms = jnp.dot(
            turned_ref[...],
            gathered(table_ref, ext, k, 0, tile_slots),
            preferred_element_type=jnp.float32,
        )
        terms = terms.T * scale
        for b in range(2):
            place = 2 * k + b - late * offset_count

            @pl.when((place >= 0) & (place < offset_count))
            def _():
                out_ref[place] = terms[b * part : (b + 1) * part]
                pltpu.make_async_copy(out_ref.at[place], out_hbm.at[place], sem).start()

        return carry

    lax.fori_loop(0, count, turn, 0)
    pltpu.make_async_copy(out_ref, out_hbm, sem).wait()


def turn_weights(weights, after):
    def kernel(_, w_ref, out_ref):
        for k in range(w_ref.shape[0]):
            out_ref[k] = w_ref[k].astype(jnp.float32).T.astype(out_ref.dtype)

    offset_count, channels, _ = weights.shape
    step = chunk_of(offset_count, 3)
    spec = pl.BlockSpec((step, channels, channels), lambda k: (k, 0, 0))
    return pl.pallas_call(
        kernel,
        grid=(offset_count // step,),
        out_shape=jax.ShapeDtypeStruct(weights.shape, weights.dtype),
        in_specs=[SMEM, spec],
        out_specs=spec,
        compiler_params=pltpu.CompilerParams(vmem_limit_bytes=16 * MIB),
        cost_estimate=pl.CostEstimate(flops=8 * 10**9, bytes_accessed=7 * MIB, transcendentals=0),
        name="turn_weights",
    )(after, weights)


def forward_and_terms(table, half, tiles, order, halos, weights, cotangent, scale, after):
    tile_slots, voxels, channels = tiles.shape
    offset_count = weights.shape[0]
    directions, halo = len(halos), halos[0].shape[0]
    empty = tile_slots + directions * halo
    group = chunk_of(tile_slots, 8)
    groups = tile_slots // group
    rows = group * voxels
    deep = chunk_of(offset_count, 9)

    def kernel(table_ref, half_ref, tiles_ref, *refs):
        halo_refs, refs = refs[:directions], refs[directions:]
        w_hbm, cot_hbm, _, out_hbm, grad_hbm, turned_hbm, ext_hbm, half_hbm = refs[:8]
        w_ref, cot_ref, out_ref, grad, turned_ref, ext, half_out, acc, sems, w_sems = refs[8:]
        copies = [pltpu.make_async_copy(tiles_ref, ext.at[pl.ds(0, tile_slots)], sems.at[0])]
        for d, halo_ref in zip(order, halo_refs):
            place = ext.at[pl.ds(tile_slots + d * halo, halo)]
            copies.append(pltpu.make_async_copy(halo_ref, place, sems.at[d + 6]))

        def load_mats(step):
            part = pl.ds(step * deep, deep)
            return pltpu.make_async_copy(w_hbm.at[part], w_ref.at[part], w_sems.at[step])

        load_cot = pltpu.make_async_copy(cot_hbm, cot_ref, sems.at[1])
        for copy in copies + [load_mats(n) for n in range(offset_count // deep)] + [load_cot]:
            copy.start()
        ext[empty] = jnp.zeros((voxels, channels), ext.dtype)
        acc[...] = jnp.zeros_like(acc)
        for copy in copies:
            copy.wait()
        saves = [pltpu.make_async_copy(ext, ext_hbm, sems.at[2])]
        saves[0].start()

        def turn(step, carry):
            load_mats(step).wait()
            mats = w_ref[pl.ds(step * deep, deep)].reshape(deep * channels, channels)
            for g in range(groups):
                lhs = jnp.concatenate(
                    [
                        gathered(table_ref, ext, step * deep + j, g * group, group)
                        for j in range(deep)
                    ],
                    axis=1,
                )
                acc[g] += jnp.dot(lhs, mats, preferred_element_type=jnp.float32)
            return carry

        lax.fori_loop(0, offset_count // deep, turn, 0)
        load_cot.wait()

        def finish(t, carry):
            pre = acc[t // group, pl.ds(pl.multiple_of((t % group) * voxels, voxels), voxels), :]
            sigma = jax.nn.sigmoid(pre)
            out_ref[t] = (ext[t].astype(jnp.float32) + pre * sigma).astype(out_ref.dtype)
            incoming = cot_ref[t].astype(jnp.float32)
            grad[t] = (incoming * sigma * (1.0 + pre * (1.0 - sigma))).astype(grad.dtype)
            return carry

        lax.fori_loop(0, tile_slots, finish, 0)
        for g in range(groups):
            part = grad[pl.ds(g * group, group)].reshape(rows, channels)
            turned_ref[:, pl.ds(g * rows, rows)] = part.astype(jnp.float32).T.astype(jnp.bfloat16)
        saves += [
            pltpu.make_async_copy(out_ref, out_hbm, sems.at[3]),
            pltpu.make_async_copy(grad, grad_hbm, sems.at[4]),
            pltpu.make_async_copy(turned_ref, turned_hbm, sems.at[5]),
        ]
        for save in saves[1:]:
            save.start()
        write_half(
            table_ref, half_ref[0], ext, turned_ref, half_out, half_hbm, sems.at[directions + 6], scale
        )
        for save in saves:
            save.wait()

    flops = 3 * offset_count * tile_slots * voxels * channels * channels
    out_shape = [
        jax.ShapeDtypeStruct(tiles.shape, jnp.bfloat16),
        jax.ShapeDtypeStruct(tiles.shape, jnp.bfloat16),
        jax.ShapeDtypeStruct((channels, tile_slots * voxels), jnp.bfloat16),
        jax.ShapeDtypeStruct((empty + 1, voxels, channels), jnp.bfloat16),
        jax.ShapeDtypeStruct((offset_count, channels // 2, channels), jnp.float32),
    ]
    return pl.pallas_call(
        kernel,
        out_shape=out_shape,
        in_specs=[SMEM, SMEM, HBM] + [ANY] * directions + [HBM, HBM, ANY],
        out_specs=[HBM] * 5,
        scratch_shapes=[
            pltpu.VMEM(weights.shape, jnp.bfloat16),
            pltpu.VMEM(tiles.shape, jnp.bfloat16),
        ]
        + [pltpu.VMEM(one.shape, one.dtype) for one in out_shape]
        + [
            pltpu.VMEM((groups, rows, channels), jnp.float32),
            pltpu.SemaphoreType.DMA((directions + 7,)),
            pltpu.SemaphoreType.DMA((offset_count // deep,)),
        ],
        compiler_params=pltpu.CompilerParams(vmem_limit_bytes=60 * MIB),
        cost_estimate=pl.CostEstimate(flops=flops, bytes_accessed=20 * MIB, transcendentals=0),
        name="forward_and_terms",
    )(table, half, tiles, *halos, weights, cotangent, after)


def weight_terms(table, half, ext, turned, offset_count, scale):
    channels = ext.shape[2]

    def kernel(table_ref, half_ref, ext_hbm, turned_hbm, out_hbm, ext_ref, turned_ref, out_ref, sems):
        copies = [pltpu.make_async_copy(turned_hbm, turned_ref, sems.at[0])]
        slots = ext_ref.shape[0]
        for n in range(4):
            part = pl.ds(n * slots // 4, (n + 1) * slots // 4 - n * slots // 4)
            copies.append(pltpu.make_async_copy(ext_hbm.at[part], ext_ref.at[part], sems.at[n + 1]))
        for copy in copies:
            copy.start()
        for copy in copies:
            copy.wait()
        write_half(table_ref, half_ref[0], ext_ref, turned_ref, out_ref, out_hbm, sems.at[5], scale)

    flops = offset_count * turned.shape[1] * channels * channels
    out_shape = jax.ShapeDtypeStruct((offset_count, channels // 2, channels), jnp.float32)
    return pl.pallas_call(
        kernel,
        out_shape=out_shape,
        in_specs=[SMEM, SMEM, HBM, HBM],
        out_specs=HBM,
        scratch_shapes=[
            pltpu.VMEM(ext.shape, ext.dtype),
            pltpu.VMEM(turned.shape, turned.dtype),
            pltpu.VMEM(out_shape.shape, out_shape.dtype),
            pltpu.SemaphoreType.DMA((6,)),
        ],
        compiler_params=pltpu.CompilerParams(vmem_limit_bytes=60 * MIB),
        cost_estimate=pl.CostEstimate(flops=flops, bytes_accessed=6 * MIB, transcendentals=0),
        name="weight_terms",
    )(table, half, ext, turned)


def input_grad(table, pre_grad, turned_weights, halo):
    tile_slots, voxels, channels = pre_grad.shape
    offset_count = turned_weights.shape[0]
    empty = tile_slots + len(DIRECTIONS) * halo
    group = chunk_of(tile_slots, 8)
    groups = tile_slots // group
    rows = group * voxels
    unroll = chunk_of(offset_count, 3)
    bundles = len(BUNDLES)

    def kernel(table_ref, grad_hbm, w_hbm, own_hbm, *refs):
        adjoints_hbm, refs = refs[:bundles], refs[bundles:]
        own_ref, adjoints, refs = refs[0], refs[1 : bundles + 1], refs[bundles + 1 :]
        even, odd, grad, w_ref, sems = refs
        copies = [
            pltpu.make_async_copy(grad_hbm, grad, sems.at[0]),
            pltpu.make_async_copy(w_hbm, w_ref, sems.at[1]),
        ]
        for copy in copies:
            copy.start()
        for one in (even, odd):
            one[...] = jnp.zeros_like(one)
        for copy in copies:
            copy.wait()

        def turn(step, carry):
            for j in range(unroll):
                k = step * unroll + j
                for g in range(groups):
                    back = jnp.dot(
                        grad[pl.ds(g * group, group)].reshape(rows, channels),
                        w_ref[k],
                        preferred_element_type=jnp.float32,
                    )
                    for t in range(group):
                        slot = table_ref[k, g * group + t]
                        sums = (even, odd)[t % 2]
                        sums[slot] += back[t * voxels : (t + 1) * voxels]
            return carry

        lax.fori_loop(0, offset_count // unroll, turn, 0)

        saves = []
        for n, (bundle, adjoint) in enumerate(zip(BUNDLES, adjoints)):
            for m, pair in enumerate(bundle):
                for h in range(halo):
                    slot = tile_slots + DIRECTIONS.index(pair) * halo + h
                    adjoint[m * halo + h] = (even[slot] + odd[slot]).astype(jnp.bfloat16)
            saves.append(pltpu.make_async_copy(adjoint, adjoints_hbm[n], sems.at[n + 2]))
            saves[-1].start()

        def own(t, carry):
            own_ref[t] = even[t] + odd[t]
            return carry

        half = tile_slots // 2
        for n in range(2):
            lax.fori_loop(n * half, (n + 1) * half, own, 0)
            part = pl.ds(n * half, half)
            saves.append(
                pltpu.make_async_copy(own_ref.at[part], own_hbm.at[part], sems.at[bundles + 2 + n])
            )
            saves[-1].start()
        for save in saves:
            save.wait()

    flops = 2 * offset_count * tile_slots * voxels * channels * channels
    out_shape = [jax.ShapeDtypeStruct(pre_grad.shape, jnp.float32)] + [
        jax.ShapeDtypeStruct((len(bundle) * halo, voxels, channels), jnp.bfloat16)
        for bundle in BUNDLES
    ]
    return pl.pallas_call(
        kernel,
        out_shape=out_shape,
        in_specs=[SMEM, HBM, HBM],
        out_specs=[HBM] * (bundles + 1),
        scratch_shapes=[pltpu.VMEM(one.shape, one.dtype) for one in out_shape]
        + [pltpu.VMEM((empty + 1, voxels, channels), jnp.float32)] * 2
        + [
            pltpu.VMEM(pre_grad.shape, jnp.bfloat16),
            pltpu.VMEM(turned_weights.shape, jnp.bfloat16),
            pltpu.SemaphoreType.DMA((bundles + 4,)),
        ],
        compiler_params=pltpu.CompilerParams(vmem_limit_bytes=60 * MIB),
        cost_estimate=pl.CostEstimate(flops=flops, bytes_accessed=12 * MIB, transcendentals=0),
        name="input_grad",
    )(table, pre_grad, turned_weights)


def to_other_core(x):
    return lax.ppermute(x, "core", [(0, 1), (1, 0)])


def ring(axis):
    size = lax.axis_size(axis)

    def move(x, by):
        return lax.ppermute(x, axis, [(i, (i + by) % size) for i in range(size)])

    return size, lax.axis_index(axis), move


def given_out(terms, ring):
    size, place, _ = ring
    parts = []
    for s in range(size):
        blocks = [
            lax.dynamic_index_in_dim(
                one.reshape(size, one.shape[0] // size, one.shape[1]), (place + s) % size, keepdims=False
            )
            for one in terms
        ]
        parts.append(sum(blocks[1:], blocks[0]))
    return parts[0], [one.astype(jnp.bfloat16) for one in parts[1:]]


def handed(parts, ring):
    return [ring[2](one, s + 1) for s, one in enumerate(parts)]


def added(mine, arrived):
    for one in arrived:
        mine = mine + one.astype(jnp.float32)
    return mine


def fetched(piece, ring):
    return [ring[2](piece, -s) for s in range(1, ring[0])]


def in_order(piece, others, ring):
    size, place, _ = ring
    whole = jnp.zeros((size,) + piece.shape, piece.dtype)
    for s, one in enumerate([piece, *others]):
        whole = lax.dynamic_update_index_in_dim(whole, one, (place + s) % size, 0)
    return whole.reshape(size * piece.shape[0], piece.shape[1])


def together(*values):
    return lax.optimization_barrier(values)


def widen(place, half, whole):
    rows, channels = half.shape
    turns = chunk_of(rows // 16, 3)
    step = rows // turns

    def kernel(place_ref, half_ref, *refs):
        refs[-1][...] = half_ref[...].astype(jnp.float32)

    given = [] if whole is None else [whole]
    return pl.pallas_call(
        kernel,
        grid_spec=pltpu.PrefetchScalarGridSpec(
            num_scalar_prefetch=1,
            grid=(turns,),
            in_specs=[pl.BlockSpec((step, channels), lambda i, place: (i, 0))] + [ANY] * len(given),
            out_specs=pl.BlockSpec((step, channels), lambda i, place: (place[0] * turns + i, 0)),
        ),
        out_shape=jax.ShapeDtypeStruct((2 * rows, channels), jnp.float32),
        input_output_aliases={2: 0} if given else {},
        compiler_params=pltpu.CompilerParams(vmem_limit_bytes=24 * MIB),
        name="widen",
    )(place, half, *given)


def combine(lists, own, cotangent, returned):
    halo = lists.shape[1]
    tile_slots = own.shape[0]
    arrays = [array for array, _ in returned]

    def kernel(lists_ref, own_ref, cot_ref, *refs):
        out_ref, acc = refs[len(arrays) :]

        def start(t, carry):
            acc[t] = own_ref[t] + cot_ref[t].astype(jnp.float32)
            return carry

        lax.fori_loop(0, tile_slots, start, 0)
        for ref, (_, pairs) in zip(refs, returned):
            for n, pair in enumerate(pairs):
                for h in range(halo):
                    tile = lists_ref[DIRECTIONS.index(pair), h]
                    acc[tile] += ref[n * halo + h].astype(jnp.float32)

        def finish(t, carry):
            out_ref[t] = acc[t].astype(out_ref.dtype)
            return carry

        lax.fori_loop(0, tile_slots, finish, 0)

    return pl.pallas_call(
        kernel,
        out_shape=jax.ShapeDtypeStruct(own.shape, jnp.bfloat16),
        in_specs=[SMEM] + [VMEM] * (len(arrays) + 2),
        out_specs=VMEM,
        scratch_shapes=[pltpu.VMEM(own.shape, jnp.float32)],
        compiler_params=pltpu.CompilerParams(vmem_limit_bytes=16 * MIB),
        name="combine",
    )(lists, own, cotangent, *arrays)


def shards(
    features, weights, cotangent, send_lists, block_offset, block_input, block_output, block_count
):
    tiles = features[0, 0]
    incoming = cotangent[0, 0]
    lists = send_lists[0, 0]
    tile_slots, voxels, channels = tiles.shape
    directions, halo = lists.shape
    device_total = x_size() * lax.axis_size("gy")
    scale = 1.0 / math.sqrt(voxels * tile_slots * device_total)
    offset_count = weights.shape[0]
    core = lax.axis_index("core").astype(jnp.int32)[None]

    packets = pack(tiles, lists)
    order = [
        DIRECTIONS.index(pair)
        for pair in ((-1, 0), (1, 0), (-1, -1), (1, 1), (-1, 1), (1, -1), (0, -1), (0, 1))
    ]
    arrived = {d: travel(packets[d], *DIRECTIONS[d]) for d in order}
    table = source_table(
        block_offset[0, 0],
        block_input[0, 0].T,
        block_output[0, 0].T,
        block_count[0],
        offset_count,
        tile_slots,
        tile_slots + directions * halo,
        arrived[order[0]],
    )
    turned_weights = turn_weights(weights, table)
    halos = [arrived[d] for d in order]
    out_features, pre_grad, turned, ext, send = forward_and_terms(
        table, 1 - core, tiles, order, halos, weights, incoming, scale, turned_weights
    )
    received = to_other_core(send)
    keep = weight_terms(table, core, ext, turned, offset_count, scale)
    levels = ring("gy"), ring("gz")
    mine, out = given_out([keep.reshape(-1, channels), received.reshape(-1, channels)], levels[0])

    pre_grad, *out = together(pre_grad, *out)
    moved = handed(out, levels[0])
    own, low, high, low_both, high_both, behind, ahead = input_grad(table, pre_grad, turned_weights, halo)
    low, high = travel(low, 0, 1), travel(high, 0, -1)
    low, high, *moved = together(low, high, *moved)
    low_both, high_both = travel(low_both, 0, 1), travel(high_both, 0, -1)

    mine, out = given_out([added(mine, moved)], levels[1])
    piece = added(mine, handed(out, levels[1])).astype(jnp.bfloat16)
    low_both, piece = together(low_both, piece)
    piece = in_order(piece, fetched(piece, levels[1]), levels[1])
    high_both, piece = together(high_both, piece)
    behind = jnp.concatenate([behind, low_both[:halo], high_both[:halo]])
    ahead = jnp.concatenate([ahead, low_both[halo:], high_both[halo:]])
    behind, ahead = travel(behind, 1, 0), travel(ahead, -1, 0)
    own_half = in_order(piece, fetched(piece, levels[0]), levels[0])
    behind, ahead, own_half = together(behind, ahead, own_half)
    feat_grad = combine(
        lists,
        own,
        incoming,
        [
            (low, ((0, -1),)),
            (high, ((0, 1),)),
            (behind, ((-1, 0), (-1, -1), (-1, 1))),
            (ahead, ((1, 0), (1, -1), (1, 1))),
        ],
    )
    other_half = to_other_core(own_half)
    weight_grad = widen(1 - core, other_half, widen(core, own_half, None)).reshape(weights.shape)
    return (out_features[None, None], feat_grad[None, None], weight_grad)


def solution(mesh):
    size_x, size_y = mesh.devices.shape
    split = Mesh(mesh.devices.reshape(size_x // 2, 2, size_y), ("gz", "core", "gy"))
    place = P(("gz", "core"), "gy")
    return jax.shard_map(
        shards,
        mesh=split,
        in_specs=(place, P(), place, place, place, place, place, place),
        out_specs=(place, place, P()),
        check_vma=False,
    )
```

```python
import math

import jax
import jax.numpy as jnp
from jax import lax
from jax.experimental import pallas as pl
from jax.experimental.pallas import tpu as pltpu
from jax.sharding import Mesh
from jax.sharding import PartitionSpec as P

DIRECTIONS = ((-1, -1), (-1, 0), (-1, 1), (0, -1), (0, 1), (1, -1), (1, 0), (1, 1))
BUNDLES = (
    ((0, -1),),
    ((0, 1),),
    ((-1, -1), (1, -1)),
    ((-1, 1), (1, 1)),
    ((-1, 0),),
    ((1, 0),),
)
MIB = 1024 * 1024
ANY = pl.BlockSpec(memory_space=pl.ANY)
HBM = pl.BlockSpec(memory_space=pltpu.HBM)
VMEM = pl.BlockSpec(memory_space=pltpu.VMEM)
SMEM = pl.BlockSpec(memory_space=pltpu.SMEM)


def chunk_of(size, wanted):
    return max(c for c in range(1, wanted + 1) if size % c == 0)


def x_size():
    return lax.axis_size("gz") * lax.axis_size("core")


def travel(packet, step_x, step_y):
    size_x, size_y = x_size(), lax.axis_size("gy")
    pairs = [
        (i * size_y + j, (i + step_x) * size_y + j + step_y)
        for i in range(size_x)
        for j in range(size_y)
        if 0 <= i + step_x < size_x and 0 <= j + step_y < size_y
    ]
    return lax.ppermute(packet, ("gz", "core", "gy"), pairs)


def pack(tiles, lists):
    halo = lists.shape[1]
    _, voxels, channels = tiles.shape

    def kernel(lists_ref, tiles_ref, *packets):
        for d, packet in enumerate(packets):
            for h in range(halo):
                packet[h] = tiles_ref[lists_ref[d, h]]

    return pl.pallas_call(
        kernel,
        out_shape=[jax.ShapeDtypeStruct((halo, voxels, channels), tiles.dtype)] * len(DIRECTIONS),
        in_specs=[SMEM, VMEM],
        out_specs=[VMEM] * len(DIRECTIONS),
        compiler_params=pltpu.CompilerParams(vmem_limit_bytes=16 * MIB),
        name="pack",
    )(lists, tiles)


def source_table(offsets, inputs, outputs, count, offset_count, tile_slots, empty, after):
    rows, blocks = inputs.shape

    def kernel(offsets_ref, inputs_ref, outputs_ref, count_ref, _, table_ref):
        def clear(k, carry):
            for t in range(tile_slots):
                table_ref[k, t] = empty
            return carry

        lax.fori_loop(0, offset_count, clear, 0)

        def block(n, carry):
            k = offsets_ref[n]
            for q in range(rows):
                table_ref[k, outputs_ref[q, n]] = inputs_ref[q, n]
            return carry

        lax.fori_loop(0, jnp.minimum(count_ref[0], blocks), block, 0)

    return pl.pallas_call(
        kernel,
        out_shape=jax.ShapeDtypeStruct((offset_count, tile_slots + 1), jnp.int32),
        in_specs=[SMEM] * 4 + [ANY],
        out_specs=SMEM,
        cost_estimate=pl.CostEstimate(flops=4 * 10**9, bytes_accessed=MIB, transcendentals=0),
        name="source_table",
    )(offsets, inputs, outputs, count, after)


def gathered(table_ref, ext, k, first, count):
    return jnp.concatenate([ext[table_ref[k, first + t]] for t in range(count)], axis=0)


def write_half(table_ref, late, ext, turned_ref, out_ref, out_hbm, sem, scale):
    offset_count, part, _ = out_ref.shape
    tile_slots = table_ref.shape[1] - 1
    count = (offset_count + 1) // 2

    def turn(j, carry):
        k = late * (offset_count - count) + j
        terms = jnp.dot(
            turned_ref[...],
            gathered(table_ref, ext, k, 0, tile_slots),
            preferred_element_type=jnp.float32,
        )
        terms = terms.T * scale
        for b in range(2):
            place = 2 * k + b - late * offset_count

            @pl.when((place >= 0) & (place < offset_count))
            def _():
                out_ref[place] = terms[b * part : (b + 1) * part]
                pltpu.make_async_copy(out_ref.at[place], out_hbm.at[place], sem).start()

        return carry

    lax.fori_loop(0, count, turn, 0)
    pltpu.make_async_copy(out_ref, out_hbm, sem).wait()


def turn_weights(weights, after):
    def kernel(_, w_ref, out_ref):
        for k in range(w_ref.shape[0]):
            out_ref[k] = w_ref[k].astype(jnp.float32).T.astype(out_ref.dtype)

    offset_count, channels, _ = weights.shape
    step = chunk_of(offset_count, 3)
    spec = pl.BlockSpec((step, channels, channels), lambda k: (k, 0, 0))
    return pl.pallas_call(
        kernel,
        grid=(offset_count // step,),
        out_shape=jax.ShapeDtypeStruct(weights.shape, weights.dtype),
        in_specs=[SMEM, spec],
        out_specs=spec,
        compiler_params=pltpu.CompilerParams(vmem_limit_bytes=16 * MIB),
        cost_estimate=pl.CostEstimate(flops=8 * 10**9, bytes_accessed=7 * MIB, transcendentals=0),
        name="turn_weights",
    )(after, weights)


def forward_and_terms(table, half, tiles, halos, weights, cotangent, scale, after):
    tile_slots, voxels, channels = tiles.shape
    offset_count = weights.shape[0]
    directions, halo = len(halos), halos[0].shape[0]
    empty = tile_slots + directions * halo
    group = chunk_of(tile_slots, 8)
    groups = tile_slots // group
    rows = group * voxels
    deep = chunk_of(offset_count, 9)

    def kernel(table_ref, half_ref, tiles_ref, *refs):
        halo_refs, refs = refs[:directions], refs[directions:]
        w_hbm, cot_hbm, _, out_hbm, grad_hbm, turned_hbm, ext_hbm, half_hbm = refs[:8]
        w_ref, cot_ref, out_ref, grad, turned_ref, ext, half_out, acc, sems, w_sems = refs[8:]
        copies = [pltpu.make_async_copy(tiles_ref, ext.at[pl.ds(0, tile_slots)], sems.at[0])]
        for d, halo_ref in enumerate(halo_refs):
            place = ext.at[pl.ds(tile_slots + d * halo, halo)]
            copies.append(pltpu.make_async_copy(halo_ref, place, sems.at[d + 6]))

        def load_mats(step):
            part = pl.ds(step * deep, deep)
            return pltpu.make_async_copy(w_hbm.at[part], w_ref.at[part], w_sems.at[step])

        load_cot = pltpu.make_async_copy(cot_hbm, cot_ref, sems.at[1])
        for copy in copies + [load_mats(n) for n in range(offset_count // deep)] + [load_cot]:
            copy.start()
        ext[empty] = jnp.zeros((voxels, channels), ext.dtype)
        acc[...] = jnp.zeros_like(acc)
        for copy in copies:
            copy.wait()
        saves = [pltpu.make_async_copy(ext, ext_hbm, sems.at[2])]
        saves[0].start()

        def turn(step, carry):
            load_mats(step).wait()
            mats = w_ref[pl.ds(step * deep, deep)].reshape(deep * channels, channels)
            for g in range(groups):
                lhs = jnp.concatenate(
                    [
                        gathered(table_ref, ext, step * deep + j, g * group, group)
                        for j in range(deep)
                    ],
                    axis=1,
                )
                acc[g] += jnp.dot(lhs, mats, preferred_element_type=jnp.float32)
            return carry

        lax.fori_loop(0, offset_count // deep, turn, 0)
        load_cot.wait()

        def finish(t, carry):
            pre = acc[t // group, pl.ds(pl.multiple_of((t % group) * voxels, voxels), voxels), :]
            sigma = jax.nn.sigmoid(pre)
            out_ref[t] = (ext[t].astype(jnp.float32) + pre * sigma).astype(out_ref.dtype)
            incoming = cot_ref[t].astype(jnp.float32)
            grad[t] = (incoming * sigma * (1.0 + pre * (1.0 - sigma))).astype(grad.dtype)
            return carry

        lax.fori_loop(0, tile_slots, finish, 0)
        for g in range(groups):
            part = grad[pl.ds(g * group, group)].reshape(rows, channels)
            turned_ref[:, pl.ds(g * rows, rows)] = part.astype(jnp.float32).T.astype(jnp.bfloat16)
        saves += [
            pltpu.make_async_copy(out_ref, out_hbm, sems.at[3]),
            pltpu.make_async_copy(grad, grad_hbm, sems.at[4]),
            pltpu.make_async_copy(turned_ref, turned_hbm, sems.at[5]),
        ]
        for save in saves[1:]:
            save.start()
        write_half(
            table_ref, half_ref[0], ext, turned_ref, half_out, half_hbm, sems.at[directions + 6], scale
        )
        for save in saves:
            save.wait()

    flops = 3 * offset_count * tile_slots * voxels * channels * channels
    out_shape = [
        jax.ShapeDtypeStruct(tiles.shape, jnp.bfloat16),
        jax.ShapeDtypeStruct(tiles.shape, jnp.bfloat16),
        jax.ShapeDtypeStruct((channels, tile_slots * voxels), jnp.bfloat16),
        jax.ShapeDtypeStruct((empty + 1, voxels, channels), jnp.bfloat16),
        jax.ShapeDtypeStruct((offset_count, channels // 2, channels), jnp.float32),
    ]
    return pl.pallas_call(
        kernel,
        out_shape=out_shape,
        in_specs=[SMEM, SMEM, HBM] + [ANY] * directions + [HBM, HBM, ANY],
        out_specs=[HBM] * 5,
        scratch_shapes=[
            pltpu.VMEM(weights.shape, jnp.bfloat16),
            pltpu.VMEM(tiles.shape, jnp.bfloat16),
        ]
        + [pltpu.VMEM(one.shape, one.dtype) for one in out_shape]
        + [
            pltpu.VMEM((groups, rows, channels), jnp.float32),
            pltpu.SemaphoreType.DMA((directions + 7,)),
            pltpu.SemaphoreType.DMA((offset_count // deep,)),
        ],
        compiler_params=pltpu.CompilerParams(vmem_limit_bytes=60 * MIB),
        cost_estimate=pl.CostEstimate(flops=flops, bytes_accessed=20 * MIB, transcendentals=0),
        name="forward_and_terms",
    )(table, half, tiles, *halos, weights, cotangent, after)


def weight_terms(table, half, ext, turned, offset_count, scale):
    channels = ext.shape[2]

    def kernel(table_ref, half_ref, ext_hbm, turned_hbm, out_hbm, ext_ref, turned_ref, out_ref, sems):
        copies = [pltpu.make_async_copy(turned_hbm, turned_ref, sems.at[0])]
        slots = ext_ref.shape[0]
        for n in range(4):
            part = pl.ds(n * slots // 4, (n + 1) * slots // 4 - n * slots // 4)
            copies.append(pltpu.make_async_copy(ext_hbm.at[part], ext_ref.at[part], sems.at[n + 1]))
        for copy in copies:
            copy.start()
        for copy in copies:
            copy.wait()
        write_half(table_ref, half_ref[0], ext_ref, turned_ref, out_ref, out_hbm, sems.at[5], scale)

    flops = offset_count * turned.shape[1] * channels * channels
    out_shape = jax.ShapeDtypeStruct((offset_count, channels // 2, channels), jnp.float32)
    return pl.pallas_call(
        kernel,
        out_shape=out_shape,
        in_specs=[SMEM, SMEM, HBM, HBM],
        out_specs=HBM,
        scratch_shapes=[
            pltpu.VMEM(ext.shape, ext.dtype),
            pltpu.VMEM(turned.shape, turned.dtype),
            pltpu.VMEM(out_shape.shape, out_shape.dtype),
            pltpu.SemaphoreType.DMA((6,)),
        ],
        compiler_params=pltpu.CompilerParams(vmem_limit_bytes=60 * MIB),
        cost_estimate=pl.CostEstimate(flops=flops, bytes_accessed=6 * MIB, transcendentals=0),
        name="weight_terms",
    )(table, half, ext, turned)


def input_grad(table, pre_grad, turned_weights, halo):
    tile_slots, voxels, channels = pre_grad.shape
    offset_count = turned_weights.shape[0]
    empty = tile_slots + len(DIRECTIONS) * halo
    group = chunk_of(tile_slots, 8)
    groups = tile_slots // group
    rows = group * voxels
    unroll = chunk_of(offset_count, 3)
    bundles = len(BUNDLES)

    def kernel(table_ref, grad_hbm, w_hbm, own_hbm, *refs):
        adjoints_hbm, refs = refs[:bundles], refs[bundles:]
        own_ref, adjoints, refs = refs[0], refs[1 : bundles + 1], refs[bundles + 1 :]
        even, odd, grad, w_ref, sems = refs
        copies = [
            pltpu.make_async_copy(grad_hbm, grad, sems.at[0]),
            pltpu.make_async_copy(w_hbm, w_ref, sems.at[1]),
        ]
        for copy in copies:
            copy.start()
        for one in (even, odd):
            one[...] = jnp.zeros_like(one)
        for copy in copies:
            copy.wait()

        def turn(step, carry):
            for j in range(unroll):
                k = step * unroll + j
                for g in range(groups):
                    back = jnp.dot(
                        grad[pl.ds(g * group, group)].reshape(rows, channels),
                        w_ref[k],
                        preferred_element_type=jnp.float32,
                    )
                    for t in range(group):
                        slot = table_ref[k, g * group + t]
                        sums = (even, odd)[t % 2]
                        sums[slot] += back[t * voxels : (t + 1) * voxels]
            return carry

        lax.fori_loop(0, offset_count // unroll, turn, 0)

        saves = []
        for n, (bundle, adjoint) in enumerate(zip(BUNDLES, adjoints)):
            for m, pair in enumerate(bundle):
                for h in range(halo):
                    slot = tile_slots + DIRECTIONS.index(pair) * halo + h
                    adjoint[m * halo + h] = (even[slot] + odd[slot]).astype(jnp.bfloat16)
            saves.append(pltpu.make_async_copy(adjoint, adjoints_hbm[n], sems.at[n + 2]))
            saves[-1].start()

        def own(t, carry):
            own_ref[t] = even[t] + odd[t]
            return carry

        half = tile_slots // 2
        for n in range(2):
            lax.fori_loop(n * half, (n + 1) * half, own, 0)
            part = pl.ds(n * half, half)
            saves.append(
                pltpu.make_async_copy(own_ref.at[part], own_hbm.at[part], sems.at[bundles + 2 + n])
            )
            saves[-1].start()
        for save in saves:
            save.wait()

    flops = 2 * offset_count * tile_slots * voxels * channels * channels
    out_shape = [jax.ShapeDtypeStruct(pre_grad.shape, jnp.float32)] + [
        jax.ShapeDtypeStruct((len(bundle) * halo, voxels, channels), jnp.bfloat16)
        for bundle in BUNDLES
    ]
    return pl.pallas_call(
        kernel,
        out_shape=out_shape,
        in_specs=[SMEM, HBM, HBM],
        out_specs=[HBM] * (bundles + 1),
        scratch_shapes=[pltpu.VMEM(one.shape, one.dtype) for one in out_shape]
        + [pltpu.VMEM((empty + 1, voxels, channels), jnp.float32)] * 2
        + [
            pltpu.VMEM(pre_grad.shape, jnp.bfloat16),
            pltpu.VMEM(turned_weights.shape, jnp.bfloat16),
            pltpu.SemaphoreType.DMA((bundles + 4,)),
        ],
        compiler_params=pltpu.CompilerParams(vmem_limit_bytes=60 * MIB),
        cost_estimate=pl.CostEstimate(flops=flops, bytes_accessed=12 * MIB, transcendentals=0),
        name="input_grad",
    )(table, pre_grad, turned_weights)


def to_other_core(x):
    return lax.ppermute(x, "core", [(0, 1), (1, 0)])


def ring(axis):
    size = lax.axis_size(axis)

    def move(x, by):
        return lax.ppermute(x, axis, [(i, (i + by) % size) for i in range(size)])

    return size, lax.axis_index(axis), move


def given_out(terms, ring):
    size, place, _ = ring
    parts = []
    for s in range(size):
        blocks = [
            lax.dynamic_index_in_dim(
                one.reshape(size, one.shape[0] // size, one.shape[1]), (place + s) % size, keepdims=False
            )
            for one in terms
        ]
        parts.append(sum(blocks[1:], blocks[0]))
    return parts[0], [one.astype(jnp.bfloat16) for one in parts[1:]]


def handed(parts, ring):
    return [ring[2](one, s + 1) for s, one in enumerate(parts)]


def added(mine, arrived):
    for one in arrived:
        mine = mine + one.astype(jnp.float32)
    return mine


def fetched(piece, ring):
    return [ring[2](piece, -s) for s in range(1, ring[0])]


def in_order(piece, others, ring):
    size, place, _ = ring
    whole = jnp.zeros((size,) + piece.shape, piece.dtype)
    for s, one in enumerate([piece, *others]):
        whole = lax.dynamic_update_index_in_dim(whole, one, (place + s) % size, 0)
    return whole.reshape(size * piece.shape[0], piece.shape[1])


def together(*values):
    return lax.optimization_barrier(values)


def widen(place, half, whole):
    rows, channels = half.shape
    turns = chunk_of(rows // 16, 3)
    step = rows // turns

    def kernel(place_ref, half_ref, *refs):
        refs[-1][...] = half_ref[...].astype(jnp.float32)

    given = [] if whole is None else [whole]
    return pl.pallas_call(
        kernel,
        grid_spec=pltpu.PrefetchScalarGridSpec(
            num_scalar_prefetch=1,
            grid=(turns,),
            in_specs=[pl.BlockSpec((step, channels), lambda i, place: (i, 0))] + [ANY] * len(given),
            out_specs=pl.BlockSpec((step, channels), lambda i, place: (place[0] * turns + i, 0)),
        ),
        out_shape=jax.ShapeDtypeStruct((2 * rows, channels), jnp.float32),
        input_output_aliases={2: 0} if given else {},
        compiler_params=pltpu.CompilerParams(vmem_limit_bytes=24 * MIB),
        name="widen",
    )(place, half, *given)


def combine(lists, own, cotangent, returned):
    halo = lists.shape[1]
    tile_slots = own.shape[0]
    arrays = [array for array, _ in returned]

    def kernel(lists_ref, own_ref, cot_ref, *refs):
        out_ref, acc = refs[len(arrays) :]

        def start(t, carry):
            acc[t] = own_ref[t] + cot_ref[t].astype(jnp.float32)
            return carry

        lax.fori_loop(0, tile_slots, start, 0)
        for ref, (_, pairs) in zip(refs, returned):
            for n, pair in enumerate(pairs):
                for h in range(halo):
                    tile = lists_ref[DIRECTIONS.index(pair), h]
                    acc[tile] += ref[n * halo + h].astype(jnp.float32)

        def finish(t, carry):
            out_ref[t] = acc[t].astype(out_ref.dtype)
            return carry

        lax.fori_loop(0, tile_slots, finish, 0)

    return pl.pallas_call(
        kernel,
        out_shape=jax.ShapeDtypeStruct(own.shape, jnp.bfloat16),
        in_specs=[SMEM] + [VMEM] * (len(arrays) + 2),
        out_specs=VMEM,
        scratch_shapes=[pltpu.VMEM(own.shape, jnp.float32)],
        compiler_params=pltpu.CompilerParams(vmem_limit_bytes=16 * MIB),
        name="combine",
    )(lists, own, cotangent, *arrays)


def shards(
    features, weights, cotangent, send_lists, block_offset, block_input, block_output, block_count
):
    tiles = features[0, 0]
    incoming = cotangent[0, 0]
    lists = send_lists[0, 0]
    tile_slots, voxels, channels = tiles.shape
    directions, halo = lists.shape
    device_total = x_size() * lax.axis_size("gy")
    scale = 1.0 / math.sqrt(voxels * tile_slots * device_total)
    offset_count = weights.shape[0]
    core = lax.axis_index("core").astype(jnp.int32)[None]

    packets = pack(tiles, lists)
    halos = [travel(packets[d], *DIRECTIONS[d]) for d in range(directions)]
    table = source_table(
        block_offset[0, 0],
        block_input[0, 0].T,
        block_output[0, 0].T,
        block_count[0],
        offset_count,
        tile_slots,
        tile_slots + directions * halo,
        halos[0],
    )
    turned_weights = turn_weights(weights, table)
    out_features, pre_grad, turned, ext, send = forward_and_terms(
        table, 1 - core, tiles, halos, weights, incoming, scale, turned_weights
    )
    received = to_other_core(send)
    keep = weight_terms(table, core, ext, turned, offset_count, scale)
    levels = ring("gy"), ring("gz")
    mine, out = given_out([keep.reshape(-1, channels), received.reshape(-1, channels)], levels[0])

    pre_grad, *out = together(pre_grad, *out)
    moved = handed(out, levels[0])
    own, low, high, low_both, high_both, behind, ahead = input_grad(table, pre_grad, turned_weights, halo)
    low, high = travel(low, 0, 1), travel(high, 0, -1)
    low, high, *moved = together(low, high, *moved)
    low_both, high_both = travel(low_both, 0, 1), travel(high_both, 0, -1)

    mine, out = given_out([added(mine, moved)], levels[1])
    piece = added(mine, handed(out, levels[1])).astype(jnp.bfloat16)
    low_both, piece = together(low_both, piece)
    piece = in_order(piece, fetched(piece, levels[1]), levels[1])
    high_both, piece = together(high_both, piece)
    behind = jnp.concatenate([behind, low_both[:halo], high_both[:halo]])
    ahead = jnp.concatenate([ahead, low_both[halo:], high_both[halo:]])
    behind, ahead = travel(behind, 1, 0), travel(ahead, -1, 0)
    own_half = in_order(piece, fetched(piece, levels[0]), levels[0])
    behind, ahead, own_half = together(behind, ahead, own_half)
    feat_grad = combine(
        lists,
        own,
        incoming,
        [
            (low, ((0, -1),)),
            (high, ((0, 1),)),
            (behind, ((-1, 0), (-1, -1), (-1, 1))),
            (ahead, ((1, 0), (1, -1), (1, 1))),
        ],
    )
    other_half = to_other_core(own_half)
    weight_grad = widen(1 - core, other_half, widen(core, own_half, None)).reshape(weights.shape)
    return (out_features[None, None], feat_grad[None, None], weight_grad)


def solution(mesh):
    size_x, size_y = mesh.devices.shape
    split = Mesh(mesh.devices.reshape(size_x // 2, 2, size_y), ("gz", "core", "gy"))
    place = P(("gz", "core"), "gy")
    return jax.shard_map(
        shards,
        mesh=split,
        in_specs=(place, P(), place, place, place, place, place, place),
        out_specs=(place, place, P()),
        check_vma=False,
    )
```

```python
import math

import jax
import jax.numpy as jnp
from jax import lax
from jax.experimental import pallas as pl
from jax.experimental.pallas import tpu as pltpu
from jax.sharding import Mesh
from jax.sharding import PartitionSpec as P

DIRECTIONS = ((-1, -1), (-1, 0), (-1, 1), (0, -1), (0, 1), (1, -1), (1, 0), (1, 1))
BUNDLES = (
    ((0, -1),),
    ((0, 1),),
    ((-1, -1), (1, -1)),
    ((-1, 1), (1, 1)),
    ((-1, 0),),
    ((1, 0),),
)
MIB = 1024 * 1024
ANY = pl.BlockSpec(memory_space=pl.ANY)
HBM = pl.BlockSpec(memory_space=pltpu.HBM)
VMEM = pl.BlockSpec(memory_space=pltpu.VMEM)
SMEM = pl.BlockSpec(memory_space=pltpu.SMEM)


def chunk_of(size, wanted):
    return max(c for c in range(1, wanted + 1) if size % c == 0)


def x_size():
    return lax.axis_size("gz") * lax.axis_size("core")


def travel(packet, step_x, step_y):
    size_x, size_y = x_size(), lax.axis_size("gy")
    pairs = [
        (i * size_y + j, (i + step_x) * size_y + j + step_y)
        for i in range(size_x)
        for j in range(size_y)
        if 0 <= i + step_x < size_x and 0 <= j + step_y < size_y
    ]
    return lax.ppermute(packet, ("gz", "core", "gy"), pairs)


def pack(tiles, lists):
    halo = lists.shape[1]
    _, voxels, channels = tiles.shape

    def kernel(lists_ref, tiles_ref, *packets):
        for d, packet in enumerate(packets):
            for h in range(halo):
                packet[h] = tiles_ref[lists_ref[d, h]]

    return pl.pallas_call(
        kernel,
        out_shape=[jax.ShapeDtypeStruct((halo, voxels, channels), tiles.dtype)] * len(DIRECTIONS),
        in_specs=[SMEM, VMEM],
        out_specs=[VMEM] * len(DIRECTIONS),
        compiler_params=pltpu.CompilerParams(vmem_limit_bytes=16 * MIB),
        name="pack",
    )(lists, tiles)


def source_table(offsets, inputs, outputs, count, offset_count, tile_slots, empty, after):
    rows, blocks = inputs.shape

    def kernel(offsets_ref, inputs_ref, outputs_ref, count_ref, _, table_ref):
        def clear(k, carry):
            for t in range(tile_slots):
                table_ref[k, t] = empty
            return carry

        lax.fori_loop(0, offset_count, clear, 0)

        def block(n, carry):
            k = offsets_ref[n]
            for q in range(rows):
                table_ref[k, outputs_ref[q, n]] = inputs_ref[q, n]
            return carry

        lax.fori_loop(0, jnp.minimum(count_ref[0], blocks), block, 0)

    return pl.pallas_call(
        kernel,
        out_shape=jax.ShapeDtypeStruct((offset_count, tile_slots + 1), jnp.int32),
        in_specs=[SMEM] * 4 + [ANY],
        out_specs=SMEM,
        cost_estimate=pl.CostEstimate(flops=4 * 10**9, bytes_accessed=MIB, transcendentals=0),
        name="source_table",
    )(offsets, inputs, outputs, count, after)


def gathered(table_ref, ext, k, first, count):
    return jnp.concatenate([ext[table_ref[k, first + t]] for t in range(count)], axis=0)


def write_half(table_ref, late, ext, turned_ref, out_ref, out_hbm, sem, scale):
    offset_count, part, _ = out_ref.shape
    tile_slots = table_ref.shape[1] - 1
    count = (offset_count + 1) // 2

    def turn(j, carry):
        k = late * (offset_count - count) + j
        terms = jnp.dot(
            turned_ref[...],
            gathered(table_ref, ext, k, 0, tile_slots),
            preferred_element_type=jnp.float32,
        )
        terms = terms.T * scale
        for b in range(2):
            place = 2 * k + b - late * offset_count

            @pl.when((place >= 0) & (place < offset_count))
            def _():
                out_ref[place] = terms[b * part : (b + 1) * part]
                pltpu.make_async_copy(out_ref.at[place], out_hbm.at[place], sem).start()

        return carry

    lax.fori_loop(0, count, turn, 0)
    pltpu.make_async_copy(out_ref, out_hbm, sem).wait()


def turn_weights(weights, after):
    def kernel(_, w_ref, out_ref):
        for k in range(w_ref.shape[0]):
            out_ref[k] = w_ref[k].astype(jnp.float32).T.astype(out_ref.dtype)

    offset_count, channels, _ = weights.shape
    step = chunk_of(offset_count, 3)
    spec = pl.BlockSpec((step, channels, channels), lambda k: (k, 0, 0))
    return pl.pallas_call(
        kernel,
        grid=(offset_count // step,),
        out_shape=jax.ShapeDtypeStruct(weights.shape, weights.dtype),
        in_specs=[SMEM, spec],
        out_specs=spec,
        compiler_params=pltpu.CompilerParams(vmem_limit_bytes=60 * MIB),
        cost_estimate=pl.CostEstimate(flops=8 * 10**9, bytes_accessed=7 * MIB, transcendentals=0),
        name="turn_weights",
    )(after, weights)


def forward_and_terms(table, half, tiles, halos, weights, cotangent, scale, after):
    tile_slots, voxels, channels = tiles.shape
    offset_count = weights.shape[0]
    directions, halo = len(halos), halos[0].shape[0]
    empty = tile_slots + directions * halo
    group = chunk_of(tile_slots, 8)
    groups = tile_slots // group
    rows = group * voxels
    deep = chunk_of(offset_count, 9)

    def kernel(table_ref, half_ref, tiles_ref, *refs):
        halo_refs, refs = refs[:directions], refs[directions:]
        w_hbm, cot_hbm, _, out_hbm, grad_hbm, turned_hbm, ext_hbm, half_hbm = refs[:8]
        w_ref, cot_ref, out_ref, grad, turned_ref, ext, half_out, acc, sems, w_sems = refs[8:]
        copies = [pltpu.make_async_copy(tiles_ref, ext.at[pl.ds(0, tile_slots)], sems.at[0])]
        for d, halo_ref in enumerate(halo_refs):
            place = ext.at[pl.ds(tile_slots + d * halo, halo)]
            copies.append(pltpu.make_async_copy(halo_ref, place, sems.at[d + 6]))

        def load_mats(step):
            part = pl.ds(step * deep, deep)
            return pltpu.make_async_copy(w_hbm.at[part], w_ref.at[part], w_sems.at[step])

        load_cot = pltpu.make_async_copy(cot_hbm, cot_ref, sems.at[1])
        for copy in copies + [load_mats(n) for n in range(offset_count // deep)] + [load_cot]:
            copy.start()
        ext[empty] = jnp.zeros((voxels, channels), ext.dtype)
        acc[...] = jnp.zeros_like(acc)
        for copy in copies:
            copy.wait()
        saves = [pltpu.make_async_copy(ext, ext_hbm, sems.at[2])]
        saves[0].start()

        def turn(step, carry):
            load_mats(step).wait()
            mats = w_ref[pl.ds(step * deep, deep)].reshape(deep * channels, channels)
            for g in range(groups):
                lhs = jnp.concatenate(
                    [
                        gathered(table_ref, ext, step * deep + j, g * group, group)
                        for j in range(deep)
                    ],
                    axis=1,
                )
                acc[g] += jnp.dot(lhs, mats, preferred_element_type=jnp.float32)
            return carry

        lax.fori_loop(0, offset_count // deep, turn, 0)
        load_cot.wait()

        def finish(t, carry):
            pre = acc[t // group, pl.ds(pl.multiple_of((t % group) * voxels, voxels), voxels), :]
            sigma = jax.nn.sigmoid(pre)
            out_ref[t] = (ext[t].astype(jnp.float32) + pre * sigma).astype(out_ref.dtype)
            incoming = cot_ref[t].astype(jnp.float32)
            grad[t] = (incoming * sigma * (1.0 + pre * (1.0 - sigma))).astype(grad.dtype)
            return carry

        lax.fori_loop(0, tile_slots, finish, 0)
        for g in range(groups):
            part = grad[pl.ds(g * group, group)].reshape(rows, channels)
            turned_ref[:, pl.ds(g * rows, rows)] = part.astype(jnp.float32).T.astype(jnp.bfloat16)
        saves += [
            pltpu.make_async_copy(out_ref, out_hbm, sems.at[3]),
            pltpu.make_async_copy(grad, grad_hbm, sems.at[4]),
            pltpu.make_async_copy(turned_ref, turned_hbm, sems.at[5]),
        ]
        for save in saves[1:]:
            save.start()
        write_half(
            table_ref, half_ref[0], ext, turned_ref, half_out, half_hbm, sems.at[directions + 6], scale
        )
        for save in saves:
            save.wait()

    flops = 3 * offset_count * tile_slots * voxels * channels * channels
    out_shape = [
        jax.ShapeDtypeStruct(tiles.shape, jnp.bfloat16),
        jax.ShapeDtypeStruct(tiles.shape, jnp.bfloat16),
        jax.ShapeDtypeStruct((channels, tile_slots * voxels), jnp.bfloat16),
        jax.ShapeDtypeStruct((empty + 1, voxels, channels), jnp.bfloat16),
        jax.ShapeDtypeStruct((offset_count, channels // 2, channels), jnp.float32),
    ]
    return pl.pallas_call(
        kernel,
        out_shape=out_shape,
        in_specs=[SMEM, SMEM, HBM] + [ANY] * directions + [HBM, HBM, ANY],
        out_specs=[HBM] * 5,
        scratch_shapes=[
            pltpu.VMEM(weights.shape, jnp.bfloat16),
            pltpu.VMEM(tiles.shape, jnp.bfloat16),
        ]
        + [pltpu.VMEM(one.shape, one.dtype) for one in out_shape]
        + [
            pltpu.VMEM((groups, rows, channels), jnp.float32),
            pltpu.SemaphoreType.DMA((directions + 7,)),
            pltpu.SemaphoreType.DMA((offset_count // deep,)),
        ],
        compiler_params=pltpu.CompilerParams(vmem_limit_bytes=60 * MIB),
        cost_estimate=pl.CostEstimate(flops=flops, bytes_accessed=20 * MIB, transcendentals=0),
        name="forward_and_terms",
    )(table, half, tiles, *halos, weights, cotangent, after)


def weight_terms(table, half, ext, turned, offset_count, scale):
    channels = ext.shape[2]

    def kernel(table_ref, half_ref, ext_hbm, turned_hbm, out_hbm, ext_ref, turned_ref, out_ref, sems):
        copies = [pltpu.make_async_copy(turned_hbm, turned_ref, sems.at[0])]
        slots = ext_ref.shape[0]
        for n in range(4):
            part = pl.ds(n * slots // 4, (n + 1) * slots // 4 - n * slots // 4)
            copies.append(pltpu.make_async_copy(ext_hbm.at[part], ext_ref.at[part], sems.at[n + 1]))
        for copy in copies:
            copy.start()
        for copy in copies:
            copy.wait()
        write_half(table_ref, half_ref[0], ext_ref, turned_ref, out_ref, out_hbm, sems.at[5], scale)

    flops = offset_count * turned.shape[1] * channels * channels
    out_shape = jax.ShapeDtypeStruct((offset_count, channels // 2, channels), jnp.float32)
    return pl.pallas_call(
        kernel,
        out_shape=out_shape,
        in_specs=[SMEM, SMEM, HBM, HBM],
        out_specs=HBM,
        scratch_shapes=[
            pltpu.VMEM(ext.shape, ext.dtype),
            pltpu.VMEM(turned.shape, turned.dtype),
            pltpu.VMEM(out_shape.shape, out_shape.dtype),
            pltpu.SemaphoreType.DMA((6,)),
        ],
        compiler_params=pltpu.CompilerParams(vmem_limit_bytes=60 * MIB),
        cost_estimate=pl.CostEstimate(flops=flops, bytes_accessed=6 * MIB, transcendentals=0),
        name="weight_terms",
    )(table, half, ext, turned)


def input_grad(table, pre_grad, turned_weights, halo):
    tile_slots, voxels, channels = pre_grad.shape
    offset_count = turned_weights.shape[0]
    empty = tile_slots + len(DIRECTIONS) * halo
    group = chunk_of(tile_slots, 8)
    groups = tile_slots // group
    rows = group * voxels
    unroll = chunk_of(offset_count, 3)
    bundles = len(BUNDLES)

    def kernel(table_ref, grad_hbm, w_hbm, own_hbm, *refs):
        adjoints_hbm, refs = refs[:bundles], refs[bundles:]
        own_ref, adjoints, refs = refs[0], refs[1 : bundles + 1], refs[bundles + 1 :]
        even, odd, grad, w_ref, sems = refs
        copies = [
            pltpu.make_async_copy(grad_hbm, grad, sems.at[0]),
            pltpu.make_async_copy(w_hbm, w_ref, sems.at[1]),
        ]
        for copy in copies:
            copy.start()
        for one in (even, odd):
            one[...] = jnp.zeros_like(one)
        for copy in copies:
            copy.wait()

        def turn(step, carry):
            for j in range(unroll):
                k = step * unroll + j
                for g in range(groups):
                    back = jnp.dot(
                        grad[pl.ds(g * group, group)].reshape(rows, channels),
                        w_ref[k],
                        preferred_element_type=jnp.float32,
                    )
                    for t in range(group):
                        slot = table_ref[k, g * group + t]
                        sums = (even, odd)[t % 2]
                        sums[slot] += back[t * voxels : (t + 1) * voxels]
            return carry

        lax.fori_loop(0, offset_count // unroll, turn, 0)

        saves = []
        for n, (bundle, adjoint) in enumerate(zip(BUNDLES, adjoints)):
            for m, pair in enumerate(bundle):
                for h in range(halo):
                    slot = tile_slots + DIRECTIONS.index(pair) * halo + h
                    adjoint[m * halo + h] = (even[slot] + odd[slot]).astype(jnp.bfloat16)
            saves.append(pltpu.make_async_copy(adjoint, adjoints_hbm[n], sems.at[n + 2]))
            saves[-1].start()

        def own(t, carry):
            own_ref[t] = even[t] + odd[t]
            return carry

        half = tile_slots // 2
        for n in range(2):
            lax.fori_loop(n * half, (n + 1) * half, own, 0)
            part = pl.ds(n * half, half)
            saves.append(
                pltpu.make_async_copy(own_ref.at[part], own_hbm.at[part], sems.at[bundles + 2 + n])
            )
            saves[-1].start()
        for save in saves:
            save.wait()

    flops = 2 * offset_count * tile_slots * voxels * channels * channels
    out_shape = [jax.ShapeDtypeStruct(pre_grad.shape, jnp.float32)] + [
        jax.ShapeDtypeStruct((len(bundle) * halo, voxels, channels), jnp.bfloat16)
        for bundle in BUNDLES
    ]
    return pl.pallas_call(
        kernel,
        out_shape=out_shape,
        in_specs=[SMEM, HBM, HBM],
        out_specs=[HBM] * (bundles + 1),
        scratch_shapes=[pltpu.VMEM(one.shape, one.dtype) for one in out_shape]
        + [pltpu.VMEM((empty + 1, voxels, channels), jnp.float32)] * 2
        + [
            pltpu.VMEM(pre_grad.shape, jnp.bfloat16),
            pltpu.VMEM(turned_weights.shape, jnp.bfloat16),
            pltpu.SemaphoreType.DMA((bundles + 4,)),
        ],
        compiler_params=pltpu.CompilerParams(vmem_limit_bytes=60 * MIB),
        cost_estimate=pl.CostEstimate(flops=flops, bytes_accessed=12 * MIB, transcendentals=0),
        name="input_grad",
    )(table, pre_grad, turned_weights)


def to_other_core(x):
    return lax.ppermute(x, "core", [(0, 1), (1, 0)])


def ring(axis):
    size = lax.axis_size(axis)

    def move(x, by):
        return lax.ppermute(x, axis, [(i, (i + by) % size) for i in range(size)])

    return size, lax.axis_index(axis), move


def given_out(terms, ring):
    size, place, _ = ring
    parts = []
    for s in range(size):
        blocks = [
            lax.dynamic_index_in_dim(
                one.reshape(size, one.shape[0] // size, one.shape[1]), (place + s) % size, keepdims=False
            )
            for one in terms
        ]
        parts.append(sum(blocks[1:], blocks[0]))
    return parts[0], [one.astype(jnp.bfloat16) for one in parts[1:]]


def handed(parts, ring):
    return [ring[2](one, s + 1) for s, one in enumerate(parts)]


def added(mine, arrived):
    for one in arrived:
        mine = mine + one.astype(jnp.float32)
    return mine


def fetched(piece, ring):
    return [ring[2](piece, -s) for s in range(1, ring[0])]


def in_order(piece, others, ring):
    size, place, _ = ring
    whole = jnp.zeros((size,) + piece.shape, piece.dtype)
    for s, one in enumerate([piece, *others]):
        whole = lax.dynamic_update_index_in_dim(whole, one, (place + s) % size, 0)
    return whole.reshape(size * piece.shape[0], piece.shape[1])


def together(*values):
    return lax.optimization_barrier(values)


def widen(place, half, whole):
    rows, channels = half.shape
    turns = chunk_of(rows // 16, 3)
    step = rows // turns

    def kernel(place_ref, half_ref, *refs):
        refs[-1][...] = half_ref[...].astype(jnp.float32)

    given = [] if whole is None else [whole]
    return pl.pallas_call(
        kernel,
        grid_spec=pltpu.PrefetchScalarGridSpec(
            num_scalar_prefetch=1,
            grid=(turns,),
            in_specs=[pl.BlockSpec((step, channels), lambda i, place: (i, 0))] + [ANY] * len(given),
            out_specs=pl.BlockSpec((step, channels), lambda i, place: (place[0] * turns + i, 0)),
        ),
        out_shape=jax.ShapeDtypeStruct((2 * rows, channels), jnp.float32),
        input_output_aliases={2: 0} if given else {},
        compiler_params=pltpu.CompilerParams(vmem_limit_bytes=24 * MIB),
        name="widen",
    )(place, half, *given)


def combine(lists, own, cotangent, returned):
    halo = lists.shape[1]
    tile_slots = own.shape[0]
    arrays = [array for array, _ in returned]

    def kernel(lists_ref, own_ref, cot_ref, *refs):
        out_ref, acc = refs[len(arrays) :]

        def start(t, carry):
            acc[t] = own_ref[t] + cot_ref[t].astype(jnp.float32)
            return carry

        lax.fori_loop(0, tile_slots, start, 0)
        for ref, (_, pairs) in zip(refs, returned):
            for n, pair in enumerate(pairs):
                for h in range(halo):
                    tile = lists_ref[DIRECTIONS.index(pair), h]
                    acc[tile] += ref[n * halo + h].astype(jnp.float32)

        def finish(t, carry):
            out_ref[t] = acc[t].astype(out_ref.dtype)
            return carry

        lax.fori_loop(0, tile_slots, finish, 0)

    return pl.pallas_call(
        kernel,
        out_shape=jax.ShapeDtypeStruct(own.shape, jnp.bfloat16),
        in_specs=[SMEM] + [VMEM] * (len(arrays) + 2),
        out_specs=VMEM,
        scratch_shapes=[pltpu.VMEM(own.shape, jnp.float32)],
        compiler_params=pltpu.CompilerParams(vmem_limit_bytes=16 * MIB),
        name="combine",
    )(lists, own, cotangent, *arrays)


def shards(
    features, weights, cotangent, send_lists, block_offset, block_input, block_output, block_count
):
    tiles = features[0, 0]
    incoming = cotangent[0, 0]
    lists = send_lists[0, 0]
    tile_slots, voxels, channels = tiles.shape
    directions, halo = lists.shape
    device_total = x_size() * lax.axis_size("gy")
    scale = 1.0 / math.sqrt(voxels * tile_slots * device_total)
    offset_count = weights.shape[0]
    core = lax.axis_index("core").astype(jnp.int32)[None]

    packets = pack(tiles, lists)
    table = source_table(
        block_offset[0, 0],
        block_input[0, 0].T,
        block_output[0, 0].T,
        block_count[0],
        offset_count,
        tile_slots,
        tile_slots + directions * halo,
        packets[0],
    )
    turned_weights = turn_weights(weights, table)
    order = [
        DIRECTIONS.index(pair)
        for pair in ((-1, -1), (1, 1), (-1, 0), (1, 0), (-1, 1), (1, -1), (0, -1), (0, 1))
    ]
    arrived = {d: travel(packets[d], *DIRECTIONS[d]) for d in order}
    halos = [arrived[d] for d in range(directions)]
    out_features, pre_grad, turned, ext, send = forward_and_terms(
        table, 1 - core, tiles, halos, weights, incoming, scale, turned_weights
    )
    received = to_other_core(send)
    keep = weight_terms(table, core, ext, turned, offset_count, scale)
    levels = ring("gy"), ring("gz")
    mine, out = given_out([keep.reshape(-1, channels), received.reshape(-1, channels)], levels[0])

    pre_grad, *out = together(pre_grad, *out)
    moved = handed(out, levels[0])
    own, low, high, low_both, high_both, behind, ahead = input_grad(table, pre_grad, turned_weights, halo)
    low, high = travel(low, 0, 1), travel(high, 0, -1)
    low, high, *moved = together(low, high, *moved)
    low_both, high_both = travel(low_both, 0, 1), travel(high_both, 0, -1)

    mine, out = given_out([added(mine, moved)], levels[1])
    piece = added(mine, handed(out, levels[1])).astype(jnp.bfloat16)
    low_both, piece = together(low_both, piece)
    piece = in_order(piece, fetched(piece, levels[1]), levels[1])
    high_both, piece = together(high_both, piece)
    behind = jnp.concatenate([behind, low_both[:halo], high_both[:halo]])
    ahead = jnp.concatenate([ahead, low_both[halo:], high_both[halo:]])
    behind, ahead = travel(behind, 1, 0), travel(ahead, -1, 0)
    own_half = in_order(piece, fetched(piece, levels[0]), levels[0])
    behind, ahead, own_half = together(behind, ahead, own_half)
    feat_grad = combine(
        lists,
        own,
        incoming,
        [
            (low, ((0, -1),)),
            (high, ((0, 1),)),
            (behind, ((-1, 0), (-1, -1), (-1, 1))),
            (ahead, ((1, 0), (1, -1), (1, 1))),
        ],
    )
    other_half = to_other_core(own_half)
    weight_grad = widen(1 - core, other_half, widen(core, own_half, None)).reshape(weights.shape)
    return (out_features[None, None], feat_grad[None, None], weight_grad)


def solution(mesh):
    size_x, size_y = mesh.devices.shape
    split = Mesh(mesh.devices.reshape(size_x // 2, 2, size_y), ("gz", "core", "gy"))
    place = P(("gz", "core"), "gy")
    return jax.shard_map(
        shards,
        mesh=split,
        in_specs=(place, P(), place, place, place, place, place, place),
        out_specs=(place, place, P()),
        check_vma=False,
    )
```
